256 devices in a mesh: tok: 4 (over z_hi), voc: 64 (over z_lo, y, x, core).
Axes of the slice: x: 4, y: 4, z: 8 (z_hi: 4, z_lo: 2; z = z_hi * 2 + z_lo), core: 2. Of those that a mesh axis runs over, the one named last changes fastest.
Arguments:
- hidden: bfloat16 [512, 3584], P('tok'), may hold values from -15 to 15
- valid_mask: int32 [512], P('tok'), may hold values from 0 to 1, as said below
- student_head: bfloat16 [192000, 3584], P(('voc', 'tok')), may hold values from -0.09375 to 0.09375
- teacher_logits: bfloat16 [512, 192000], P('tok', 'voc'), may hold values from -12 to 12
Outputs:
- token_kl: float32 [512], P('tok')
- d_hidden: bfloat16 [512, 3584], P('tok', 'voc')
- d_head: bfloat16 [192000, 3584], P(('voc', 'tok'))
The draws below stay inside these ranges and needn't reach their ends.
Inputs may be any that keep to these rules, and one draw needn't show every extreme that they name: `valid_mask`: the last token of every block of 128 tokens is valid, and in at least one such block every token is valid.
All inputs are finite; a program needn't handle non-finite values.
Results may differ from the reference program's by a relative error of at most 0.005.
Values may be sent and summed in bfloat16 or wider, within the bound.
A program may use at most 64 MiB of HBM per device.

```python
import jax
import jax.numpy as jnp
from jax import lax

D = 3584
V = 192000
TOK_DEV = 128
TOKENS = 512
SLAB = 750


def draw_valid_mask(key, part):
    key = jax.random.fold_in(key, 7)
    position = jnp.arange(TOKENS, dtype=jnp.int32)
    level = 200 + 750 * position // TOKENS
    ticket = jax.random.randint(jax.random.fold_in(key, 1), (TOKENS,), 0, 1000, dtype=jnp.int32)
    block_count = TOKENS // TOK_DEV
    full_block = jax.random.randint(jax.random.fold_in(key, 2), (), 0, block_count, dtype=jnp.int32)
    forced = (position % TOK_DEV == TOK_DEV - 1) | (position // TOK_DEV == full_block)
    return jnp.where((ticket < level) | forced, 1, 0).astype(jnp.int32)


def levels(stream_key, shape, shards, smallest, top_value):
    gain = 1.0
    for dim, parts in shards:
        heights = jax.random.uniform(jax.random.fold_in(jax.random.fold_in(stream_key, 6), dim), (parts,), jnp.float32, smallest / len(shards), top_value / len(shards))
        gain = gain * jnp.repeat(jnp.exp(heights), shape[dim] // parts).reshape((-1,) + (1,) * (len(shape) - 1 - dim))
    return gain


def bell_draw(own_key, extent, deviation, bound, shards=(), kind=jnp.bfloat16):
    gain = levels(own_key, extent, shards, -0.22, 0.18) if shards else 1.0
    result = jax.random.normal(own_key, extent, jnp.float32) * deviation * gain
    return jnp.minimum(jnp.maximum(result, -bound), bound).astype(kind)


def setup_inputs(seed: int = 0) -> dict:
    key_list = jax.random.split(jax.random.key(seed), 5)
    hidden = bell_draw(key_list[0], (TOKENS, D), 3.0, 15.0, ((0, 4),))
    valid_mask = draw_valid_mask(jax.random.fold_in(key_list[4], 71), 0)
    student_head = bell_draw(key_list[2], (V, D), D ** -0.5, 0.09375, ((0, 256),))
    teacher_logits = bell_draw(key_list[3], (TOKENS, V), 3.0, 12.0, ((0, 4), (1, 64)))
    return {"hidden": hidden, "valid_mask": valid_mask, "student_head": student_head, "teacher_logits": teacher_logits}


CAP = 30.0


def slab_pieces(hidden, student_head, teacher_logits, slab_index):
    head_rows = lax.dynamic_slice_in_dim(student_head, slab_index * SLAB, SLAB, 0)
    raw_logits = lax.dot_general(hidden, head_rows, (((1,), (1,)), ((), ())), preferred_element_type=jnp.float32)
    capped = CAP * jnp.tanh(raw_logits / CAP)
    target = lax.dynamic_slice_in_dim(teacher_logits, slab_index * SLAB, SLAB, 1).astype(jnp.float32)
    return head_rows, capped, target


def reference(hidden, valid_mask, student_head, teacher_logits):
    slab_count = V // SLAB
    indices = jnp.arange(slab_count, dtype=jnp.int32)

    def first_pass(totals, slab_index):
        head_rows, capped, target = slab_pieces(hidden, student_head, teacher_logits, slab_index)
        student_exp = jnp.exp(capped)
        teacher_exp = jnp.exp(target)
        return (totals[0] + jnp.sum(student_exp, axis=1), totals[1] + jnp.sum(teacher_exp, axis=1),
                totals[2] + jnp.sum(teacher_exp * (target - capped), axis=1)), None

    zeros_vec = jnp.zeros((TOKENS,), jnp.float32)
    (student_total, teacher_total, cross), _ = lax.scan(first_pass, (zeros_vec, zeros_vec, zeros_vec), indices)
    token_kl = cross / teacher_total - jnp.log(teacher_total) + jnp.log(student_total)
    token_count = jnp.sum(valid_mask.astype(jnp.float32))
    loss_scale = TOKENS / token_count
    row_weight = loss_scale * valid_mask.astype(jnp.float32)

    def second_pass(grad_hidden, slab_index):
        head_rows, capped, target = slab_pieces(hidden, student_head, teacher_logits, slab_index)
        student_exp = jnp.exp(capped)
        teacher_exp = jnp.exp(target)
        grad = row_weight[:, None] * (student_exp / student_total[:, None] - teacher_exp / teacher_total[:, None])
        grad = (grad * (1.0 - (capped / CAP) ** 2)).astype(jnp.bfloat16)
        head_grad = lax.dot_general(grad, hidden, (((0,), (0,)), ((), ())), preferred_element_type=jnp.float32)
        grad_hidden = grad_hidden + jnp.dot(grad, head_rows, preferred_element_type=jnp.float32)
        return grad_hidden, head_grad.astype(jnp.bfloat16)

    grad_hidden, head_slabs = lax.scan(second_pass, jnp.zeros((TOKENS, D), jnp.float32), indices)
    return token_kl, grad_hidden.astype(jnp.bfloat16), head_slabs.reshape(V, D)
```

```python
import jax
import jax.numpy as jnp
from jax import lax
from jax.experimental import pallas as pl
from jax.experimental.pallas import tpu as pltpu
from jax.sharding import PartitionSpec as P

CAP = 30.0
D = 3584
ROWS = 128
HALF = 256
SLAB = 750
VP = 768
QCOL = D // 4
PIECE = ROWS // 4
CHIPCOL = 112
MESH = pl.DeviceIdType.MESH
F32 = jnp.float32
BF16 = jnp.bfloat16


def kernel(
    hid, mask, head, teach, kl_out, dhid_out, DH,
    H, HD, HDT, EYE, tin, TS, TR, RLY, TSIB, CP, ES, GV, GTD,
    TT, TG1, TT2, TG2, TOT, AL, BE, CR, CG1, CR2, CG2, KL,
    OWN, NEXT, B1, R1, F1, B2, R2, B3, RZ,
    local, hs, hr, zs, zr, p1s, p1r, p2s, p2r, cs, cr, ts, tr, gs, gr,
    as1, ar1, as2, ar2, bs1, br1, bs2, br2, q1s, q1r, q2s, q2r, rzs, rzr,
):
    a = lax.axis_index("tok")
    v = lax.axis_index("voc")
    c = lax.rem(v, 2)
    x = lax.rem(v // 2, 4)
    y = lax.rem(v // 8, 4)
    zl = v // 32
    z = 2 * a + zl
    p = jnp.where(c == 0, x, y)
    q = jnp.where(c == 0, y, x)

    def dev(a_, zl_, y_, x_, c_):
        return (a_, zl_ * 32 + y_ * 8 + x_ * 2 + c_)

    def at_p(p_):
        return dev(a, zl, jnp.where(c == 0, y, p_), jnp.where(c == 0, p_, x), c)

    def at_q(q_):
        return dev(a, zl, jnp.where(c == 0, q_, y), jnp.where(c == 0, x, q_), c)

    sib = dev(a, zl, y, x, 1 - c)

    def at_a(a_):
        return dev(a_, zl, y, x, c)

    def at_xy(k):
        return dev(a, zl, k // 4, lax.rem(k, 4), c)

    def at_zc(k):
        return dev(k // 4, lax.rem(k // 2, 2), y, x, lax.rem(k, 2))

    def mod4(k):
        return lax.rem(k + 8, 4)

    me_xy = y * 4 + x
    me_zc = z * 2 + c

    pending = []

    def send(src, dst, ssem, rsem, to):
        copy = pltpu.make_async_remote_copy(
            src_ref=src, dst_ref=dst, send_sem=ssem, recv_sem=rsem, device_id=to, device_id_type=MESH
        )
        copy.start()
        pending.append(copy)

    def arrived(dst, ssem, rsem):
        pltpu.make_async_remote_copy(
            src_ref=dst, dst_ref=dst, send_sem=ssem, recv_sem=rsem, device_id=sib, device_id_type=MESH
        ).wait_recv()

    load_teach = pltpu.make_async_copy(teach, tin, local.at[0])
    load_teach.start()
    load_hid = pltpu.make_async_copy(hid, H.at[pl.ds(0, ROWS)], local.at[1])
    load_hid.start()
    load_head = pltpu.make_async_copy(head, DH, local.at[2])
    load_head.start()

    barrier = pltpu.get_barrier_semaphore()
    for k in range(1, 16):
        pl.semaphore_signal(barrier, inc=1, device_id=at_xy(lax.rem(me_xy + k, 16)), device_id_type=MESH)
        pl.semaphore_signal(barrier, inc=1, device_id=at_zc(lax.rem(me_zc + k, 16)), device_id_type=MESH)
    pl.semaphore_wait(barrier, 30)

    def span(start, size):
        return pl.ds(pl.multiple_of(start, 16), size)

    def cols(q_):
        return pl.ds(pl.multiple_of(q_ * QCOL, 128), QCOL)

    def base(g):
        return ROWS + c * ROWS + g * ROWS

    later = []

    def each_group(step):
        step(0)

        @pl.when(c == 1)
        def _():
            step(1)

    def send_group(g, make):
        copy = make(g)
        copy.start()
        if g == 0:
            pending.append(copy)
        else:
            later.append(lambda: make(1))

    def remote(src, dst, ssem, rsem, to):
        return pltpu.make_async_remote_copy(
            src_ref=src, dst_ref=dst, send_sem=ssem, recv_sem=rsem, device_id=to, device_id_type=MESH
        )

    each_group(lambda g: send_group(g, lambda g: remote(
        hid.at[span(p * PIECE, PIECE), cols(q)], H.at[span(base(g) + p * PIECE, PIECE), cols(q)],
        zs.at[g], zr.at[g], at_a(mod4(a - 1 - c - g)),
    )))

    load_teach.wait()
    place = lax.broadcasted_iota(jnp.int32, (VP, ROWS), 0)
    teacher_sum = jnp.zeros((1, ROWS), F32)
    for t in range(4):
        start = t * SLAB // 16 * 16
        off = t * SLAB - start
        height = min(VP + 16, 3000 - start)
        tall = tin[start : start + height].astype(F32)
        if height < VP + 16:
            tall = jnp.concatenate([tall, jnp.zeros((VP + 16 - height, ROWS), F32)], axis=0)
        if off:
            tall = pltpu.roll(tall, VP + 16 - off, 0)
        part = jnp.where(place < SLAB, tall[:VP], -30000.0)
        TS[t] = part.astype(BF16)
        teacher_sum = teacher_sum + jnp.sum(jnp.exp(part), axis=0, keepdims=True)
    way = jnp.where(c == 0, 1, 3)
    send(TS.at[mod4(a + 2)], RLY, ts.at[2], tr.at[2], at_a(mod4(a + way)))
    send(TS.at[mod4(a + 1)], TR.at[3], ts.at[0], tr.at[0], at_a(mod4(a + 1)))
    send(TS.at[mod4(a + 3)], TR.at[1], ts.at[1], tr.at[1], at_a(mod4(a + 3)))
    TR[0] = TS[a]

    TT[...] = jnp.zeros_like(TT)
    TT[pl.ds(4 + a, 1)] = teacher_sum
    TT[pl.ds(8 + a, 1)] = mask[...].astype(F32)

    nt = (((1,), (1,)), ((), ()))
    EYE[...] = jnp.where(
        lax.broadcasted_iota(jnp.int32, (256, 256), 0) == lax.broadcasted_iota(jnp.int32, (256, 256), 1), 1.0, 0.0
    ).astype(BF16)

    def turn(slab, half):
        for n in range(7):
            at = pl.ds(half * 1792 + n * 256, 256)
            out = lax.dot_general(
                EYE[...], HD[slab * VP : (slab + 1) * VP, at], nt, preferred_element_type=F32
            ).astype(BF16)
            done = 0
            while done < 256:
                chip, row = divmod(n * 256 + done, CHIPCOL)
                size = min(CHIPCOL - row, 256 - done)
                HDT[half, chip // 4, chip % 4, row : row + size, slab * VP : (slab + 1) * VP] = out[done : done + size]
                done += size

    def piece(g, p_):
        return H.at[span(base(g) + p_ * PIECE, PIECE), cols(q)]

    def first_step(g):
        arrived(piece(g, p), zs.at[g], zr.at[g])
        for d in range(1, 4):
            send_group(g, lambda g, d=d: remote(
                piece(g, p), piece(g, p), p1s.at[g, d - 1], p1r.at[g, d - 1], at_p(mod4(p + d)),
            ))

    each_group(first_step)

    load_head.wait()
    for k in range(3):
        if k == 2:
            HD[736:768] = jnp.concatenate([DH[736:750].astype(F32), jnp.zeros((18, D), F32)], axis=0).astype(BF16)

        @pl.loop(k * 8, min(k * 8 + 8, 23))
        def _(i):
            HD[pl.ds(pl.multiple_of(i * 32, 32), 32)] = DH[pl.ds(pl.multiple_of(i * 32, 32), 32)]

        send(HD.at[k * 256 : (k + 1) * 256], HD.at[VP + k * 256 : VP + (k + 1) * 256], hs.at[k], hr.at[k], sib)

    def first_end(g):
        for d in range(1, 4):
            arrived(piece(g, mod4(p - d)), p1s.at[g, d - 1], p1r.at[g, d - 1])

    each_group(first_end)

    right, left = at_q(mod4(q + 1)), at_q(mod4(q - 1))
    before, after, across = mod4(q - 1), mod4(q + 1), mod4(q + 2)

    def part_of(g, half, q_):
        return H.at[span(base(g) + half * 64, 64), cols(q_)]

    def pass_on(n, half, q_, to):
        each_group(lambda g: send_group(g, lambda g: remote(
            part_of(g, half, q_), part_of(g, half, q_), p2s.at[g, n], p2r.at[g, n], to,
        )))

    def passed(n, half, q_):
        each_group(lambda g: arrived(part_of(g, half, q_), p2s.at[g, n], p2r.at[g, n]))

    my_half = pl.ds(pl.multiple_of(c * HALF, HALF), HALF)

    def logits(slab, q_, first=False):
        rr = slice(slab * VP, (slab + 1) * VP)
        out = lax.dot_general(HD[rr, cols(q_)], H[my_half, cols(q_)], nt, preferred_element_type=F32)
        CP[rr] = out if first else CP[rr] + out

    pass_on(0, 0, q, right)
    pass_on(1, 1, q, left)
    pass_on(2, 1, q, right)
    pass_on(3, 0, q, left)
    load_hid.wait()
    logits(0, q, True)
    turn(0, 0)
    passed(0, 0, before)
    pass_on(4, 0, before, right)
    passed(1, 1, after)
    pass_on(5, 1, after, left)
    turn(0, 1)
    passed(2, 1, before)
    logits(0, before)
    passed(3, 0, after)
    logits(0, after)
    for k in range(3):
        arrived(HD.at[VP + k * 256 : VP + (k + 1) * 256], hs.at[k], hr.at[k])
    logits(1, q, True)
    logits(1, before)
    logits(1, after)
    passed(4, 0, across)
    passed(5, 1, across)
    logits(0, across)
    logits(1, across)

    arrived(RLY, ts.at[2], tr.at[2])
    send(RLY, TR.at[2], ts.at[3], tr.at[3], at_a(mod4(a + way)))

    def share(g):
        return H.at[span(base(g), ROWS)]

    each_group(lambda g: send_group(g, lambda g: remote(share(g), share(g), cs.at[g], cr.at[g], sib)))

    in_slab = lax.broadcasted_iota(jnp.int32, (256, HALF), 0) < SLAB - 512
    student_sum = jnp.zeros((1, HALF), F32)
    for k in range(6):
        rr = slice(k * 256, (k + 1) * 256)
        capped = CAP * jnp.tanh(CP[rr] * (1.0 / CAP))
        exps = jnp.exp(capped)
        if k % 3 == 2:
            exps = jnp.where(in_slab, exps, 0.0)
        CP[rr] = capped
        ES[rr] = exps
        student_sum = student_sum + jnp.sum(exps, axis=0, keepdims=True)
    my_rows = (mod4(a + 2 * c), mod4(a + 2 * c + 1))
    for i in range(2):
        TT[pl.ds(my_rows[i], 1)] = student_sum[:, i * 128 : (i + 1) * 128]

    def exchange_start(tile, slots, ssem, rsem, me, at):
        for k in range(1, 16):
            send(tile, slots.at[me], ssem.at[k - 1], rsem.at[k - 1], at(lax.rem(me + k, 16)))

    def exchange_end(tile, slots, ssem, rsem, me):
        slots[me] = tile[...]
        for k in range(1, 16):
            arrived(slots.at[lax.rem(me + 16 - k, 16)], ssem.at[k - 1], rsem.at[k - 1])
        total = slots[0]
        for k in range(1, 16):
            total = total + slots[k]
        return total

    exchange_start(TT, TG1, as1, ar1, me_xy, at_xy)

    def factors(slab, cross_sum):
        for k in range(6):
            rr = slice(slab * VP + k * 128, slab * VP + (k + 1) * 128)
            vv = slice(k * 128, (k + 1) * 128)
            if slab == 0:
                target = jnp.concatenate([TR[2 * c, vv], TR[2 * c + 1, vv]], axis=1).astype(F32)
            else:
                target = jnp.concatenate([TSIB[0, vv], TSIB[1, vv]], axis=1).astype(F32)
            expd = jnp.exp(target)
            capped = CP[rr]
            cross_sum = cross_sum + jnp.sum(expd * (target - capped), axis=0, keepdims=True)
            ratio = capped * (1.0 / CAP)
            slope = 1.0 - ratio * ratio
            ES[rr] = ES[rr] * slope
            CP[rr] = expd * slope
        return cross_sum

    turn(1, 0)
    TT2[...] = exchange_end(TT, TG1, as1, ar1, me_xy)
    exchange_start(TT2, TG2, as2, ar2, me_zc, at_zc)
    arrived(TR.at[3], ts.at[0], tr.at[0])
    arrived(TR.at[1], ts.at[1], tr.at[1])
    arrived(TR.at[2], ts.at[3], tr.at[3])
    send(TR.at[pl.ds(2 * (1 - c), 2)], TSIB, ts.at[4], tr.at[4], sib)
    cross_sum = factors(0, jnp.zeros((1, HALF), F32))
    turn(1, 1)
    arrived(TSIB, ts.at[4], tr.at[4])
    cross_sum = factors(1, cross_sum)
    TOT[...] = exchange_end(TT2, TG2, as2, ar2, me_zc)

    valid = TOT[8:12] * (1.0 / 64.0)
    weight = valid * (512.0 / jnp.sum(valid))
    AL[0:4] = weight / TOT[0:4]
    BE[0:4] = weight / TOT[4:8]
    alpha = jnp.concatenate([AL[pl.ds(r, 1)] for r in my_rows], axis=1)
    beta = jnp.concatenate([BE[pl.ds(r, 1)] for r in my_rows], axis=1)
    for k in range(12):
        rr = slice(k * 128, (k + 1) * 128)
        grad = (ES[rr] * alpha - CP[rr] * beta).astype(BF16)
        GV[rr] = grad
        if k < 6:
            GTD[rr, my_half] = grad

    up, down, far = mod4(p + 1), mod4(p - 1), mod4(p + 2)

    def partial(n, p_):
        rows = []
        for i in range(4):
            rows.append(HDT[n, jnp.where(c == 0, i, p_), jnp.where(c == 0, p_, i)])
        return jnp.dot(jnp.concatenate(rows, axis=0), GV[...], preferred_element_type=F32)

    def put(ref, n, block):
        for i in range(4):
            ref[n, i] = block[i * CHIPCOL : (i + 1) * CHIPCOL].astype(ref.dtype)

    put(B1, 0, partial(0, far))
    send(B1.at[0], R1.at[0], q1s.at[0], q1r.at[0], at_p(up))
    put(B1, 1, partial(1, far))
    send(B1.at[1], R1.at[1], q1s.at[1], q1r.at[1], at_p(down))
    put(B1, 3, partial(0, down))
    send(B1.at[3], R1.at[3], q1s.at[3], q1r.at[3], at_p(down))
    put(B1, 2, partial(1, up))
    send(B1.at[2], R1.at[2], q1s.at[2], q1r.at[2], at_p(up))
    send(GV.at[VP : 2 * VP], GTD.at[:, my_half], gs.at[0], gr.at[0], sib)
    put(NEXT, 0, partial(0, up))
    put(NEXT, 1, partial(1, down))

    CR[...] = jnp.zeros_like(CR)
    for i in range(2):
        CR[pl.ds(my_rows[i], 1)] = cross_sum[:, i * 128 : (i + 1) * 128]
    exchange_start(CR, CG1, bs1, br1, me_xy, at_xy)

    def head_chunk(n):
        at = pl.ds(pl.multiple_of(n * 512, 512), 512)
        out = jnp.dot(GTD[...], H[:, at], preferred_element_type=F32)
        DH[:, at] = out[:SLAB].astype(BF16)

    def head_chunks(first, last):
        @pl.loop(first, last)
        def _(n):
            head_chunk(n)

    def relay(k):
        arrived(R1.at[k], q1s.at[k], q1r.at[k])
        near = up if k == 0 else down

        @pl.loop(0, 4)
        def _(i):
            F1[k, i] = (NEXT[k, i] + R1[k, i].astype(F32)).astype(BF16)

        send(F1.at[k], R1.at[4 + k], q1s.at[4 + k], q1r.at[4 + k], at_p(near))

    def second(k):
        arrived(R1.at[3 - k], q1s.at[3 - k], q1r.at[3 - k])
        arrived(R1.at[4 + k], q1s.at[4 + k], q1r.at[4 + k])

        @pl.loop(0, 4)
        def _(i):
            total = OWN[k, i] + R1[3 - k, i].astype(F32) + R1[4 + k, i].astype(F32)
            OWN[k, i] = total
            B2[k, i] = total.astype(BF16)

        for d in (2, 1, 3):
            n = k * 3 + d - 1
            to = mod4(q + d)
            send(B2.at[k, to], R2.at[k, d - 1], q2s.at[n], q2r.at[n], at_q(to))

    relay(0)
    put(OWN, 0, partial(0, p))
    put(OWN, 1, partial(1, p))
    relay(1)
    arrived(GTD.at[:, pl.ds(pl.multiple_of((1 - c) * HALF, HALF), HALF)], gs.at[0], gr.at[0])

    arrived(H.at[span(ROWS + (1 - c) * ROWS, ROWS)], cs.at[0], cr.at[0])

    @pl.when(c == 0)
    def _():
        arrived(H.at[3 * ROWS : 4 * ROWS], cs.at[1], cr.at[1])

    head_chunks(0, 2)
    head_chunks(2, 5)
    second(0)
    head_chunks(5, 6)
    second(1)
    CR2[...] = exchange_end(CR, CG1, bs1, br1, me_xy)
    exchange_start(CR2, CG2, bs2, br2, me_zc, at_zc)
    head_chunks(6, 7)

    at_home = (c == 0) & (zl == 0)
    at_home_hi = (c == 0) & (zl == 1)

    def to_owner(k, i, c_):
        n = k * 4 + i * 2 + c_
        return pltpu.make_async_remote_copy(
            src_ref=B3.at[k, i, c_], dst_ref=RZ.at[z], send_sem=rzs.at[n], recv_sem=rzr.at[z],
            device_id=dev(mod4(a + 2 * c + i), k, y, x, c_), device_id_type=MESH,
        )

    owners = [(k, i, c_) for k in range(2) for i in range(2) for c_ in range(2)]
    for k in range(2):
        total = OWN[k, q]
        for d in range(1, 4):
            arrived(R2.at[k, d - 1], q2s.at[k * 3 + d - 1], q2r.at[k * 3 + d - 1])
            total = total + R2[k, d - 1].astype(F32)
        for i in range(2):
            for c_ in range(2):
                B3[k, i, c_] = total[48 * c_ : 48 * c_ + 64, i * 128 : (i + 1) * 128].astype(BF16)
                if i == 0 and c_ == 0:
                    home = at_home if k == 0 else at_home_hi

                    @pl.when(jnp.logical_not(home))
                    def _():
                        to_owner(k, i, c_).start()

                    @pl.when(home)
                    def _():
                        RZ[z] = B3[k, 0, 0]
                else:
                    to_owner(k, i, c_).start()

    cross = exchange_end(CR2, CG2, bs2, br2, me_zc)
    KL[0:4] = cross[0:4] / TOT[4:8] - jnp.log(TOT[4:8]) + jnp.log(TOT[0:4])
    kl_out[...] = KL[pl.ds(a, 1)]

    for copy in pending:
        copy.wait_send()

    @pl.when(c == 1)
    def _():
        for make in later:
            make().wait_send()

    for k, i, c_ in owners:
        if i == 0 and c_ == 0:
            home = at_home if k == 0 else at_home_hi

            @pl.when(jnp.logical_not(home))
            def _():
                to_owner(k, i, c_).wait_send()
        else:
            to_owner(k, i, c_).wait_send()

    @pl.when(c == 1)
    def _():
        arrived(RZ.at[z], rzs.at[0], rzr.at[z])

    for k in range(1, 8):
        source = lax.rem(z + k, 8)
        arrived(RZ.at[source], rzs.at[0], rzr.at[source])
    total = RZ[0].astype(F32)
    for k in range(1, 8):
        total = total + RZ[k].astype(F32)
    dhid_out[...] = jnp.where(c == 0, total[0:56], total[8:64]).astype(BF16)


def on_device(hidden, valid_mask, student_head, teacher_logits):
    vm = pltpu.VMEM
    dma = pltpu.SemaphoreType.DMA
    any_spec = pl.BlockSpec(memory_space=pl.ANY)
    vmem_spec = pl.BlockSpec(memory_space=pltpu.VMEM)
    kl, dhid, dhead = pl.pallas_call(
        kernel,
        out_shape=(vm((1, ROWS), F32), vm((56, ROWS), BF16), vm((SLAB, D), BF16)),
        in_specs=[any_spec, vmem_spec, any_spec, any_spec],
        out_specs=(vmem_spec, vmem_spec, vmem_spec),
        scratch_shapes=[
            vm((512, D), BF16),
            vm((2 * VP, D), BF16),
            vm((2, 4, 4, CHIPCOL, 2 * VP), BF16),
            vm((256, 256), BF16),
            vm((3000, ROWS), BF16),
            vm((4, VP, ROWS), BF16),
            vm((4, VP, ROWS), BF16),
            vm((VP, ROWS), BF16),
            vm((2, VP, ROWS), BF16),
            vm((2 * VP, HALF), F32),
            vm((2 * VP, HALF), F32),
            vm((2 * VP, HALF), BF16),
            vm((VP, 512), BF16),
            vm((16, 128), F32),
            vm((16, 16, 128), F32),
            vm((16, 128), F32),
            vm((16, 16, 128), F32),
            vm((16, 128), F32),
            vm((8, 128), F32),
            vm((8, 128), F32),
            vm((8, 128), F32),
            vm((16, 8, 128), F32),
            vm((8, 128), F32),
            vm((16, 8, 128), F32),
            vm((8, 128), F32),
            vm((2, 4, CHIPCOL, HALF), F32),
            vm((2, 4, CHIPCOL, HALF), F32),
            vm((4, 4, CHIPCOL, HALF), BF16),
            vm((6, 4, CHIPCOL, HALF), BF16),
            vm((2, 4, CHIPCOL, HALF), BF16),
            vm((2, 4, CHIPCOL, HALF), BF16),
            vm((2, 3, CHIPCOL, HALF), BF16),
            vm((2, 2, 2, 64, 128), BF16),
            vm((8, 64, 128), BF16),
            dma((3,)),
            dma((3,)), dma((3,)),
            dma((2,)), dma((2,)),
            dma((2, 3)), dma((2, 3)), dma((2, 6)), dma((2, 6)),
            dma((2,)), dma((2,)),
            dma((5,)), dma((5,)),
            dma((1,)), dma((1,)),
            dma((15,)), dma((15,)), dma((15,)), dma((15,)),
            dma((15,)), dma((15,)), dma((15,)), dma((15,)),
            dma((6,)), dma((6,)), dma((6,)), dma((6,)),
            dma((8,)), dma((8,)),
        ],
        compiler_params=pltpu.CompilerParams(
            collective_id=0, has_side_effects=True, vmem_limit_bytes=50 * 1024 * 1024
        ),
        cost_estimate=pl.CostEstimate(flops=3 * 2 * 512 * 750 * 3584, bytes_accessed=13_000_000, transcendentals=0),
    )(hidden, valid_mask.reshape(1, ROWS), student_head, teacher_logits.T)
    return kl.reshape(ROWS), dhid.T, dhead


def solution(mesh):
    return jax.shard_map(
        on_device,
        mesh=mesh,
        in_specs=(P("tok", None), P("tok"), P(("voc", "tok"), None), P("tok", "voc")),
        out_specs=(P("tok"), P("tok", "voc"), P(("voc", "tok"), None)),
        check_vma=False,
    )
```

```python
import jax
import jax.numpy as jnp
from jax import lax
from jax.experimental import pallas as pl
from jax.experimental.pallas import tpu as pltpu
from jax.sharding import PartitionSpec as P

CAP = 30.0
D = 3584
ROWS = 128
HALF = 256
SLAB = 750
VP = 768
QCOL = D // 4
PIECE = ROWS // 4
CHIPCOL = 112
MESH = pl.DeviceIdType.MESH
F32 = jnp.float32
BF16 = jnp.bfloat16


def kernel(
    hid, mask, head, teach, kl_out, dhid_out, DH,
    H, HD, HDT, EYE, tin, TS, TR, RLY, TSIB, CP, ES, GV, GTD,
    TT, TG1, TT2, TG2, TOT, AL, BE, CR, CG1, CR2, CG2, KL,
    OWN, NEXT, B1, R1, F1, B2, R2, B3, RZ,
    local, hs, hr, zs, zr, p1s, p1r, p2s, p2r, cs, cr, ts, tr, gs, gr,
    as1, ar1, as2, ar2, bs1, br1, bs2, br2, q1s, q1r, f1s, f1r, q2s, q2r, rzs, rzr,
):
    a = lax.axis_index("tok")
    v = lax.axis_index("voc")
    c = lax.rem(v, 2)
    x = lax.rem(v // 2, 4)
    y = lax.rem(v // 8, 4)
    zl = v // 32
    z = 2 * a + zl
    p = jnp.where(c == 0, x, y)
    q = jnp.where(c == 0, y, x)

    def dev(a_, zl_, y_, x_, c_):
        return (a_, zl_ * 32 + y_ * 8 + x_ * 2 + c_)

    def at_p(p_):
        return dev(a, zl, jnp.where(c == 0, y, p_), jnp.where(c == 0, p_, x), c)

    def at_q(q_):
        return dev(a, zl, jnp.where(c == 0, q_, y), jnp.where(c == 0, x, q_), c)

    sib = dev(a, zl, y, x, 1 - c)

    def at_a(a_):
        return dev(a_, zl, y, x, c)

    def at_xy(k):
        return dev(a, zl, k // 4, lax.rem(k, 4), c)

    def at_zc(k):
        return dev(k // 4, lax.rem(k // 2, 2), y, x, lax.rem(k, 2))

    def mod4(k):
        return lax.rem(k + 8, 4)

    me_xy = y * 4 + x
    me_zc = z * 2 + c

    pending = []

    def send(src, dst, ssem, rsem, to):
        copy = pltpu.make_async_remote_copy(
            src_ref=src, dst_ref=dst, send_sem=ssem, recv_sem=rsem, device_id=to, device_id_type=MESH
        )
        copy.start()
        pending.append(copy)

    def arrived(dst, ssem, rsem):
        pltpu.make_async_remote_copy(
            src_ref=dst, dst_ref=dst, send_sem=ssem, recv_sem=rsem, device_id=sib, device_id_type=MESH
        ).wait_recv()

    load_teach = pltpu.make_async_copy(teach, tin, local.at[0])
    load_teach.start()
    load_hid = pltpu.make_async_copy(hid, H.at[pl.ds(0, ROWS)], local.at[1])
    load_hid.start()

    barrier = pltpu.get_barrier_semaphore()
    for k in range(1, 16):
        pl.semaphore_signal(barrier, inc=1, device_id=at_xy(lax.rem(me_xy + k, 16)), device_id_type=MESH)
        pl.semaphore_signal(barrier, inc=1, device_id=at_zc(lax.rem(me_zc + k, 16)), device_id_type=MESH)
    pl.semaphore_wait(barrier, 30)

    def span(start, size):
        return pl.ds(pl.multiple_of(start, 16), size)

    def cols(q_):
        return pl.ds(pl.multiple_of(q_ * QCOL, 128), QCOL)

    def base(g):
        return ROWS + c * ROWS + g * ROWS

    later = []

    def each_group(step):
        step(0)

        @pl.when(c == 1)
        def _():
            step(1)

    def send_group(g, make):
        copy = make(g)
        copy.start()
        if g == 0:
            pending.append(copy)
        else:
            later.append(lambda: make(1))

    def remote(src, dst, ssem, rsem, to):
        return pltpu.make_async_remote_copy(
            src_ref=src, dst_ref=dst, send_sem=ssem, recv_sem=rsem, device_id=to, device_id_type=MESH
        )

    each_group(lambda g: send_group(g, lambda g: remote(
        hid.at[span(p * PIECE, PIECE), cols(q)], H.at[span(base(g) + p * PIECE, PIECE), cols(q)],
        zs.at[g], zr.at[g], at_a(mod4(a - 1 - c - g)),
    )))

    load_head = pltpu.make_async_copy(head.at[pl.ds(0, 736)], HD.at[0:736], local.at[2])
    load_head.start()
    send(head.at[pl.ds(0, 736)], HD.at[VP : VP + 736], hs.at[0], hr.at[0], sib)
    load_tail = pltpu.make_async_copy(head, DH, local.at[3])
    load_tail.start()

    load_teach.wait()
    place = lax.broadcasted_iota(jnp.int32, (VP, ROWS), 0)
    teacher_sum = jnp.zeros((1, ROWS), F32)
    for t in range(4):
        start = t * SLAB // 16 * 16
        off = t * SLAB - start
        height = min(VP + 16, 3000 - start)
        tall = tin[start : start + height].astype(F32)
        if height < VP + 16:
            tall = jnp.concatenate([tall, jnp.zeros((VP + 16 - height, ROWS), F32)], axis=0)
        if off:
            tall = pltpu.roll(tall, VP + 16 - off, 0)
        part = jnp.where(place < SLAB, tall[:VP], -30000.0)
        TS[t] = part.astype(BF16)
        teacher_sum = teacher_sum + jnp.sum(jnp.exp(part), axis=0, keepdims=True)
    way = jnp.where(c == 0, 1, 3)
    send(TS.at[mod4(a + 2)], RLY, ts.at[2], tr.at[2], at_a(mod4(a + way)))
    TR[0] = TS[a]

    TT[...] = jnp.zeros_like(TT)
    TT[pl.ds(4 + a, 1)] = teacher_sum
    TT[pl.ds(8 + a, 1)] = mask[...].astype(F32)

    nt = (((1,), (1,)), ((), ()))
    EYE[...] = jnp.where(
        lax.broadcasted_iota(jnp.int32, (256, 256), 0) == lax.broadcasted_iota(jnp.int32, (256, 256), 1), 1.0, 0.0
    ).astype(BF16)

    def turn(slab, half):
        for n in range(7):
            at = pl.ds(half * 1792 + n * 256, 256)
            out = lax.dot_general(
                EYE[...], HD[slab * VP : (slab + 1) * VP, at], nt, preferred_element_type=F32
            ).astype(BF16)
            done = 0
            while done < 256:
                chip, row = divmod(n * 256 + done, CHIPCOL)
                size = min(CHIPCOL - row, 256 - done)
                HDT[half, chip // 4, chip % 4, row : row + size, slab * VP : (slab + 1) * VP] = out[done : done + size]
                done += size

    def piece(g, p_):
        return H.at[span(base(g) + p_ * PIECE, PIECE), cols(q)]

    def first_step(g):
        arrived(piece(g, p), zs.at[g], zr.at[g])
        for d in range(1, 4):
            send_group(g, lambda g, d=d: remote(
                piece(g, p), piece(g, p), p1s.at[g, d - 1], p1r.at[g, d - 1], at_p(mod4(p + d)),
            ))

    each_group(first_step)

    load_tail.wait()
    HD[736:768] = jnp.concatenate([DH[736:750].astype(F32), jnp.zeros((18, D), F32)], axis=0).astype(BF16)
    send(HD.at[736:768], HD.at[VP + 736 : VP + 768], hs.at[1], hr.at[1], sib)
    load_head.wait()

    def first_end(g):
        for d in range(1, 4):
            arrived(piece(g, mod4(p - d)), p1s.at[g, d - 1], p1r.at[g, d - 1])

    right, left = at_q(mod4(q + 1)), at_q(mod4(q - 1))
    before, after, across = mod4(q - 1), mod4(q + 1), mod4(q + 2)

    def part_of(g, half, q_):
        return H.at[span(base(g) + half * 64, 64), cols(q_)]

    def pass_on(g, n, half, q_, to):
        send_group(g, lambda g: remote(part_of(g, half, q_), part_of(g, half, q_), p2s.at[g, n], p2r.at[g, n], to))

    def passed(n, half, q_):
        each_group(lambda g: arrived(part_of(g, half, q_), p2s.at[g, n], p2r.at[g, n]))

    def second_step(g):
        first_end(g)
        pass_on(g, 0, 0, q, right)
        pass_on(g, 1, 1, q, left)
        pass_on(g, 2, 1, q, right)
        pass_on(g, 3, 0, q, left)

    def relay_step(g):
        arrived(part_of(g, 0, before), p2s.at[g, 0], p2r.at[g, 0])
        pass_on(g, 4, 0, before, right)
        arrived(part_of(g, 1, after), p2s.at[g, 1], p2r.at[g, 1])
        pass_on(g, 5, 1, after, left)

    each_group(second_step)
    send(TS.at[mod4(a + 1)], TR.at[3], ts.at[0], tr.at[0], at_a(mod4(a + 1)))
    send(TS.at[mod4(a + 3)], TR.at[1], ts.at[1], tr.at[1], at_a(mod4(a + 3)))

    my_half = pl.ds(pl.multiple_of(c * HALF, HALF), HALF)

    def logits(slab, q_, first=False):
        rr = slice(slab * VP, (slab + 1) * VP)
        out = lax.dot_general(HD[rr, cols(q_)], H[my_half, cols(q_)], nt, preferred_element_type=F32)
        CP[rr] = out if first else CP[rr] + out

    load_hid.wait()
    logits(0, q, True)
    turn(0, 0)
    each_group(relay_step)

    arrived(RLY, ts.at[2], tr.at[2])
    send(RLY, TR.at[2], ts.at[3], tr.at[3], at_a(mod4(a + way)))
    turn(0, 1)
    passed(2, 1, before)
    logits(0, before)
    passed(3, 0, after)
    logits(0, after)
    arrived(HD.at[VP : VP + 736], hs.at[0], hr.at[0])
    arrived(HD.at[VP + 736 : VP + 768], hs.at[1], hr.at[1])
    logits(1, q, True)
    logits(1, before)
    logits(1, after)
    passed(4, 0, across)
    passed(5, 1, across)
    in_slab = lax.broadcasted_iota(jnp.int32, (256, HALF), 0) < SLAB - 512

    def exponentials(slab, student_sum):
        for k in range(3):
            rr = slice(slab * VP + k * 256, slab * VP + (k + 1) * 256)
            capped = CAP * jnp.tanh(CP[rr] * (1.0 / CAP))
            exps = jnp.exp(capped)
            if k == 2:
                exps = jnp.where(in_slab, exps, 0.0)
            CP[rr] = capped
            ES[rr] = exps
            student_sum = student_sum + jnp.sum(exps, axis=0, keepdims=True)
        return student_sum

    logits(0, across)
    logits(1, across)
    student_sum = exponentials(0, jnp.zeros((1, HALF), F32))
    student_sum = exponentials(1, student_sum)
    my_rows = (mod4(a + 2 * c), mod4(a + 2 * c + 1))
    for i in range(2):
        TT[pl.ds(my_rows[i], 1)] = student_sum[:, i * 128 : (i + 1) * 128]

    def exchange_start(tile, slots, ssem, rsem, me, at):
        for k in range(1, 16):
            send(tile, slots.at[me], ssem.at[k - 1], rsem.at[k - 1], at(lax.rem(me + k, 16)))

    def exchange_end(tile, slots, ssem, rsem, me):
        slots[me] = tile[...]
        for k in range(1, 16):
            arrived(slots.at[lax.rem(me + 16 - k, 16)], ssem.at[k - 1], rsem.at[k - 1])
        total = slots[0]
        for k in range(1, 16):
            total = total + slots[k]
        return total

    exchange_start(TT, TG1, as1, ar1, me_xy, at_xy)

    def share(g):
        return H.at[span(base(g), ROWS)]

    each_group(lambda g: send_group(g, lambda g: remote(share(g), share(g), cs.at[g], cr.at[g], sib)))

    def factors(slab, cross_sum):
        for k in range(6):
            rr = slice(slab * VP + k * 128, slab * VP + (k + 1) * 128)
            vv = slice(k * 128, (k + 1) * 128)
            if slab == 0:
                target = jnp.concatenate([TR[2 * c, vv], TR[2 * c + 1, vv]], axis=1).astype(F32)
            else:
                target = jnp.concatenate([TSIB[0, vv], TSIB[1, vv]], axis=1).astype(F32)
            expd = jnp.exp(target)
            capped = CP[rr]
            cross_sum = cross_sum + jnp.sum(expd * (target - capped), axis=0, keepdims=True)
            ratio = capped * (1.0 / CAP)
            slope = 1.0 - ratio * ratio
            ES[rr] = ES[rr] * slope
            CP[rr] = expd * slope
        return cross_sum

    turn(1, 0)

    def give(i):
        send(TR.at[2 * (1 - c) + i], TSIB.at[i], ts.at[4 + i], tr.at[4 + i], sib)

    arrived(TR.at[3], ts.at[0], tr.at[0])
    arrived(TR.at[1], ts.at[1], tr.at[1])
    give(1)
    TT2[...] = exchange_end(TT, TG1, as1, ar1, me_xy)
    exchange_start(TT2, TG2, as2, ar2, me_zc, at_zc)
    arrived(TR.at[2], ts.at[3], tr.at[3])
    give(0)
    cross_sum = factors(0, jnp.zeros((1, HALF), F32))
    turn(1, 1)
    for i in range(2):
        arrived(TSIB.at[i], ts.at[4 + i], tr.at[4 + i])
    cross_sum = factors(1, cross_sum)
    TOT[...] = exchange_end(TT2, TG2, as2, ar2, me_zc)

    valid = TOT[8:12] * (1.0 / 64.0)
    weight = valid * (512.0 / jnp.sum(valid))
    AL[0:4] = weight / TOT[0:4]
    BE[0:4] = weight / TOT[4:8]
    alpha = jnp.concatenate([AL[pl.ds(r, 1)] for r in my_rows], axis=1)
    beta = jnp.concatenate([BE[pl.ds(r, 1)] for r in my_rows], axis=1)
    for k in range(12):
        rr = slice(k * 128, (k + 1) * 128)
        grad = (ES[rr] * alpha - CP[rr] * beta).astype(BF16)
        GV[rr] = grad
        if k < 6:
            GTD[rr, my_half] = grad

    up, down, far = mod4(p + 1), mod4(p - 1), mod4(p + 2)

    def partial(n, p_):
        rows = []
        for i in range(4):
            rows.append(HDT[n, jnp.where(c == 0, i, p_), jnp.where(c == 0, p_, i)])
        return jnp.dot(jnp.concatenate(rows, axis=0), GV[...], preferred_element_type=F32)

    def put(ref, n, block):
        for i in range(4):
            ref[n, i] = block[i * CHIPCOL : (i + 1) * CHIPCOL].astype(ref.dtype)

    put(B1, 0, partial(0, far))
    send(B1.at[0], R1.at[0], q1s.at[0], q1r.at[0], at_p(up))
    put(B1, 1, partial(1, far))
    send(B1.at[1], R1.at[1], q1s.at[1], q1r.at[1], at_p(down))
    put(B1, 3, partial(0, down))
    send(B1.at[3], R1.at[3], q1s.at[3], q1r.at[3], at_p(down))
    put(B1, 2, partial(1, up))
    send(B1.at[2], R1.at[2], q1s.at[2], q1r.at[2], at_p(up))
    send(GV.at[VP : 2 * VP], GTD.at[:, my_half], gs.at[0], gr.at[0], sib)
    put(NEXT, 0, partial(0, up))
    put(NEXT, 1, partial(1, down))

    CR[...] = jnp.zeros_like(CR)
    for i in range(2):
        CR[pl.ds(my_rows[i], 1)] = cross_sum[:, i * 128 : (i + 1) * 128]
    exchange_start(CR, CG1, bs1, br1, me_xy, at_xy)

    def head_chunk(n):
        at = pl.ds(pl.multiple_of(n * 512, 512), 512)
        out = jnp.dot(GTD[...], H[:, at], preferred_element_type=F32)
        DH[:, at] = out[:SLAB].astype(BF16)

    def head_chunks(first, last):
        @pl.loop(first, last)
        def _(n):
            head_chunk(n)

    qup, qdown, qfar = mod4(q + 1), mod4(q - 1), mod4(q + 2)
    order = (qfar, qup, qdown, q)

    def relay(k):
        arrived(R1.at[k], q1s.at[k], q1r.at[k])
        near = up if k == 0 else down
        for n, i in enumerate(order):
            F1[k, i] = (NEXT[k, i] + R1[k, i].astype(F32)).astype(BF16)
            send(F1.at[k, i], R1.at[4 + k, i], f1s.at[k, n], f1r.at[k, n], at_p(near))

    def second(k, n):
        i = order[n]
        arrived(R1.at[4 + k, i], f1s.at[k, n], f1r.at[k, n])
        total = OWN[k, i] + R1[3 - k, i].astype(F32) + R1[4 + k, i].astype(F32)
        if n == 3:
            OWN[k, i] = total
        else:
            B2[k, i] = total.astype(BF16)
            send(B2.at[k, i], R2.at[k, n], q2s.at[k * 3 + n], q2r.at[k * 3 + n], at_q(i))

    relay(0)
    relay(1)
    put(OWN, 0, partial(0, p))
    put(OWN, 1, partial(1, p))
    arrived(GTD.at[:, pl.ds(pl.multiple_of((1 - c) * HALF, HALF), HALF)], gs.at[0], gr.at[0])
    arrived(H.at[span(ROWS + (1 - c) * ROWS, ROWS)], cs.at[0], cr.at[0])

    @pl.when(c == 0)
    def _():
        arrived(H.at[3 * ROWS : 4 * ROWS], cs.at[1], cr.at[1])

    head_chunks(0, 2)
    arrived(R1.at[3], q1s.at[3], q1r.at[3])
    arrived(R1.at[2], q1s.at[2], q1r.at[2])
    for n in range(4):
        for k in range(2):
            second(k, n)
    CR2[...] = exchange_end(CR, CG1, bs1, br1, me_xy)
    exchange_start(CR2, CG2, bs2, br2, me_zc, at_zc)
    head_chunks(2, 4)

    at_home = (c == 0) & (zl == 0)
    at_home_hi = (c == 0) & (zl == 1)

    def to_owner(k, i, c_):
        n = k * 4 + i * 2 + c_
        return pltpu.make_async_remote_copy(
            src_ref=B3.at[k, i, c_], dst_ref=RZ.at[z], send_sem=rzs.at[n], recv_sem=rzr.at[z],
            device_id=dev(mod4(a + 2 * c + i), k, y, x, c_), device_id_type=MESH,
        )

    owners = [(k, i, c_) for k in range(2) for i in range(2) for c_ in range(2)]
    for k in range(2):
        total = OWN[k, q]
        for n in range(3):
            arrived(R2.at[k, n], q2s.at[k * 3 + n], q2r.at[k * 3 + n])
            total = total + R2[k, n].astype(F32)
        for i in range(2):
            for c_ in range(2):
                B3[k, i, c_] = total[48 * c_ : 48 * c_ + 64, i * 128 : (i + 1) * 128].astype(BF16)
                if i == 0 and c_ == 0:
                    home = at_home if k == 0 else at_home_hi

                    @pl.when(jnp.logical_not(home))
                    def _():
                        to_owner(k, i, c_).start()

                    @pl.when(home)
                    def _():
                        RZ[z] = B3[k, 0, 0]
                else:
                    to_owner(k, i, c_).start()

    head_chunks(4, 7)
    cross = exchange_end(CR2, CG2, bs2, br2, me_zc)
    KL[0:4] = cross[0:4] / TOT[4:8] - jnp.log(TOT[4:8]) + jnp.log(TOT[0:4])
    kl_out[...] = KL[pl.ds(a, 1)]

    for copy in pending:
        copy.wait_send()

    @pl.when(c == 1)
    def _():
        for make in later:
            make().wait_send()

    for k, i, c_ in owners:
        if i == 0 and c_ == 0:
            home = at_home if k == 0 else at_home_hi

            @pl.when(jnp.logical_not(home))
            def _():
                to_owner(k, i, c_).wait_send()
        else:
            to_owner(k, i, c_).wait_send()

    @pl.when(c == 1)
    def _():
        arrived(RZ.at[z], rzs.at[0], rzr.at[z])

    for k in range(1, 8):
        source = lax.rem(z + k, 8)
        arrived(RZ.at[source], rzs.at[0], rzr.at[source])
    total = RZ[0].astype(F32)
    for k in range(1, 8):
        total = total + RZ[k].astype(F32)
    dhid_out[...] = jnp.where(c == 0, total[0:56], total[8:64]).astype(BF16)


def on_device(hidden, valid_mask, student_head, teacher_logits):
    vm = pltpu.VMEM
    dma = pltpu.SemaphoreType.DMA
    any_spec = pl.BlockSpec(memory_space=pl.ANY)
    vmem_spec = pl.BlockSpec(memory_space=pltpu.VMEM)
    kl, dhid, dhead = pl.pallas_call(
        kernel,
        out_shape=(vm((1, ROWS), F32), vm((56, ROWS), BF16), vm((SLAB, D), BF16)),
        in_specs=[any_spec, vmem_spec, any_spec, any_spec],
        out_specs=(vmem_spec, vmem_spec, vmem_spec),
        scratch_shapes=[
            vm((512, D), BF16),
            vm((2 * VP, D), BF16),
            vm((2, 4, 4, CHIPCOL, 2 * VP), BF16),
            vm((256, 256), BF16),
            vm((3000, ROWS), BF16),
            vm((4, VP, ROWS), BF16),
            vm((4, VP, ROWS), BF16),
            vm((VP, ROWS), BF16),
            vm((2, VP, ROWS), BF16),
            vm((2 * VP, HALF), F32),
            vm((2 * VP, HALF), F32),
            vm((2 * VP, HALF), BF16),
            vm((VP, 512), BF16),
            vm((16, 128), F32),
            vm((16, 16, 128), F32),
            vm((16, 128), F32),
            vm((16, 16, 128), F32),
            vm((16, 128), F32),
            vm((8, 128), F32),
            vm((8, 128), F32),
            vm((8, 128), F32),
            vm((16, 8, 128), F32),
            vm((8, 128), F32),
            vm((16, 8, 128), F32),
            vm((8, 128), F32),
            vm((2, 4, CHIPCOL, HALF), F32),
            vm((2, 4, CHIPCOL, HALF), F32),
            vm((4, 4, CHIPCOL, HALF), BF16),
            vm((6, 4, CHIPCOL, HALF), BF16),
            vm((2, 4, CHIPCOL, HALF), BF16),
            vm((2, 4, CHIPCOL, HALF), BF16),
            vm((2, 3, CHIPCOL, HALF), BF16),
            vm((2, 2, 2, 64, 128), BF16),
            vm((8, 64, 128), BF16),
            dma((4,)),
            dma((2,)), dma((2,)),
            dma((2,)), dma((2,)),
            dma((2, 3)), dma((2, 3)), dma((2, 6)), dma((2, 6)),
            dma((2,)), dma((2,)),
            dma((6,)), dma((6,)),
            dma((1,)), dma((1,)),
            dma((15,)), dma((15,)), dma((15,)), dma((15,)),
            dma((15,)), dma((15,)), dma((15,)), dma((15,)),
            dma((4,)), dma((4,)), dma((2, 4)), dma((2, 4)), dma((6,)), dma((6,)),
            dma((8,)), dma((8,)),
        ],
        compiler_params=pltpu.CompilerParams(
            collective_id=0, has_side_effects=True, vmem_limit_bytes=50 * 1024 * 1024
        ),
        cost_estimate=pl.CostEstimate(flops=3 * 2 * 512 * 750 * 3584, bytes_accessed=13_000_000, transcendentals=0),
    )(hidden, valid_mask.reshape(1, ROWS), student_head, teacher_logits.T)
    return kl.reshape(ROWS), dhid.T, dhead


def solution(mesh):
    return jax.shard_map(
        on_device,
        mesh=mesh,
        in_specs=(P("tok", None), P("tok"), P(("voc", "tok"), None), P("tok", "voc")),
        out_specs=(P("tok"), P("tok", "voc"), P(("voc", "tok"), None)),
        check_vma=False,
    )
```

```python
import jax
import jax.numpy as jnp
from jax import lax
from jax.experimental import pallas as pl
from jax.experimental.pallas import tpu as pltpu
from jax.sharding import PartitionSpec as P

CAP = 30.0
D = 3584
ROWS = 128
HALF = 256
SLAB = 750
VP = 768
QCOL = D // 4
PIECE = ROWS // 4
CHIPCOL = 112
MESH = pl.DeviceIdType.MESH
F32 = jnp.float32
BF16 = jnp.bfloat16


def kernel(
    hid, mask, head, teach, kl_out, dhid_out, DH,
    H, HD, HDT, EYE, tin, TS, TR, RLY, TSIB, CP, ES, GV, GTD,
    TT, TG1, TT2, TG2, TOT, AL, BE, CR, CG1, CR2, CG2, KL,
    OWN, NEXT, B1, R1, F1, B2, R2, B3, RZ,
    local, hs, hr, zs, zr, p1s, p1r, p2s, p2r, cs, cr, ts, tr, gs, gr,
    as1, ar1, as2, ar2, bs1, br1, bs2, br2, q1s, q1r, f1s, f1r, q2s, q2r, rzs, rzr,
):
    a = lax.axis_index("tok")
    v = lax.axis_index("voc")
    c = lax.rem(v, 2)
    x = lax.rem(v // 2, 4)
    y = lax.rem(v // 8, 4)
    zl = v // 32
    z = 2 * a + zl
    p = jnp.where(c == 0, x, y)
    q = jnp.where(c == 0, y, x)

    def dev(a_, zl_, y_, x_, c_):
        return (a_, zl_ * 32 + y_ * 8 + x_ * 2 + c_)

    def at_p(p_):
        return dev(a, zl, jnp.where(c == 0, y, p_), jnp.where(c == 0, p_, x), c)

    def at_q(q_):
        return dev(a, zl, jnp.where(c == 0, q_, y), jnp.where(c == 0, x, q_), c)

    sib = dev(a, zl, y, x, 1 - c)

    def at_a(a_):
        return dev(a_, zl, y, x, c)

    def at_xy(k):
        return dev(a, zl, k // 4, lax.rem(k, 4), c)

    def at_zc(k):
        return dev(k // 4, lax.rem(k // 2, 2), y, x, lax.rem(k, 2))

    def mod4(k):
        return lax.rem(k + 8, 4)

    me_xy = y * 4 + x
    me_zc = z * 2 + c

    pending = []

    def send(src, dst, ssem, rsem, to):
        copy = pltpu.make_async_remote_copy(
            src_ref=src, dst_ref=dst, send_sem=ssem, recv_sem=rsem, device_id=to, device_id_type=MESH
        )
        copy.start()
        pending.append(copy)

    def arrived(dst, ssem, rsem):
        pltpu.make_async_remote_copy(
            src_ref=dst, dst_ref=dst, send_sem=ssem, recv_sem=rsem, device_id=sib, device_id_type=MESH
        ).wait_recv()

    barrier = pltpu.get_barrier_semaphore()
    for k in range(1, 16):
        pl.semaphore_signal(barrier, inc=1, device_id=at_zc(lax.rem(me_zc + k, 16)), device_id_type=MESH)
    for k in range(1, 16):
        pl.semaphore_signal(barrier, inc=1, device_id=at_xy(lax.rem(me_xy + k, 16)), device_id_type=MESH)

    load_teach = pltpu.make_async_copy(teach, tin, local.at[0])
    load_teach.start()
    load_hid = pltpu.make_async_copy(hid, H.at[pl.ds(0, ROWS)], local.at[1])
    load_hid.start()

    pl.semaphore_wait(barrier, 30)

    def span(start, size):
        return pl.ds(pl.multiple_of(start, 16), size)

    def cols(q_):
        return pl.ds(pl.multiple_of(q_ * QCOL, 128), QCOL)

    def base(g):
        return ROWS + c * ROWS + g * ROWS

    later = []

    def each_group(step):
        step(0)

        @pl.when(c == 1)
        def _():
            step(1)

    def send_group(g, make):
        copy = make(g)
        copy.start()
        if g == 0:
            pending.append(copy)
        else:
            later.append(lambda: make(1))

    def remote(src, dst, ssem, rsem, to):
        return pltpu.make_async_remote_copy(
            src_ref=src, dst_ref=dst, send_sem=ssem, recv_sem=rsem, device_id=to, device_id_type=MESH
        )

    each_group(lambda g: send_group(g, lambda g: remote(
        hid.at[span(p * PIECE, PIECE), cols(q)], H.at[span(base(g) + p * PIECE, PIECE), cols(q)],
        zs.at[g], zr.at[g],
        dev(mod4(a - 1 - c - g), jnp.where((c == 1) & (g == 0), 1 - zl, zl), y, x, c),
    )))

    load_head = pltpu.make_async_copy(head.at[pl.ds(0, 736)], HD.at[0:736], local.at[2])
    load_head.start()
    send(head.at[pl.ds(0, 736)], HD.at[VP : VP + 736], hs.at[0], hr.at[0], sib)
    load_tail = pltpu.make_async_copy(head, DH, local.at[3])
    load_tail.start()

    load_teach.wait()
    place = lax.broadcasted_iota(jnp.int32, (VP, ROWS), 0)
    teacher_sum = jnp.zeros((1, ROWS), F32)
    for t in range(4):
        start = t * SLAB // 16 * 16
        off = t * SLAB - start
        height = min(VP + 16, 3000 - start)
        tall = tin[start : start + height].astype(F32)
        if height < VP + 16:
            tall = jnp.concatenate([tall, jnp.zeros((VP + 16 - height, ROWS), F32)], axis=0)
        if off:
            tall = pltpu.roll(tall, VP + 16 - off, 0)
        part = jnp.where(place < SLAB, tall[:VP], -30000.0)
        TS[t] = part.astype(BF16)
        teacher_sum = teacher_sum + jnp.sum(jnp.exp(part), axis=0, keepdims=True)
    way = jnp.where(c == 0, 1, 3)
    send(TS.at[mod4(a + 2)], RLY, ts.at[2], tr.at[2], at_a(mod4(a + way)))
    TR[0] = TS[a]

    TT[...] = jnp.zeros_like(TT)
    TT[pl.ds(4 + a, 1)] = teacher_sum
    TT[pl.ds(8 + a, 1)] = mask[...].astype(F32)

    nt = (((1,), (1,)), ((), ()))
    EYE[...] = jnp.where(
        lax.broadcasted_iota(jnp.int32, (256, 256), 0) == lax.broadcasted_iota(jnp.int32, (256, 256), 1), 1.0, 0.0
    ).astype(BF16)

    def turn(slab, half):
        for n in range(7):
            at = pl.ds(half * 1792 + n * 256, 256)
            out = lax.dot_general(
                EYE[...], HD[slab * VP : (slab + 1) * VP, at], nt, preferred_element_type=F32
            ).astype(BF16)
            done = 0
            while done < 256:
                chip, row = divmod(n * 256 + done, CHIPCOL)
                size = min(CHIPCOL - row, 256 - done)
                HDT[half, chip // 4, chip % 4, row : row + size, slab * VP : (slab + 1) * VP] = out[done : done + size]
                done += size

    def piece(g, p_):
        return H.at[span(base(g) + p_ * PIECE, PIECE), cols(q)]

    def first_step(g):
        arrived(piece(g, p), zs.at[g], zr.at[g])
        for d in range(1, 4):
            send_group(g, lambda g, d=d: remote(
                piece(g, p), piece(g, p), p1s.at[g, d - 1], p1r.at[g, d - 1], at_p(mod4(p + d)),
            ))

    each_group(first_step)

    load_tail.wait()
    HD[736:768] = jnp.concatenate([DH[736:750].astype(F32), jnp.zeros((18, D), F32)], axis=0).astype(BF16)
    send(HD.at[736:768], HD.at[VP + 736 : VP + 768], hs.at[1], hr.at[1], sib)
    load_head.wait()
    turn(0, 0)

    def first_end(g):
        for d in range(1, 4):
            arrived(piece(g, mod4(p - d)), p1s.at[g, d - 1], p1r.at[g, d - 1])

    right, left = at_q(mod4(q + 1)), at_q(mod4(q - 1))
    before, after, across = mod4(q - 1), mod4(q + 1), mod4(q + 2)

    def part_of(g, half, q_):
        return H.at[span(base(g) + half * 64, 64), cols(q_)]

    def pass_on(g, n, half, q_, to):
        send_group(g, lambda g: remote(part_of(g, half, q_), part_of(g, half, q_), p2s.at[g, n], p2r.at[g, n], to))

    def passed(n, half, q_):
        each_group(lambda g: arrived(part_of(g, half, q_), p2s.at[g, n], p2r.at[g, n]))

    def second_step(g):
        first_end(g)
        pass_on(g, 0, 0, q, right)
        pass_on(g, 1, 1, q, left)
        pass_on(g, 2, 1, q, right)
        pass_on(g, 3, 0, q, left)

    def relay_step(g):
        arrived(part_of(g, 0, before), p2s.at[g, 0], p2r.at[g, 0])
        pass_on(g, 4, 0, before, right)
        arrived(part_of(g, 1, after), p2s.at[g, 1], p2r.at[g, 1])
        pass_on(g, 5, 1, after, left)

    each_group(second_step)
    send(TS.at[mod4(a + 1)], TR.at[3], ts.at[0], tr.at[0], at_a(mod4(a + 1)))
    send(TS.at[mod4(a + 3)], TR.at[1], ts.at[1], tr.at[1], at_a(mod4(a + 3)))

    my_half = pl.ds(pl.multiple_of(c * HALF, HALF), HALF)

    def logits(slab, q_, first=False):
        rr = slice(slab * VP, (slab + 1) * VP)
        out = lax.dot_general(HD[rr, cols(q_)], H[my_half, cols(q_)], nt, preferred_element_type=F32)
        CP[rr] = out if first else CP[rr] + out

    load_hid.wait()
    logits(0, q, True)
    turn(0, 1)
    each_group(relay_step)

    arrived(RLY, ts.at[2], tr.at[2])
    send(RLY, TR.at[2], ts.at[3], tr.at[3], at_a(mod4(a + way)))
    passed(2, 1, before)
    logits(0, before)
    passed(3, 0, after)
    logits(0, after)
    arrived(HD.at[VP : VP + 736], hs.at[0], hr.at[0])
    arrived(HD.at[VP + 736 : VP + 768], hs.at[1], hr.at[1])
    logits(1, q, True)
    logits(1, before)
    logits(1, after)
    passed(4, 0, across)
    passed(5, 1, across)
    in_slab = lax.broadcasted_iota(jnp.int32, (256, HALF), 0) < SLAB - 512

    def exponentials(slab, student_sum):
        for k in range(3):
            rr = slice(slab * VP + k * 256, slab * VP + (k + 1) * 256)
            capped = CAP * jnp.tanh(CP[rr] * (1.0 / CAP))
            exps = jnp.exp(capped)
            if k == 2:
                exps = jnp.where(in_slab, exps, 0.0)
            CP[rr] = capped
            ES[rr] = exps
            student_sum = student_sum + jnp.sum(exps, axis=0, keepdims=True)
        return student_sum

    logits(0, across)
    logits(1, across)
    student_sum = exponentials(0, jnp.zeros((1, HALF), F32))
    student_sum = exponentials(1, student_sum)
    my_rows = (mod4(a + 2 * c), mod4(a + 2 * c + 1))
    for i in range(2):
        TT[pl.ds(my_rows[i], 1)] = student_sum[:, i * 128 : (i + 1) * 128]

    def exchange_start(tile, slots, ssem, rsem, me, at):
        for k in range(1, 16):
            send(tile, slots.at[me], ssem.at[k - 1], rsem.at[k - 1], at(lax.rem(me + k, 16)))

    def exchange_end(tile, slots, ssem, rsem, me):
        slots[me] = tile[...]
        for k in range(1, 16):
            arrived(slots.at[lax.rem(me + 16 - k, 16)], ssem.at[k - 1], rsem.at[k - 1])
        total = slots[0]
        for k in range(1, 16):
            total = total + slots[k]
        return total

    exchange_start(TT, TG1, as1, ar1, me_xy, at_xy)

    def factors(slab, cross_sum):
        for k in range(6):
            rr = slice(slab * VP + k * 128, slab * VP + (k + 1) * 128)
            vv = slice(k * 128, (k + 1) * 128)
            if slab == 0:
                target = jnp.concatenate([TR[2 * c, vv], TR[2 * c + 1, vv]], axis=1).astype(F32)
            else:
                target = jnp.concatenate([TSIB[0, vv], TSIB[1, vv]], axis=1).astype(F32)
            expd = jnp.exp(target)
            capped = CP[rr]
            cross_sum = cross_sum + jnp.sum(expd * (target - capped), axis=0, keepdims=True)
            ratio = capped * (1.0 / CAP)
            slope = 1.0 - ratio * ratio
            ES[rr] = ES[rr] * slope
            CP[rr] = expd * slope
        return cross_sum

    turn(1, 0)

    def give(i):
        send(TR.at[2 * (1 - c) + i], TSIB.at[i], ts.at[4 + i], tr.at[4 + i], sib)

    arrived(TR.at[3], ts.at[0], tr.at[0])
    arrived(TR.at[1], ts.at[1], tr.at[1])
    give(1)
    TT2[...] = exchange_end(TT, TG1, as1, ar1, me_xy)
    exchange_start(TT2, TG2, as2, ar2, me_zc, at_zc)
    arrived(TR.at[2], ts.at[3], tr.at[3])
    give(0)
    cross_sum = factors(0, jnp.zeros((1, HALF), F32))
    turn(1, 1)
    for i in range(2):
        arrived(TSIB.at[i], ts.at[4 + i], tr.at[4 + i])
    cross_sum = factors(1, cross_sum)
    TOT[...] = exchange_end(TT2, TG2, as2, ar2, me_zc)

    valid = TOT[8:12] * (1.0 / 64.0)
    weight = valid * (512.0 / jnp.sum(valid))
    AL[0:4] = weight / TOT[0:4]
    BE[0:4] = weight / TOT[4:8]
    alpha = jnp.concatenate([AL[pl.ds(r, 1)] for r in my_rows], axis=1)
    beta = jnp.concatenate([BE[pl.ds(r, 1)] for r in my_rows], axis=1)
    for k in range(12):
        rr = slice(k * 128, (k + 1) * 128)
        grad = (ES[rr] * alpha - CP[rr] * beta).astype(BF16)
        GV[rr] = grad
        if k < 6:
            GTD[rr, my_half] = grad

    up, down, far = mod4(p + 1), mod4(p - 1), mod4(p + 2)

    def partial(n, p_):
        rows = []
        for i in range(4):
            rows.append(HDT[n, jnp.where(c == 0, i, p_), jnp.where(c == 0, p_, i)])
        return jnp.dot(jnp.concatenate(rows, axis=0), GV[...], preferred_element_type=F32)

    def put(ref, n, block):
        for i in range(4):
            ref[n, i] = block[i * CHIPCOL : (i + 1) * CHIPCOL].astype(ref.dtype)

    put(B1, 0, partial(0, far))
    send(B1.at[0], R1.at[0], q1s.at[0], q1r.at[0], at_p(up))
    put(B1, 1, partial(1, far))
    send(B1.at[1], R1.at[1], q1s.at[1], q1r.at[1], at_p(down))
    put(B1, 3, partial(0, down))
    send(B1.at[3], R1.at[3], q1s.at[3], q1r.at[3], at_p(down))
    put(B1, 2, partial(1, up))
    send(B1.at[2], R1.at[2], q1s.at[2], q1r.at[2], at_p(up))
    send(GV.at[VP : 2 * VP], GTD.at[:, my_half], gs.at[0], gr.at[0], sib)

    def share(g):
        return H.at[span(base(g), ROWS)]

    each_group(lambda g: send_group(g, lambda g: remote(share(g), share(g), cs.at[g], cr.at[g], sib)))


    def head_chunk(n):
        at = pl.ds(pl.multiple_of(n * 512, 512), 512)
        out = jnp.dot(GTD[...], H[:, at], preferred_element_type=F32)
        DH[:, at] = out[:SLAB].astype(BF16)

    def head_chunks(first, last):
        @pl.loop(first, last)
        def _(n):
            head_chunk(n)

    qup, qdown, qfar = mod4(q + 1), mod4(q - 1), mod4(q + 2)
    order = (qfar, qup, qdown, q)

    def relay(k):
        arrived(R1.at[k], q1s.at[k], q1r.at[k])
        near = up if k == 0 else down
        for n, i in enumerate(order):
            F1[k, i] = (NEXT[k, i] + R1[k, i].astype(F32)).astype(BF16)
            send(F1.at[k, i], R1.at[4 + k, i], f1s.at[k, n], f1r.at[k, n], at_p(near))

    def second(k, n):
        i = order[n]
        arrived(R1.at[4 + k, i], f1s.at[k, n], f1r.at[k, n])
        total = OWN[k, i] + R1[3 - k, i].astype(F32) + R1[4 + k, i].astype(F32)
        if n == 3:
            OWN[k, i] = total
        else:
            B2[k, i] = total.astype(BF16)
            send(B2.at[k, i], R2.at[k, n], q2s.at[k * 3 + n], q2r.at[k * 3 + n], at_q(i))

    put(NEXT, 0, partial(0, up))
    relay(0)
    put(NEXT, 1, partial(1, down))
    relay(1)

    CR[...] = jnp.zeros_like(CR)
    for i in range(2):
        CR[pl.ds(my_rows[i], 1)] = cross_sum[:, i * 128 : (i + 1) * 128]
    exchange_start(CR, CG1, bs1, br1, me_xy, at_xy)

    put(OWN, 0, partial(0, p))
    put(OWN, 1, partial(1, p))
    arrived(GTD.at[:, pl.ds(pl.multiple_of((1 - c) * HALF, HALF), HALF)], gs.at[0], gr.at[0])
    arrived(H.at[span(ROWS + (1 - c) * ROWS, ROWS)], cs.at[0], cr.at[0])

    @pl.when(c == 0)
    def _():
        arrived(H.at[3 * ROWS : 4 * ROWS], cs.at[1], cr.at[1])

    head_chunks(0, 1)
    arrived(R1.at[3], q1s.at[3], q1r.at[3])
    arrived(R1.at[2], q1s.at[2], q1r.at[2])
    for n in range(4):
        for k in range(2):
            second(k, n)
    CR2[...] = exchange_end(CR, CG1, bs1, br1, me_xy)
    exchange_start(CR2, CG2, bs2, br2, me_zc, at_zc)
    head_chunks(1, 3)

    at_home = (c == 0) & (zl == 0)
    at_home_hi = (c == 0) & (zl == 1)

    def to_owner(k, i, c_):
        n = k * 4 + i * 2 + c_
        return pltpu.make_async_remote_copy(
            src_ref=B3.at[k, i, c_], dst_ref=RZ.at[z], send_sem=rzs.at[n], recv_sem=rzr.at[z],
            device_id=dev(mod4(a + 2 * c + i), k, y, x, c_), device_id_type=MESH,
        )

    owners = [(k, i, c_) for k in range(2) for i in range(2) for c_ in range(2)]
    for k in range(2):
        total = OWN[k, q]
        for n in range(3):
            arrived(R2.at[k, n], q2s.at[k * 3 + n], q2r.at[k * 3 + n])
            total = total + R2[k, n].astype(F32)
        for i in range(2):
            for c_ in range(2):
                B3[k, i, c_] = total[48 * c_ : 48 * c_ + 64, i * 128 : (i + 1) * 128].astype(BF16)
                if i == 0 and c_ == 0:
                    home = at_home if k == 0 else at_home_hi

                    @pl.when(jnp.logical_not(home))
                    def _():
                        to_owner(k, i, c_).start()

                    @pl.when(home)
                    def _():
                        RZ[z] = B3[k, 0, 0]
                else:
                    to_owner(k, i, c_).start()

    head_chunks(3, 7)
    cross = exchange_end(CR2, CG2, bs2, br2, me_zc)
    KL[0:4] = cross[0:4] / TOT[4:8] - jnp.log(TOT[4:8]) + jnp.log(TOT[0:4])
    kl_out[...] = KL[pl.ds(a, 1)]

    for copy in pending:
        copy.wait_send()

    @pl.when(c == 1)
    def _():
        for make in later:
            make().wait_send()

    for k, i, c_ in owners:
        if i == 0 and c_ == 0:
            home = at_home if k == 0 else at_home_hi

            @pl.when(jnp.logical_not(home))
            def _():
                to_owner(k, i, c_).wait_send()
        else:
            to_owner(k, i, c_).wait_send()

    @pl.when(c == 1)
    def _():
        arrived(RZ.at[z], rzs.at[0], rzr.at[z])

    for k in range(1, 8):
        source = lax.rem(z + k, 8)
        arrived(RZ.at[source], rzs.at[0], rzr.at[source])
    total = RZ[0].astype(F32)
    for k in range(1, 8):
        total = total + RZ[k].astype(F32)
    dhid_out[...] = jnp.where(c == 0, total[0:56], total[8:64]).astype(BF16)


def results(kl, dhid, dhead, kl_out, dhid_out, dhead_out, sem):
    copies = [
        pltpu.make_async_copy(dhid, dhid_out, sem.at[7]),
        pltpu.make_async_copy(kl, kl_out, sem.at[8]),
    ]
    for n in range(7):
        at = pl.ds(n * 512, 512)
        copies.append(pltpu.make_async_copy(dhead.at[:, at], dhead_out.at[:, at], sem.at[n]))
    for copy in copies:
        copy.start()
    for copy in copies:
        copy.wait()


def on_device(hidden, valid_mask, student_head, teacher_logits):
    vm = pltpu.VMEM
    dma = pltpu.SemaphoreType.DMA
    any_spec = pl.BlockSpec(memory_space=pl.ANY)
    vmem_spec = pl.BlockSpec(memory_space=pltpu.VMEM)
    kl, dhid, dhead = pl.pallas_call(
        kernel,
        out_shape=(vm((1, ROWS), F32), vm((56, ROWS), BF16), vm((SLAB, D), BF16)),
        in_specs=[any_spec, vmem_spec, any_spec, any_spec],
        out_specs=(vmem_spec, vmem_spec, vmem_spec),
        scratch_shapes=[
            vm((512, D), BF16),
            vm((2 * VP, D), BF16),
            vm((2, 4, 4, CHIPCOL, 2 * VP), BF16),
            vm((256, 256), BF16),
            vm((3000, ROWS), BF16),
            vm((4, VP, ROWS), BF16),
            vm((4, VP, ROWS), BF16),
            vm((VP, ROWS), BF16),
            vm((2, VP, ROWS), BF16),
            vm((2 * VP, HALF), F32),
            vm((2 * VP, HALF), F32),
            vm((2 * VP, HALF), BF16),
            vm((VP, 512), BF16),
            vm((16, 128), F32),
            vm((16, 16, 128), F32),
            vm((16, 128), F32),
            vm((16, 16, 128), F32),
            vm((16, 128), F32),
            vm((8, 128), F32),
            vm((8, 128), F32),
            vm((8, 128), F32),
            vm((16, 8, 128), F32),
            vm((8, 128), F32),
            vm((16, 8, 128), F32),
            vm((8, 128), F32),
            vm((2, 4, CHIPCOL, HALF), F32),
            vm((2, 4, CHIPCOL, HALF), F32),
            vm((4, 4, CHIPCOL, HALF), BF16),
            vm((6, 4, CHIPCOL, HALF), BF16),
            vm((2, 4, CHIPCOL, HALF), BF16),
            vm((2, 4, CHIPCOL, HALF), BF16),
            vm((2, 3, CHIPCOL, HALF), BF16),
            vm((2, 2, 2, 64, 128), BF16),
            vm((8, 64, 128), BF16),
            dma((4,)),
            dma((2,)), dma((2,)),
            dma((2,)), dma((2,)),
            dma((2, 3)), dma((2, 3)), dma((2, 6)), dma((2, 6)),
            dma((2,)), dma((2,)),
            dma((6,)), dma((6,)),
            dma((1,)), dma((1,)),
            dma((15,)), dma((15,)), dma((15,)), dma((15,)),
            dma((15,)), dma((15,)), dma((15,)), dma((15,)),
            dma((4,)), dma((4,)), dma((2, 4)), dma((2, 4)), dma((6,)), dma((6,)),
            dma((8,)), dma((8,)),
        ],
        compiler_params=pltpu.CompilerParams(
            collective_id=0, has_side_effects=True, vmem_limit_bytes=50 * 1024 * 1024
        ),
        cost_estimate=pl.CostEstimate(flops=3 * 2 * 512 * 750 * 3584, bytes_accessed=13_000_000, transcendentals=0),
    )(hidden, valid_mask.reshape(1, ROWS), student_head, teacher_logits.T)
    kl, dhid, dhead = pl.pallas_call(
        results,
        out_shape=(
            jax.ShapeDtypeStruct((1, ROWS), F32),
            jax.ShapeDtypeStruct((56, ROWS), BF16),
            jax.ShapeDtypeStruct((SLAB, D), BF16),
        ),
        in_specs=[any_spec] * 3,
        out_specs=(any_spec,) * 3,
        scratch_shapes=[dma((9,))],
        compiler_params=pltpu.CompilerParams(vmem_limit_bytes=1024 * 1024),
    )(kl, dhid, dhead)
    return kl.reshape(ROWS), dhid.T, dhead


def solution(mesh):
    return jax.shard_map(
        on_device,
        mesh=mesh,
        in_specs=(P("tok", None), P("tok"), P(("voc", "tok"), None), P("tok", "voc")),
        out_specs=(P("tok"), P("tok", "voc"), P(("voc", "tok"), None)),
        check_vma=False,
    )
```

```python
import jax
import jax.numpy as jnp
from jax import lax
from jax.experimental import pallas as pl
from jax.experimental.pallas import tpu as pltpu
from jax.sharding import PartitionSpec as P

CAP = 30.0
D = 3584
ROWS = 128
HALF = 256
SLAB = 750
VP = 768
QCOL = D // 4
PIECE = ROWS // 4
CHIPCOL = 112
MESH = pl.DeviceIdType.MESH
F32 = jnp.float32
BF16 = jnp.bfloat16


def kernel(
    hid, mask, head, teach, kl_out, dhid_out, DH,
    H, HD, HDT, EYE, tin, TS, TR, RLY, TSIB, CP, ES, GV, GTD,
    TT, TG1, TT2, TG2, TOT, AL, BE, CR, CG1, CR2, CG2, KL,
    OWN, NEXT, B1, R1, F1, B2, R2, B3, RZ,
    local, hs, hr, zs, zr, p1s, p1r, p2s, p2r, cs, cr, ts, tr, gs, gr,
    as1, ar1, as2, ar2, bs1, br1, bs2, br2, q1s, q1r, f1s, f1r, q2s, q2r, rzs, rzr,
):
    a = lax.axis_index("tok")
    v = lax.axis_index("voc")
    c = lax.rem(v, 2)
    x = lax.rem(v // 2, 4)
    y = lax.rem(v // 8, 4)
    zl = v // 32
    z = 2 * a + zl
    p = jnp.where(c == 0, x, y)
    q = jnp.where(c == 0, y, x)

    def dev(a_, zl_, y_, x_, c_):
        return (a_, zl_ * 32 + y_ * 8 + x_ * 2 + c_)

    def at_p(p_):
        return dev(a, zl, jnp.where(c == 0, y, p_), jnp.where(c == 0, p_, x), c)

    def at_q(q_):
        return dev(a, zl, jnp.where(c == 0, q_, y), jnp.where(c == 0, x, q_), c)

    sib = dev(a, zl, y, x, 1 - c)

    def at_a(a_):
        return dev(a_, zl, y, x, c)

    def at_xy(k):
        return dev(a, zl, k // 4, lax.rem(k, 4), c)

    def at_zc(k):
        return dev(k // 4, lax.rem(k // 2, 2), y, x, lax.rem(k, 2))

    def mod4(k):
        return lax.rem(k + 8, 4)

    me_xy = y * 4 + x
    me_zc = z * 2 + c

    pending = []

    def send(src, dst, ssem, rsem, to):
        copy = pltpu.make_async_remote_copy(
            src_ref=src, dst_ref=dst, send_sem=ssem, recv_sem=rsem, device_id=to, device_id_type=MESH
        )
        copy.start()
        pending.append(copy)

    def arrived(dst, ssem, rsem):
        pltpu.make_async_remote_copy(
            src_ref=dst, dst_ref=dst, send_sem=ssem, recv_sem=rsem, device_id=sib, device_id_type=MESH
        ).wait_recv()

    barrier = pltpu.get_barrier_semaphore()
    for k in range(1, 16):
        pl.semaphore_signal(barrier, inc=1, device_id=at_zc(lax.rem(me_zc + k, 16)), device_id_type=MESH)
    for k in range(1, 16):
        pl.semaphore_signal(barrier, inc=1, device_id=at_xy(lax.rem(me_xy + k, 16)), device_id_type=MESH)

    load_teach = pltpu.make_async_copy(teach, tin, local.at[0])
    load_teach.start()
    load_hid = pltpu.make_async_copy(hid, H.at[pl.ds(0, ROWS)], local.at[1])
    load_hid.start()

    pl.semaphore_wait(barrier, 30)

    def span(start, size):
        return pl.ds(pl.multiple_of(start, 16), size)

    def cols(q_):
        return pl.ds(pl.multiple_of(q_ * QCOL, 128), QCOL)

    def base(g):
        return ROWS + c * ROWS + g * ROWS

    later = []

    def each_group(step):
        step(0)

        @pl.when(c == 1)
        def _():
            step(1)

    def send_group(g, make):
        copy = make(g)
        copy.start()
        if g == 0:
            pending.append(copy)
        else:
            later.append(lambda: make(1))

    def remote(src, dst, ssem, rsem, to):
        return pltpu.make_async_remote_copy(
            src_ref=src, dst_ref=dst, send_sem=ssem, recv_sem=rsem, device_id=to, device_id_type=MESH
        )

    each_group(lambda g: send_group(g, lambda g: remote(
        hid.at[span(p * PIECE, PIECE), cols(q)], H.at[span(base(g) + p * PIECE, PIECE), cols(q)],
        zs.at[g], zr.at[g],
        dev(mod4(a - 1 - c - g), jnp.where((c == 1) & (g == 0), 1 - zl, zl), y, x, c),
    )))

    load_head = pltpu.make_async_copy(head.at[pl.ds(0, 736)], HD.at[0:736], local.at[2])
    load_head.start()
    send(head.at[pl.ds(0, 736)], HD.at[VP : VP + 736], hs.at[0], hr.at[0], sib)
    load_tail = pltpu.make_async_copy(head, DH, local.at[3])
    load_tail.start()

    load_teach.wait()
    for t in range(4):
        start = t * SLAB // 16 * 16
        if t < 3:
            TS[t] = tin[start : start + VP]
        else:
            TS[t, 0 : VP - 16] = tin[start : start + VP - 16]
            rest = tin[start + VP - 16 : 3000].astype(F32)
            TS[t, VP - 16 : VP] = jnp.concatenate([rest, jnp.zeros((8, ROWS), F32)], axis=0).astype(BF16)
    way = jnp.where(c == 0, 1, 3)
    send(TS.at[mod4(a + 2)], RLY, ts.at[2], tr.at[2], at_a(mod4(a + way)))
    TR[0] = TS[a]
    teacher_sum = jnp.zeros((1, ROWS), F32)
    for start in range(0, 3000, 752):
        part = tin[start : min(start + 752, 3000)].astype(F32)
        teacher_sum = teacher_sum + jnp.sum(jnp.exp(part), axis=0, keepdims=True)

    TT[...] = jnp.zeros_like(TT)
    TT[pl.ds(4 + a, 1)] = teacher_sum
    TT[pl.ds(8 + a, 1)] = mask[...].astype(F32)

    nt = (((1,), (1,)), ((), ()))
    EYE[...] = jnp.where(
        lax.broadcasted_iota(jnp.int32, (256, 256), 0) == lax.broadcasted_iota(jnp.int32, (256, 256), 1), 1.0, 0.0
    ).astype(BF16)

    def turn(slab, half):
        for n in range(7):
            at = pl.ds(half * 1792 + n * 256, 256)
            out = lax.dot_general(
                EYE[...], HD[slab * VP : (slab + 1) * VP, at], nt, preferred_element_type=F32
            ).astype(BF16)
            done = 0
            while done < 256:
                chip, row = divmod(n * 256 + done, CHIPCOL)
                size = min(CHIPCOL - row, 256 - done)
                HDT[half, chip // 4, chip % 4, row : row + size, slab * VP : (slab + 1) * VP] = out[done : done + size]
                done += size

    def piece(g, p_):
        return H.at[span(base(g) + p_ * PIECE, PIECE), cols(q)]

    def first_step(g):
        arrived(piece(g, p), zs.at[g], zr.at[g])
        for d in range(1, 4):
            send_group(g, lambda g, d=d: remote(
                piece(g, p), piece(g, p), p1s.at[g, d - 1], p1r.at[g, d - 1], at_p(mod4(p + d)),
            ))

    each_group(first_step)

    load_tail.wait()
    HD[736:768] = jnp.concatenate([DH[736:750].astype(F32), jnp.zeros((18, D), F32)], axis=0).astype(BF16)
    send(HD.at[736:768], HD.at[VP + 736 : VP + 768], hs.at[1], hr.at[1], sib)
    load_head.wait()
    turn(0, 0)

    def first_end(g):
        for d in range(1, 4):
            arrived(piece(g, mod4(p - d)), p1s.at[g, d - 1], p1r.at[g, d - 1])

    right, left = at_q(mod4(q + 1)), at_q(mod4(q - 1))
    before, after, across = mod4(q - 1), mod4(q + 1), mod4(q + 2)

    def part_of(g, half, q_):
        return H.at[span(base(g) + half * 64, 64), cols(q_)]

    def pass_on(g, n, half, q_, to):
        send_group(g, lambda g: remote(part_of(g, half, q_), part_of(g, half, q_), p2s.at[g, n], p2r.at[g, n], to))

    def passed(n, half, q_):
        each_group(lambda g: arrived(part_of(g, half, q_), p2s.at[g, n], p2r.at[g, n]))

    def second_step(g):
        first_end(g)
        pass_on(g, 0, 0, q, right)
        pass_on(g, 1, 1, q, left)
        pass_on(g, 2, 1, q, right)
        pass_on(g, 3, 0, q, left)

    def relay_step(g):
        arrived(part_of(g, 0, before), p2s.at[g, 0], p2r.at[g, 0])
        pass_on(g, 4, 0, before, right)
        arrived(part_of(g, 1, after), p2s.at[g, 1], p2r.at[g, 1])
        pass_on(g, 5, 1, after, left)

    each_group(second_step)
    send(TS.at[mod4(a + 1)], TR.at[3], ts.at[0], tr.at[0], at_a(mod4(a + 1)))
    send(TS.at[mod4(a + 3)], TR.at[1], ts.at[1], tr.at[1], at_a(mod4(a + 3)))

    my_half = pl.ds(pl.multiple_of(c * HALF, HALF), HALF)

    def logits(slab, q_, first=False):
        rr = slice(slab * VP, (slab + 1) * VP)
        out = lax.dot_general(HD[rr, cols(q_)], H[my_half, cols(q_)], nt, preferred_element_type=F32)
        CP[rr] = out if first else CP[rr] + out

    load_hid.wait()
    logits(0, q, True)
    turn(0, 1)
    each_group(relay_step)

    arrived(RLY, ts.at[2], tr.at[2])
    send(RLY, TR.at[2], ts.at[3], tr.at[3], at_a(mod4(a + way)))
    passed(2, 1, before)
    logits(0, before)
    passed(3, 0, after)
    logits(0, after)
    arrived(HD.at[VP : VP + 736], hs.at[0], hr.at[0])
    arrived(HD.at[VP + 736 : VP + 768], hs.at[1], hr.at[1])
    logits(1, q, True)
    logits(1, before)
    logits(1, after)
    passed(4, 0, across)
    passed(5, 1, across)
    in_slab = lax.broadcasted_iota(jnp.int32, (256, HALF), 0) < SLAB - 512

    def exponentials(slab, student_sum):
        for k in range(3):
            rr = slice(slab * VP + k * 256, slab * VP + (k + 1) * 256)
            capped = CAP * jnp.tanh(CP[rr] * (1.0 / CAP))
            exps = jnp.exp(capped)
            if k == 2:
                exps = jnp.where(in_slab, exps, 0.0)
            CP[rr] = capped
            ES[rr] = exps
            student_sum = student_sum + jnp.sum(exps, axis=0, keepdims=True)
        return student_sum

    logits(0, across)
    logits(1, across)
    student_sum = exponentials(0, jnp.zeros((1, HALF), F32))
    student_sum = exponentials(1, student_sum)
    my_rows = (mod4(a + 2 * c), mod4(a + 2 * c + 1))
    for i in range(2):
        TT[pl.ds(my_rows[i], 1)] = student_sum[:, i * 128 : (i + 1) * 128]

    def exchange_start(tile, slots, ssem, rsem, me, at):
        for k in range(1, 16):
            send(tile, slots.at[me], ssem.at[k - 1], rsem.at[k - 1], at(lax.rem(me + k, 16)))

    def exchange_end(tile, slots, ssem, rsem, me):
        slots[me] = tile[...]
        for k in range(1, 16):
            arrived(slots.at[lax.rem(me + 16 - k, 16)], ssem.at[k - 1], rsem.at[k - 1])
        total = slots[0]
        for k in range(1, 16):
            total = total + slots[k]
        return total

    exchange_start(TT, TG1, as1, ar1, me_xy, at_xy)

    blocks = (3 * c, 1 + c)
    toks = (mod4(a + 3 * c), mod4(a + 1 + c))
    lanes = tuple(pl.ds(pl.multiple_of(n * 128, 128), 128) for n in (c, 1 - c))
    shift = jnp.where(a == 0, 0, VP - 16 + 2 * a)
    place = lax.broadcasted_iota(jnp.int32, (VP, ROWS), 0)

    def give(k):
        send(TR.at[(3 * (1 - c), 2 - c)[k]], TSIB.at[k], ts.at[4 + k], tr.at[4 + k], sib)

    def align(tile):
        tall = pltpu.roll(tile.astype(F32), shift, 0)
        return jnp.where(place < SLAB, tall, -30000.0)

    def factors(k, slab):
        target = align(TR[blocks[k]] if slab == 0 else TSIB[k])
        rr = slice(slab * VP, (slab + 1) * VP)
        expd = jnp.exp(target)
        capped = CP[rr, lanes[k]]
        ratio = capped * (1.0 / CAP)
        slope = 1.0 - ratio * ratio
        ES[rr, lanes[k]] = ES[rr, lanes[k]] * slope
        CP[rr, lanes[k]] = expd * slope
        return jnp.sum(expd * (target - capped), axis=0, keepdims=True)

    turn(1, 0)
    arrived(TR.at[3], ts.at[0], tr.at[0])
    give(0)
    cross_first = factors(0, 0)
    TT2[...] = exchange_end(TT, TG1, as1, ar1, me_xy)
    exchange_start(TT2, TG2, as2, ar2, me_zc, at_zc)
    arrived(TSIB.at[0], ts.at[4], tr.at[4])
    cross_first = cross_first + factors(0, 1)
    turn(1, 1)
    TOT[...] = exchange_end(TT2, TG2, as2, ar2, me_zc)

    valid = TOT[8:12] * (1.0 / 64.0)
    weight = valid * (512.0 / jnp.sum(valid))
    AL[0:4] = weight / TOT[0:4]
    BE[0:4] = weight / TOT[4:8]

    def gradient(k):
        alpha, beta = AL[pl.ds(toks[k], 1)], BE[pl.ds(toks[k], 1)]
        at = pl.ds(pl.multiple_of(c * HALF + (c, 1 - c)[k] * 128, 128), 128)
        for n in range(6):
            rr = slice(n * 256, (n + 1) * 256)
            grad = (ES[rr, lanes[k]] * alpha - CP[rr, lanes[k]] * beta).astype(BF16)
            GV[rr, lanes[k]] = grad
            if n < 3:
                GTD[rr, at] = grad

    def partial(k, p_):
        rows = []
        for i in range(4):
            for zl_ in range(2):
                rows.append(HDT[zl_, jnp.where(c == 0, i, p_), jnp.where(c == 0, p_, i)])
        return jnp.dot(jnp.concatenate(rows, axis=0), GV[:, lanes[k]], preferred_element_type=F32)

    def put(ref, n, block):
        for i in range(4):
            for zl_ in range(2):
                first = (i * 2 + zl_) * CHIPCOL
                ref[n, i, zl_] = block[first : first + CHIPCOL].astype(ref.dtype)

    up, down, far = mod4(p + 1), mod4(p - 1), mod4(p + 2)
    gradient(0)
    put(B1, 0, partial(0, far))
    send(B1.at[0], R1.at[0], q1s.at[0], q1r.at[0], at_p(up))
    put(B1, 3, partial(0, down))
    send(B1.at[3], R1.at[3], q1s.at[3], q1r.at[3], at_p(down))
    arrived(TR.at[1], ts.at[1], tr.at[1])
    arrived(TR.at[2], ts.at[3], tr.at[3])
    give(1)
    put(NEXT, 0, partial(0, up))
    cross_second = factors(1, 0)
    arrived(TSIB.at[1], ts.at[5], tr.at[5])
    cross_second = cross_second + factors(1, 1)
    gradient(1)
    put(B1, 1, partial(1, far))
    send(B1.at[1], R1.at[1], q1s.at[1], q1r.at[1], at_p(down))
    put(B1, 2, partial(1, up))
    send(B1.at[2], R1.at[2], q1s.at[2], q1r.at[2], at_p(up))

    def head_chunk(n):
        at = pl.ds(pl.multiple_of(n * 512, 512), 512)
        out = jnp.dot(GTD[...], H[:, at], preferred_element_type=F32)
        DH[:, at] = out[:SLAB].astype(BF16)

    def head_chunks(first, last):
        @pl.loop(first, last)
        def _(n):
            head_chunk(n)

    qup, qdown, qfar = mod4(q + 1), mod4(q - 1), mod4(q + 2)
    order = (qfar, qup, qdown, q)

    def relay(k):
        arrived(R1.at[k], q1s.at[k], q1r.at[k])
        near = up if k == 0 else down
        for n, i in enumerate(order):
            F1[k, i] = (NEXT[k, i] + R1[k, i].astype(F32)).astype(BF16)
            send(F1.at[k, i], R1.at[4 + k, i], f1s.at[k, n], f1r.at[k, n], at_p(near))

    def second(k, n):
        i = order[n]
        arrived(R1.at[4 + k, i], f1s.at[k, n], f1r.at[k, n])
        total = OWN[k, i] + R1[3 - k, i].astype(F32) + R1[4 + k, i].astype(F32)
        if n == 3:
            OWN[k, i] = total
        else:
            B2[k, i] = total.astype(BF16)
            send(B2.at[k, i], R2.at[k, n], q2s.at[k * 3 + n], q2r.at[k * 3 + n], at_q(i))

    relay(0)
    put(NEXT, 1, partial(1, down))
    relay(1)
    send(GV.at[VP : 2 * VP], GTD.at[:, my_half], gs.at[0], gr.at[0], sib)

    def share(g):
        return H.at[span(base(g), ROWS)]

    each_group(lambda g: send_group(g, lambda g: remote(share(g), share(g), cs.at[g], cr.at[g], sib)))

    CR[...] = jnp.zeros_like(CR)
    CR[pl.ds(toks[0], 1)] = cross_first
    CR[pl.ds(toks[1], 1)] = cross_second
    exchange_start(CR, CG1, bs1, br1, me_xy, at_xy)

    put(OWN, 0, partial(0, p))
    put(OWN, 1, partial(1, p))
    arrived(R1.at[3], q1s.at[3], q1r.at[3])
    arrived(R1.at[2], q1s.at[2], q1r.at[2])
    for n in range(4):
        for k in range(2):
            second(k, n)
    CR2[...] = exchange_end(CR, CG1, bs1, br1, me_xy)
    exchange_start(CR2, CG2, bs2, br2, me_zc, at_zc)
    arrived(GTD.at[:, pl.ds(pl.multiple_of((1 - c) * HALF, HALF), HALF)], gs.at[0], gr.at[0])
    arrived(H.at[span(ROWS + (1 - c) * ROWS, ROWS)], cs.at[0], cr.at[0])

    @pl.when(c == 0)
    def _():
        arrived(H.at[3 * ROWS : 4 * ROWS], cs.at[1], cr.at[1])

    head_chunks(0, 3)

    def to_owner(k, zl_, c_):
        n = k * 4 + zl_ * 2 + c_
        return pltpu.make_async_remote_copy(
            src_ref=B3.at[k, zl_, c_], dst_ref=RZ.at[z], send_sem=rzs.at[n], recv_sem=rzr.at[z],
            device_id=dev(toks[k], zl_, y, x, c_), device_id_type=MESH,
        )

    owners = [(k, zl_, c_) for k in range(2) for zl_ in range(2) for c_ in range(2)]
    for k in range(2):
        total = OWN[k, q]
        for n in range(3):
            arrived(R2.at[k, n], q2s.at[k * 3 + n], q2r.at[k * 3 + n])
            total = total + R2[k, n].astype(F32)
        for zl_ in range(2):
            for c_ in range(2):
                B3[k, zl_, c_] = total[zl_, 48 * c_ : 48 * c_ + 64].astype(BF16)
                if k == 0 and c_ == 0:
                    home = (c == 0) & (zl == zl_)

                    @pl.when(jnp.logical_not(home))
                    def _():
                        to_owner(k, zl_, c_).start()

                    @pl.when(home)
                    def _():
                        RZ[z] = B3[k, zl_, c_]
                else:
                    to_owner(k, zl_, c_).start()

    head_chunks(3, 7)
    cross = exchange_end(CR2, CG2, bs2, br2, me_zc)
    KL[0:4] = cross[0:4] / TOT[4:8] - jnp.log(TOT[4:8]) + jnp.log(TOT[0:4])
    kl_out[...] = KL[pl.ds(a, 1)]

    for copy in pending:
        copy.wait_send()

    @pl.when(c == 1)
    def _():
        for make in later:
            make().wait_send()

    for k, zl_, c_ in owners:
        if k == 0 and c_ == 0:

            @pl.when(jnp.logical_not((c == 0) & (zl == zl_)))
            def _():
                to_owner(k, zl_, c_).wait_send()
        else:
            to_owner(k, zl_, c_).wait_send()

    @pl.when(c == 1)
    def _():
        arrived(RZ.at[z], rzs.at[0], rzr.at[z])

    for k in range(1, 8):
        source = lax.rem(z + k, 8)
        arrived(RZ.at[source], rzs.at[0], rzr.at[source])
    total = RZ[0].astype(F32)
    for k in range(1, 8):
        total = total + RZ[k].astype(F32)
    dhid_out[...] = jnp.where(c == 0, total[0:56], total[8:64]).astype(BF16)


def results(kl, dhid, dhead, kl_out, dhid_out, dhead_out, sem):
    copies = [
        pltpu.make_async_copy(dhid, dhid_out, sem.at[7]),
        pltpu.make_async_copy(kl, kl_out, sem.at[8]),
    ]
    for n in range(7):
        at = pl.ds(n * 512, 512)
        copies.append(pltpu.make_async_copy(dhead.at[:, at], dhead_out.at[:, at], sem.at[n]))
    for copy in copies:
        copy.start()
    for copy in copies:
        copy.wait()


def on_device(hidden, valid_mask, student_head, teacher_logits):
    vm = pltpu.VMEM
    dma = pltpu.SemaphoreType.DMA
    any_spec = pl.BlockSpec(memory_space=pl.ANY)
    vmem_spec = pl.BlockSpec(memory_space=pltpu.VMEM)
    kl, dhid, dhead = pl.pallas_call(
        kernel,
        out_shape=(vm((1, ROWS), F32), vm((56, ROWS), BF16), vm((SLAB, D), BF16)),
        in_specs=[any_spec, vmem_spec, any_spec, any_spec],
        out_specs=(vmem_spec, vmem_spec, vmem_spec),
        scratch_shapes=[
            vm((512, D), BF16),
            vm((2 * VP, D), BF16),
            vm((2, 4, 4, CHIPCOL, 2 * VP), BF16),
            vm((256, 256), BF16),
            vm((3000, ROWS), BF16),
            vm((4, VP, ROWS), BF16),
            vm((4, VP, ROWS), BF16),
            vm((VP, ROWS), BF16),
            vm((2, VP, ROWS), BF16),
            vm((2 * VP, HALF), F32),
            vm((2 * VP, HALF), F32),
            vm((2 * VP, HALF), BF16),
            vm((VP, 512), BF16),
            vm((16, 128), F32),
            vm((16, 16, 128), F32),
            vm((16, 128), F32),
            vm((16, 16, 128), F32),
            vm((16, 128), F32),
            vm((8, 128), F32),
            vm((8, 128), F32),
            vm((8, 128), F32),
            vm((16, 8, 128), F32),
            vm((8, 128), F32),
            vm((16, 8, 128), F32),
            vm((8, 128), F32),
            vm((2, 4, 2, CHIPCOL, 128), F32),
            vm((2, 4, 2, CHIPCOL, 128), F32),
            vm((4, 4, 2, CHIPCOL, 128), BF16),
            vm((6, 4, 2, CHIPCOL, 128), BF16),
            vm((2, 4, 2, CHIPCOL, 128), BF16),
            vm((2, 4, 2, CHIPCOL, 128), BF16),
            vm((2, 3, 2, CHIPCOL, 128), BF16),
            vm((2, 2, 2, 64, 128), BF16),
            vm((8, 64, 128), BF16),
            dma((4,)),
            dma((2,)), dma((2,)),
            dma((2,)), dma((2,)),
            dma((2, 3)), dma((2, 3)), dma((2, 6)), dma((2, 6)),
            dma((2,)), dma((2,)),
            dma((6,)), dma((6,)),
            dma((1,)), dma((1,)),
            dma((15,)), dma((15,)), dma((15,)), dma((15,)),
            dma((15,)), dma((15,)), dma((15,)), dma((15,)),
            dma((4,)), dma((4,)), dma((2, 4)), dma((2, 4)), dma((6,)), dma((6,)),
            dma((8,)), dma((8,)),
        ],
        compiler_params=pltpu.CompilerParams(
            collective_id=0, has_side_effects=True, vmem_limit_bytes=50 * 1024 * 1024
        ),
        cost_estimate=pl.CostEstimate(flops=3 * 2 * 512 * 750 * 3584, bytes_accessed=13_000_000, transcendentals=0),
    )(hidden, valid_mask.reshape(1, ROWS), student_head, teacher_logits.T)
    kl, dhid, dhead = pl.pallas_call(
        results,
        out_shape=(
            jax.ShapeDtypeStruct((1, ROWS), F32),
            jax.ShapeDtypeStruct((56, ROWS), BF16),
            jax.ShapeDtypeStruct((SLAB, D), BF16),
        ),
        in_specs=[any_spec] * 3,
        out_specs=(any_spec,) * 3,
        scratch_shapes=[dma((9,))],
        compiler_params=pltpu.CompilerParams(vmem_limit_bytes=1024 * 1024),
    )(kl, dhid, dhead)
    return kl.reshape(ROWS), dhid.T, dhead


def solution(mesh):
    return jax.shard_map(
        on_device,
        mesh=mesh,
        in_specs=(P("tok", None), P("tok"), P(("voc", "tok"), None), P("tok", "voc")),
        out_specs=(P("tok"), P("tok", "voc"), P(("voc", "tok"), None)),
        check_vma=False,
    )
```

```python
import jax
import jax.numpy as jnp
from jax import lax
from jax.experimental import pallas as pl
from jax.experimental.pallas import tpu as pltpu
from jax.sharding import PartitionSpec as P

CAP = 30.0
D = 3584
ROWS = 128
HALF = 256
SLAB = 750
VP = 768
QCOL = D // 4
PIECE = ROWS // 4
CHIPCOL = 112
FAR_FIRST = (8, 10, 6, 9, 7, 11, 5, 12, 4, 2, 14, 13, 3, 15, 1)
MESH = pl.DeviceIdType.MESH
F32 = jnp.float32
BF16 = jnp.bfloat16


def kernel(
    hid, mask, head, teach, kl_out, dhid_out, DH,
    H, HD, HDT, EYE, tin, TS, TR, RLY, TSIB, CP, ES, GV, GTD,
    TT, TG1, TT2, TG2, TOT, AL, BE, CR, CG1, CR2, CG2, KL,
    OWN, NEXT, B1, R1, F1, B2, R2, B3, RZ,
    local, hs, hr, zs, zr, p1s, p1r, p2s, p2r, cs, cr, ts, tr, gs, gr,
    as1, ar1, as2, ar2, bs1, br1, bs2, br2, q1s, q1r, f1s, f1r, q2s, q2r, rzs, rzr,
):
    a = lax.axis_index("tok")
    v = lax.axis_index("voc")
    c = lax.rem(v, 2)
    x = lax.rem(v // 2, 4)
    y = lax.rem(v // 8, 4)
    zl = v // 32
    z = 2 * a + zl
    p = jnp.where(c == 0, x, y)
    q = jnp.where(c == 0, y, x)

    def dev(a_, zl_, y_, x_, c_):
        return (a_, zl_ * 32 + y_ * 8 + x_ * 2 + c_)

    def at_p(p_):
        return dev(a, zl, jnp.where(c == 0, y, p_), jnp.where(c == 0, p_, x), c)

    def at_q(q_):
        return dev(a, zl, jnp.where(c == 0, q_, y), jnp.where(c == 0, x, q_), c)

    sib = dev(a, zl, y, x, 1 - c)

    def at_a(a_):
        return dev(a_, zl, y, x, c)

    def at_xy(k):
        return dev(a, zl, k // 4, lax.rem(k, 4), c)

    def at_zc(k):
        return dev(k // 4, lax.rem(k // 2, 2), y, x, lax.rem(k, 2))

    def mod4(k):
        return lax.rem(k + 8, 4)

    me_xy = y * 4 + x
    me_zc = z * 2 + c

    pending = []

    def send(src, dst, ssem, rsem, to):
        copy = pltpu.make_async_remote_copy(
            src_ref=src, dst_ref=dst, send_sem=ssem, recv_sem=rsem, device_id=to, device_id_type=MESH
        )
        copy.start()
        pending.append(copy)

    def arrived(dst, ssem, rsem):
        pltpu.make_async_remote_copy(
            src_ref=dst, dst_ref=dst, send_sem=ssem, recv_sem=rsem, device_id=sib, device_id_type=MESH
        ).wait_recv()

    barrier = pltpu.get_barrier_semaphore()
    for k in FAR_FIRST:
        pl.semaphore_signal(barrier, inc=1, device_id=at_zc(lax.rem(me_zc + k, 16)), device_id_type=MESH)
    for k in range(1, 16):
        pl.semaphore_signal(barrier, inc=1, device_id=at_xy(lax.rem(me_xy + k, 16)), device_id_type=MESH)

    load_teach = pltpu.make_async_copy(teach, tin, local.at[0])
    load_teach.start()
    load_hid = pltpu.make_async_copy(hid, H.at[pl.ds(0, ROWS)], local.at[1])
    load_hid.start()

    pl.semaphore_wait(barrier, 30)

    def span(start, size):
        return pl.ds(pl.multiple_of(start, 16), size)

    def cols(q_):
        return pl.ds(pl.multiple_of(q_ * QCOL, 128), QCOL)

    def base(g):
        return ROWS + c * ROWS + g * ROWS

    later = []

    def flush():
        for copy in pending:
            copy.wait_send()
        pending.clear()

        @pl.when(c == 1)
        def _():
            for make in later:
                make().wait_send()

        later.clear()

    def each_group(step):
        step(0)

        @pl.when(c == 1)
        def _():
            step(1)

    def send_group(g, make):
        copy = make(g)
        copy.start()
        if g == 0:
            pending.append(copy)
        else:
            later.append(lambda: make(1))

    def remote(src, dst, ssem, rsem, to):
        return pltpu.make_async_remote_copy(
            src_ref=src, dst_ref=dst, send_sem=ssem, recv_sem=rsem, device_id=to, device_id_type=MESH
        )

    each_group(lambda g: send_group(g, lambda g: remote(
        hid.at[span(p * PIECE, PIECE), cols(q)], H.at[span(base(g) + p * PIECE, PIECE), cols(q)],
        zs.at[g], zr.at[g],
        dev(mod4(a - 1 - c - g), jnp.where((c == 1) & (g == 0), 1 - zl, zl), y, x, c),
    )))

    load_head = pltpu.make_async_copy(head.at[pl.ds(0, 736)], HD.at[0:736], local.at[2])
    load_head.start()
    send(head.at[pl.ds(0, 736)], HD.at[VP : VP + 736], hs.at[0], hr.at[0], sib)
    load_tail = pltpu.make_async_copy(head, DH, local.at[3])
    load_tail.start()

    load_teach.wait()
    place = lax.broadcasted_iota(jnp.int32, (VP, ROWS), 0)
    for t in range(4):
        start = t * SLAB // 16 * 16
        off = t * SLAB - start
        height = min(VP + 16, 3000 - start)
        tall = tin[start : start + height].astype(F32)
        if height < VP + 16:
            tall = jnp.concatenate([tall, jnp.zeros((VP + 16 - height, ROWS), F32)], axis=0)
        if off:
            tall = pltpu.roll(tall, VP + 16 - off, 0)
        part = jnp.where(place < SLAB, tall[:VP], -30000.0)
        TS[t] = part.astype(BF16)
    way = jnp.where(c == 0, 1, 3)
    send(TS.at[mod4(a + 2)], RLY, ts.at[2], tr.at[2], at_a(mod4(a + way)))
    TR[0] = TS[a]

    nt = (((1,), (1,)), ((), ()))
    EYE[...] = jnp.where(
        lax.broadcasted_iota(jnp.int32, (256, 256), 0) == lax.broadcasted_iota(jnp.int32, (256, 256), 1), 1.0, 0.0
    ).astype(BF16)

    def turn(slab, half):
        for n in range(7):
            at = pl.ds(half * 1792 + n * 256, 256)
            out = lax.dot_general(
                EYE[...], HD[slab * VP : (slab + 1) * VP, at], nt, preferred_element_type=F32
            ).astype(BF16)
            done = 0
            while done < 256:
                chip, row = divmod(n * 256 + done, CHIPCOL)
                size = min(CHIPCOL - row, 256 - done)
                HDT[half, chip // 4, chip % 4, row : row + size, slab * VP : (slab + 1) * VP] = out[done : done + size]
                done += size

    def piece(g, p_):
        return H.at[span(base(g) + p_ * PIECE, PIECE), cols(q)]

    def first_step(g):
        arrived(piece(g, p), zs.at[g], zr.at[g])
        for d in (2, 1, 3):
            send_group(g, lambda g, d=d: remote(
                piece(g, p), piece(g, p), p1s.at[g, d - 1], p1r.at[g, d - 1], at_p(mod4(p + d)),
            ))

    each_group(first_step)

    TT[...] = jnp.zeros_like(TT)
    teacher_sum = jnp.zeros((1, ROWS), F32)
    for t in range(4):
        teacher_sum = teacher_sum + jnp.sum(jnp.exp(TS[t].astype(F32)), axis=0, keepdims=True)
    TT[pl.ds(4 + a, 1)] = teacher_sum
    TT[pl.ds(8 + a, 1)] = mask[...].astype(F32)

    load_tail.wait()
    HD[736:768] = jnp.concatenate([DH[736:750].astype(F32), jnp.zeros((18, D), F32)], axis=0).astype(BF16)
    send(HD.at[736:768], HD.at[VP + 736 : VP + 768], hs.at[1], hr.at[1], sib)
    load_head.wait()
    turn(0, 0)

    def first_end(g):
        for d in range(1, 4):
            arrived(piece(g, mod4(p - d)), p1s.at[g, d - 1], p1r.at[g, d - 1])

    right, left = at_q(mod4(q + 1)), at_q(mod4(q - 1))
    before, after, across = mod4(q - 1), mod4(q + 1), mod4(q + 2)

    def part_of(g, half, q_):
        return H.at[span(base(g) + half * 64, 64), cols(q_)]

    def pass_on(g, n, half, q_, to):
        send_group(g, lambda g: remote(part_of(g, half, q_), part_of(g, half, q_), p2s.at[g, n], p2r.at[g, n], to))

    def passed(n, half, q_):
        each_group(lambda g: arrived(part_of(g, half, q_), p2s.at[g, n], p2r.at[g, n]))

    def second_step(g):
        first_end(g)
        pass_on(g, 0, 0, q, right)
        pass_on(g, 1, 1, q, left)
        pass_on(g, 2, 1, q, right)
        pass_on(g, 3, 0, q, left)

    def relay_step(g):
        arrived(part_of(g, 0, before), p2s.at[g, 0], p2r.at[g, 0])
        pass_on(g, 4, 0, before, right)
        arrived(part_of(g, 1, after), p2s.at[g, 1], p2r.at[g, 1])
        pass_on(g, 5, 1, after, left)

    each_group(second_step)
    send(TS.at[mod4(a + 1)], TR.at[3], ts.at[0], tr.at[0], at_a(mod4(a + 1)))
    send(TS.at[mod4(a + 3)], TR.at[1], ts.at[1], tr.at[1], at_a(mod4(a + 3)))

    my_half = pl.ds(pl.multiple_of(c * HALF, HALF), HALF)

    def logits(slab, q_, first=False):
        rr = slice(slab * VP, (slab + 1) * VP)
        out = lax.dot_general(HD[rr, cols(q_)], H[my_half, cols(q_)], nt, preferred_element_type=F32)
        CP[rr] = out if first else CP[rr] + out

    load_hid.wait()
    logits(0, q, True)
    turn(0, 1)
    each_group(relay_step)

    arrived(RLY, ts.at[2], tr.at[2])
    send(RLY, TR.at[2], ts.at[3], tr.at[3], at_a(mod4(a + way)))
    passed(2, 1, before)
    logits(0, before)
    passed(3, 0, after)
    logits(0, after)
    arrived(HD.at[VP : VP + 736], hs.at[0], hr.at[0])
    arrived(HD.at[VP + 736 : VP + 768], hs.at[1], hr.at[1])
    logits(1, q, True)
    logits(1, before)
    logits(1, after)
    passed(4, 0, across)
    passed(5, 1, across)
    in_slab = lax.broadcasted_iota(jnp.int32, (256, HALF), 0) < SLAB - 512

    def exponentials(slab, student_sum):
        for k in range(3):
            rr = slice(slab * VP + k * 256, slab * VP + (k + 1) * 256)
            capped = CAP * jnp.tanh(CP[rr] * (1.0 / CAP))
            exps = jnp.exp(capped)
            if k == 2:
                exps = jnp.where(in_slab, exps, 0.0)
            CP[rr] = capped
            ES[rr] = exps
            student_sum = student_sum + jnp.sum(exps, axis=0, keepdims=True)
        return student_sum

    logits(0, across)
    logits(1, across)
    student_sum = exponentials(0, jnp.zeros((1, HALF), F32))
    student_sum = exponentials(1, student_sum)
    my_rows = (mod4(a + 2 * c), mod4(a + 2 * c + 1))
    for i in range(2):
        TT[pl.ds(my_rows[i], 1)] = student_sum[:, i * 128 : (i + 1) * 128]

    def exchange_start(tile, slots, ssem, rsem, me, at):
        for k in FAR_FIRST:
            send(tile, slots.at[me], ssem.at[k - 1], rsem.at[k - 1], at(lax.rem(me + k, 16)))

    def exchange_end(tile, slots, ssem, rsem, me):
        slots[me] = tile[...]
        for k in range(1, 16):
            arrived(slots.at[lax.rem(me + 16 - k, 16)], ssem.at[k - 1], rsem.at[k - 1])
        total = slots[0]
        for k in range(1, 16):
            total = total + slots[k]
        return total

    gathered = list(pending), list(later)
    pending.clear()
    later.clear()
    exchange_start(TT, TG1, as1, ar1, me_xy, at_xy)

    def factors(slab, cross_sum):
        for k in range(6):
            rr = slice(slab * VP + k * 128, slab * VP + (k + 1) * 128)
            vv = slice(k * 128, (k + 1) * 128)
            if slab == 0:
                target = jnp.concatenate([TR[2 * c, vv], TR[2 * c + 1, vv]], axis=1).astype(F32)
            else:
                target = jnp.concatenate([TSIB[0, vv], TSIB[1, vv]], axis=1).astype(F32)
            expd = jnp.exp(target)
            capped = CP[rr]
            cross_sum = cross_sum + jnp.sum(expd * (target - capped), axis=0, keepdims=True)
            ratio = capped * (1.0 / CAP)
            slope = 1.0 - ratio * ratio
            ES[rr] = ES[rr] * slope
            CP[rr] = expd * slope
        return cross_sum

    for copy in gathered[0]:
        copy.wait_send()

    @pl.when(c == 1)
    def _():
        for make in gathered[1]:
            make().wait_send()

    turn(1, 0)

    def give(i):
        send(TR.at[2 * (1 - c) + i], TSIB.at[i], ts.at[4 + i], tr.at[4 + i], sib)

    arrived(TR.at[3], ts.at[0], tr.at[0])
    arrived(TR.at[1], ts.at[1], tr.at[1])
    give(1)
    TT2[...] = exchange_end(TT, TG1, as1, ar1, me_xy)
    exchange_start(TT2, TG2, as2, ar2, me_zc, at_zc)
    arrived(TR.at[2], ts.at[3], tr.at[3])
    give(0)
    cross_sum = factors(0, jnp.zeros((1, HALF), F32))
    turn(1, 1)
    for i in range(2):
        arrived(TSIB.at[i], ts.at[4 + i], tr.at[4 + i])
    cross_sum = factors(1, cross_sum)
    TOT[...] = exchange_end(TT2, TG2, as2, ar2, me_zc)

    valid = TOT[8:12] * (1.0 / 64.0)
    weight = valid * (512.0 / jnp.sum(valid))
    AL[0:4] = weight / TOT[0:4]
    BE[0:4] = weight / TOT[4:8]
    alpha = jnp.concatenate([AL[pl.ds(r, 1)] for r in my_rows], axis=1)
    beta = jnp.concatenate([BE[pl.ds(r, 1)] for r in my_rows], axis=1)
    for k in range(12):
        rr = slice(k * 128, (k + 1) * 128)
        grad = (ES[rr] * alpha - CP[rr] * beta).astype(BF16)
        GV[rr] = grad
        if k < 6:
            GTD[rr, my_half] = grad

    up, down, far = mod4(p + 1), mod4(p - 1), mod4(p + 2)

    def partial(n, p_):
        rows = []
        for i in range(4):
            rows.append(HDT[n, jnp.where(c == 0, i, p_), jnp.where(c == 0, p_, i)])
        return jnp.dot(jnp.concatenate(rows, axis=0), GV[...], preferred_element_type=F32)

    def put(ref, n, block):
        for i in range(4):
            ref[n, i] = block[i * CHIPCOL : (i + 1) * CHIPCOL].astype(ref.dtype)

    put(B1, 0, partial(0, far))
    send(B1.at[0], R1.at[0], q1s.at[0], q1r.at[0], at_p(up))
    put(B1, 1, partial(1, far))
    send(B1.at[1], R1.at[1], q1s.at[1], q1r.at[1], at_p(down))
    put(B1, 3, partial(0, down))
    send(B1.at[3], R1.at[3], q1s.at[3], q1r.at[3], at_p(down))
    put(B1, 2, partial(1, up))
    send(B1.at[2], R1.at[2], q1s.at[2], q1r.at[2], at_p(up))
    send(GV.at[VP : 2 * VP], GTD.at[:, my_half], gs.at[0], gr.at[0], sib)

    def share(g):
        return H.at[span(base(g), ROWS)]

    each_group(lambda g: send_group(g, lambda g: remote(share(g), share(g), cs.at[g], cr.at[g], sib)))


    def head_chunk(n):
        at = pl.ds(pl.multiple_of(n * 512, 512), 512)
        out = jnp.dot(GTD[...], H[:, at], preferred_element_type=F32)
        DH[:, at] = out[:SLAB].astype(BF16)

    def head_chunks(first, last):
        @pl.loop(first, last)
        def _(n):
            head_chunk(n)

    qup, qdown, qfar = mod4(q + 1), mod4(q - 1), mod4(q + 2)
    order = (qfar, qup, qdown, q)

    def relay(k):
        arrived(R1.at[k], q1s.at[k], q1r.at[k])
        near = up if k == 0 else down
        for n, i in enumerate(order):
            F1[k, i] = (NEXT[k, i] + R1[k, i].astype(F32)).astype(BF16)
            send(F1.at[k, i], R1.at[4 + k, i], f1s.at[k, n], f1r.at[k, n], at_p(near))

    def second(k, n):
        i = order[n]
        arrived(R1.at[4 + k, i], f1s.at[k, n], f1r.at[k, n])
        total = OWN[k, i] + R1[3 - k, i].astype(F32) + R1[4 + k, i].astype(F32)
        if n == 3:
            OWN[k, i] = total
        else:
            B2[k, i] = total.astype(BF16)
            send(B2.at[k, i], R2.at[k, n], q2s.at[k * 3 + n], q2r.at[k * 3 + n], at_q(i))

    put(NEXT, 0, partial(0, up))
    relay(0)
    put(NEXT, 1, partial(1, down))
    relay(1)

    CR[...] = jnp.zeros_like(CR)
    for i in range(2):
        CR[pl.ds(my_rows[i], 1)] = cross_sum[:, i * 128 : (i + 1) * 128]
    exchange_start(CR, CG1, bs1, br1, me_xy, at_xy)

    put(OWN, 0, partial(0, p))
    put(OWN, 1, partial(1, p))
    arrived(GTD.at[:, pl.ds(pl.multiple_of((1 - c) * HALF, HALF), HALF)], gs.at[0], gr.at[0])
    arrived(H.at[span(ROWS + (1 - c) * ROWS, ROWS)], cs.at[0], cr.at[0])

    @pl.when(c == 0)
    def _():
        arrived(H.at[3 * ROWS : 4 * ROWS], cs.at[1], cr.at[1])

    head_chunks(0, 2)
    arrived(R1.at[3], q1s.at[3], q1r.at[3])
    arrived(R1.at[2], q1s.at[2], q1r.at[2])
    for n in range(4):
        for k in range(2):
            second(k, n)
    CR2[...] = exchange_end(CR, CG1, bs1, br1, me_xy)
    exchange_start(CR2, CG2, bs2, br2, me_zc, at_zc)
    head_chunks(2, 4)

    at_home = (c == 0) & (zl == 0)
    at_home_hi = (c == 0) & (zl == 1)

    def to_owner(k, i, c_):
        n = k * 4 + i * 2 + c_
        return pltpu.make_async_remote_copy(
            src_ref=B3.at[k, i, c_], dst_ref=RZ.at[z], send_sem=rzs.at[n], recv_sem=rzr.at[z],
            device_id=dev(mod4(a + 2 * c + i), k, y, x, c_), device_id_type=MESH,
        )

    owners = [(k, i, c_) for k in range(2) for i in range(2) for c_ in range(2)]
    for k in range(2):
        total = OWN[k, q]
        for n in range(3):
            arrived(R2.at[k, n], q2s.at[k * 3 + n], q2r.at[k * 3 + n])
            total = total + R2[k, n].astype(F32)
        for i in range(2):
            for c_ in range(2):
                B3[k, i, c_] = total[48 * c_ : 48 * c_ + 64, i * 128 : (i + 1) * 128].astype(BF16)
                if i == 0 and c_ == 0:
                    home = at_home if k == 0 else at_home_hi

                    @pl.when(jnp.logical_not(home))
                    def _():
                        to_owner(k, i, c_).start()

                    @pl.when(home)
                    def _():
                        RZ[z] = B3[k, 0, 0]
                else:
                    to_owner(k, i, c_).start()

    head_chunks(4, 7)
    cross = exchange_end(CR2, CG2, bs2, br2, me_zc)
    KL[0:4] = cross[0:4] / TOT[4:8] - jnp.log(TOT[4:8]) + jnp.log(TOT[0:4])
    kl_out[...] = KL[pl.ds(a, 1)]

    flush()
    for k, i, c_ in owners:
        if i == 0 and c_ == 0:
            home = at_home if k == 0 else at_home_hi

            @pl.when(jnp.logical_not(home))
            def _():
                to_owner(k, i, c_).wait_send()
        else:
            to_owner(k, i, c_).wait_send()

    @pl.when(c == 1)
    def _():
        arrived(RZ.at[z], rzs.at[0], rzr.at[z])

    for k in range(1, 8):
        source = lax.rem(z + k, 8)
        arrived(RZ.at[source], rzs.at[0], rzr.at[source])
    total = RZ[0].astype(F32)
    for k in range(1, 8):
        total = total + RZ[k].astype(F32)
    dhid_out[...] = jnp.where(c == 0, total[0:56], total[8:64]).astype(BF16)


def results(kl, dhid, dhead, kl_out, dhid_out, dhead_out, sem):
    copies = [
        pltpu.make_async_copy(dhid, dhid_out, sem.at[7]),
        pltpu.make_async_copy(kl, kl_out, sem.at[8]),
    ]
    for n in range(7):
        at = pl.ds(n * 512, 512)
        copies.append(pltpu.make_async_copy(dhead.at[:, at], dhead_out.at[:, at], sem.at[n]))
    for copy in copies:
        copy.start()
    for copy in copies:
        copy.wait()


def on_device(hidden, valid_mask, student_head, teacher_logits):
    vm = pltpu.VMEM
    dma = pltpu.SemaphoreType.DMA
    any_spec = pl.BlockSpec(memory_space=pl.ANY)
    vmem_spec = pl.BlockSpec(memory_space=pltpu.VMEM)
    kl, dhid, dhead = pl.pallas_call(
        kernel,
        out_shape=(vm((1, ROWS), F32), vm((56, ROWS), BF16), vm((SLAB, D), BF16)),
        in_specs=[any_spec, vmem_spec, any_spec, any_spec],
        out_specs=(vmem_spec, vmem_spec, vmem_spec),
        scratch_shapes=[
            vm((512, D), BF16),
            vm((2 * VP, D), BF16),
            vm((2, 4, 4, CHIPCOL, 2 * VP), BF16),
            vm((256, 256), BF16),
            vm((3000, ROWS), BF16),
            vm((4, VP, ROWS), BF16),
            vm((4, VP, ROWS), BF16),
            vm((VP, ROWS), BF16),
            vm((2, VP, ROWS), BF16),
            vm((2 * VP, HALF), F32),
            vm((2 * VP, HALF), F32),
            vm((2 * VP, HALF), BF16),
            vm((VP, 512), BF16),
            vm((16, 128), F32),
            vm((16, 16, 128), F32),
            vm((16, 128), F32),
            vm((16, 16, 128), F32),
            vm((16, 128), F32),
            vm((8, 128), F32),
            vm((8, 128), F32),
            vm((8, 128), F32),
            vm((16, 8, 128), F32),
            vm((8, 128), F32),
            vm((16, 8, 128), F32),
            vm((8, 128), F32),
            vm((2, 4, CHIPCOL, HALF), F32),
            vm((2, 4, CHIPCOL, HALF), F32),
            vm((4, 4, CHIPCOL, HALF), BF16),
            vm((6, 4, CHIPCOL, HALF), BF16),
            vm((2, 4, CHIPCOL, HALF), BF16),
            vm((2, 4, CHIPCOL, HALF), BF16),
            vm((2, 3, CHIPCOL, HALF), BF16),
            vm((2, 2, 2, 64, 128), BF16),
            vm((8, 64, 128), BF16),
            dma((4,)),
            dma((2,)), dma((2,)),
            dma((2,)), dma((2,)),
            dma((2, 3)), dma((2, 3)), dma((2, 6)), dma((2, 6)),
            dma((2,)), dma((2,)),
            dma((6,)), dma((6,)),
            dma((1,)), dma((1,)),
            dma((15,)), dma((15,)), dma((15,)), dma((15,)),
            dma((15,)), dma((15,)), dma((15,)), dma((15,)),
            dma((4,)), dma((4,)), dma((2, 4)), dma((2, 4)), dma((6,)), dma((6,)),
            dma((8,)), dma((8,)),
        ],
        compiler_params=pltpu.CompilerParams(
            collective_id=0, has_side_effects=True, vmem_limit_bytes=50 * 1024 * 1024
        ),
        cost_estimate=pl.CostEstimate(flops=3 * 2 * 512 * 750 * 3584, bytes_accessed=13_000_000, transcendentals=0),
    )(hidden, valid_mask.reshape(1, ROWS), student_head, teacher_logits.T)
    kl, dhid, dhead = pl.pallas_call(
        results,
        out_shape=(
            jax.ShapeDtypeStruct((1, ROWS), F32),
            jax.ShapeDtypeStruct((56, ROWS), BF16),
            jax.ShapeDtypeStruct((SLAB, D), BF16),
        ),
        in_specs=[any_spec] * 3,
        out_specs=(any_spec,) * 3,
        scratch_shapes=[dma((9,))],
        compiler_params=pltpu.CompilerParams(vmem_limit_bytes=1024 * 1024),
    )(kl, dhid, dhead)
    return kl.reshape(ROWS), dhid.T, dhead


def solution(mesh):
    return jax.shard_map(
        on_device,
        mesh=mesh,
        in_specs=(P("tok", None), P("tok"), P(("voc", "tok"), None), P("tok", "voc")),
        out_specs=(P("tok"), P("tok", "voc"), P(("voc", "tok"), None)),
        check_vma=False,
    )
```

```python
import jax
import jax.numpy as jnp
from jax import lax
from jax.experimental import pallas as pl
from jax.experimental.pallas import tpu as pltpu
from jax.sharding import PartitionSpec as P

CAP = 30.0
D = 3584
ROWS = 128
HALF = 256
SLAB = 750
VP = 768
QCOL = D // 4
PIECE = ROWS // 4
CHIPCOL = 112
FAR_FIRST = (8, 10, 6, 9, 7, 11, 5, 12, 4, 2, 14, 13, 3, 15, 1)
MESH = pl.DeviceIdType.MESH
F32 = jnp.float32
BF16 = jnp.bfloat16


def kernel(
    hid, mask, head, teach, kl_out, dhid_out, DH,
    H, HD, HDT, EYE, tin, TS, TR, RLY, TSIB, CP, ES, GV, GTD,
    TT, TG1, TT2, TG2, TOT, AL, BE, CR, CG1, CR2, CG2, KL,
    OWN, NEXT, B1, R1, F1, B2, R2, B3, RZ,
    local, hs, hr, zs, zr, p1s, p1r, p2s, p2r, cs, cr, ts, tr, gs, gr,
    as1, ar1, as2, ar2, bs1, br1, bs2, br2, q1s, q1r, f1s, f1r, q2s, q2r, rzs, rzr,
):
    a = lax.axis_index("tok")
    v = lax.axis_index("voc")
    c = lax.rem(v, 2)
    x = lax.rem(v // 2, 4)
    y = lax.rem(v // 8, 4)
    zl = v // 32
    z = 2 * a + zl
    p = jnp.where(c == 0, x, y)
    q = jnp.where(c == 0, y, x)

    def dev(a_, zl_, y_, x_, c_):
        return (a_, zl_ * 32 + y_ * 8 + x_ * 2 + c_)

    def at_p(p_):
        return dev(a, zl, jnp.where(c == 0, y, p_), jnp.where(c == 0, p_, x), c)

    def at_q(q_):
        return dev(a, zl, jnp.where(c == 0, q_, y), jnp.where(c == 0, x, q_), c)

    sib = dev(a, zl, y, x, 1 - c)

    def at_a(a_):
        return dev(a_, zl, y, x, c)

    def at_xy(k):
        return dev(a, zl, k // 4, lax.rem(k, 4), c)

    def at_zc(k):
        return dev(k // 4, lax.rem(k // 2, 2), y, x, lax.rem(k, 2))

    def mod4(k):
        return lax.rem(k + 8, 4)

    me_xy = y * 4 + x
    me_zc = z * 2 + c

    pending = []

    def send(src, dst, ssem, rsem, to):
        copy = pltpu.make_async_remote_copy(
            src_ref=src, dst_ref=dst, send_sem=ssem, recv_sem=rsem, device_id=to, device_id_type=MESH
        )
        copy.start()
        pending.append(copy)

    def arrived(dst, ssem, rsem):
        pltpu.make_async_remote_copy(
            src_ref=dst, dst_ref=dst, send_sem=ssem, recv_sem=rsem, device_id=sib, device_id_type=MESH
        ).wait_recv()

    barrier = pltpu.get_barrier_semaphore()
    for k in FAR_FIRST:
        pl.semaphore_signal(barrier, inc=1, device_id=at_zc(lax.rem(me_zc + k, 16)), device_id_type=MESH)
    for k in range(1, 16):
        pl.semaphore_signal(barrier, inc=1, device_id=at_xy(lax.rem(me_xy + k, 16)), device_id_type=MESH)

    load_teach = pltpu.make_async_copy(teach, tin, local.at[0])
    load_teach.start()
    load_hid = pltpu.make_async_copy(hid, H.at[pl.ds(0, ROWS)], local.at[1])
    load_hid.start()

    pl.semaphore_wait(barrier, 30)

    def span(start, size):
        return pl.ds(pl.multiple_of(start, 16), size)

    def cols(q_):
        return pl.ds(pl.multiple_of(q_ * QCOL, 128), QCOL)

    def base(g):
        return ROWS + c * ROWS + g * ROWS

    later = []

    def flush():
        for copy in pending:
            copy.wait_send()
        pending.clear()

        @pl.when(c == 1)
        def _():
            for make in later:
                make().wait_send()

        later.clear()

    def each_group(step):
        step(0)

        @pl.when(c == 1)
        def _():
            step(1)

    def send_group(g, make):
        copy = make(g)
        copy.start()
        if g == 0:
            pending.append(copy)
        else:
            later.append(lambda: make(1))

    def remote(src, dst, ssem, rsem, to):
        return pltpu.make_async_remote_copy(
            src_ref=src, dst_ref=dst, send_sem=ssem, recv_sem=rsem, device_id=to, device_id_type=MESH
        )

    each_group(lambda g: send_group(g, lambda g: remote(
        hid.at[span(p * PIECE, PIECE), cols(q)], H.at[span(base(g) + p * PIECE, PIECE), cols(q)],
        zs.at[g], zr.at[g],
        dev(mod4(a - 1 - c - g), jnp.where((c == 1) & (g == 0), 1 - zl, zl), y, x, c),
    )))

    load_head = pltpu.make_async_copy(head.at[pl.ds(0, 736)], HD.at[0:736], local.at[2])
    load_head.start()
    send(head.at[pl.ds(0, 736)], HD.at[VP : VP + 736], hs.at[0], hr.at[0], sib)
    load_tail = pltpu.make_async_copy(head, DH, local.at[3])
    load_tail.start()

    load_teach.wait()
    place = lax.broadcasted_iota(jnp.int32, (VP, ROWS), 0)
    for t in range(4):
        start = t * SLAB // 16 * 16
        off = t * SLAB - start
        height = min(VP + 16, 3000 - start)
        tall = tin[start : start + height].astype(F32)
        if height < VP + 16:
            tall = jnp.concatenate([tall, jnp.zeros((VP + 16 - height, ROWS), F32)], axis=0)
        if off:
            tall = pltpu.roll(tall, VP + 16 - off, 0)
        part = jnp.where(place < SLAB, tall[:VP], -30000.0)
        TS[t] = part.astype(BF16)
    way = jnp.where(c == 0, 1, 3)
    send(TS.at[mod4(a + 2)], RLY, ts.at[2], tr.at[2], at_a(mod4(a + way)))
    TR[0] = TS[a]

    nt = (((1,), (1,)), ((), ()))
    EYE[...] = jnp.where(
        lax.broadcasted_iota(jnp.int32, (256, 256), 0) == lax.broadcasted_iota(jnp.int32, (256, 256), 1), 1.0, 0.0
    ).astype(BF16)

    def turn(slab, half):
        for n in range(7):
            at = pl.ds(half * 1792 + n * 256, 256)
            out = lax.dot_general(
                EYE[...], HD[slab * VP : (slab + 1) * VP, at], nt, preferred_element_type=F32
            ).astype(BF16)
            done = 0
            while done < 256:
                chip, row = divmod(n * 256 + done, CHIPCOL)
                size = min(CHIPCOL - row, 256 - done)
                HDT[half, chip // 4, chip % 4, row : row + size, slab * VP : (slab + 1) * VP] = out[done : done + size]
                done += size

    def piece(g, p_):
        return H.at[span(base(g) + p_ * PIECE, PIECE), cols(q)]

    def first_step(g):
        arrived(piece(g, p), zs.at[g], zr.at[g])
        for d in (2, 1, 3):
            send_group(g, lambda g, d=d: remote(
                piece(g, p), piece(g, p), p1s.at[g, d - 1], p1r.at[g, d - 1], at_p(mod4(p + d)),
            ))

    each_group(first_step)

    TT[...] = jnp.zeros_like(TT)
    teacher_sum = jnp.zeros((1, ROWS), F32)
    for t in range(4):
        teacher_sum = teacher_sum + jnp.sum(jnp.exp(TS[t].astype(F32)), axis=0, keepdims=True)
    TT[pl.ds(4 + a, 1)] = teacher_sum
    TT[pl.ds(8 + a, 1)] = mask[...].astype(F32)

    load_tail.wait()
    HD[736:768] = jnp.concatenate([DH[736:750].astype(F32), jnp.zeros((18, D), F32)], axis=0).astype(BF16)
    send(HD.at[736:768], HD.at[VP + 736 : VP + 768], hs.at[1], hr.at[1], sib)
    load_head.wait()
    turn(0, 0)

    def first_end(g):
        for d in range(1, 4):
            arrived(piece(g, mod4(p - d)), p1s.at[g, d - 1], p1r.at[g, d - 1])

    right, left = at_q(mod4(q + 1)), at_q(mod4(q - 1))
    before, after, across = mod4(q - 1), mod4(q + 1), mod4(q + 2)

    def part_of(g, half, q_):
        return H.at[span(base(g) + half * 64, 64), cols(q_)]

    def pass_on(g, n, half, q_, to):
        send_group(g, lambda g: remote(part_of(g, half, q_), part_of(g, half, q_), p2s.at[g, n], p2r.at[g, n], to))

    def passed(n, half, q_):
        each_group(lambda g: arrived(part_of(g, half, q_), p2s.at[g, n], p2r.at[g, n]))

    def second_step(g):
        first_end(g)
        pass_on(g, 0, 0, q, right)
        pass_on(g, 1, 1, q, left)
        pass_on(g, 2, 1, q, right)
        pass_on(g, 3, 0, q, left)

    def relay_step(g):
        arrived(part_of(g, 0, before), p2s.at[g, 0], p2r.at[g, 0])
        pass_on(g, 4, 0, before, right)
        arrived(part_of(g, 1, after), p2s.at[g, 1], p2r.at[g, 1])
        pass_on(g, 5, 1, after, left)

    each_group(second_step)
    send(TS.at[mod4(a + 1)], TR.at[3], ts.at[0], tr.at[0], at_a(mod4(a + 1)))
    send(TS.at[mod4(a + 3)], TR.at[1], ts.at[1], tr.at[1], at_a(mod4(a + 3)))

    my_half = pl.ds(pl.multiple_of(c * HALF, HALF), HALF)

    def logits(slab, q_, first=False):
        rr = slice(slab * VP, (slab + 1) * VP)
        out = lax.dot_general(HD[rr, cols(q_)], H[my_half, cols(q_)], nt, preferred_element_type=F32)
        CP[rr] = out if first else CP[rr] + out

    load_hid.wait()
    logits(0, q, True)
    turn(0, 1)
    each_group(relay_step)

    arrived(RLY, ts.at[2], tr.at[2])
    send(RLY, TR.at[2], ts.at[3], tr.at[3], at_a(mod4(a + way)))
    passed(2, 1, before)
    logits(0, before)
    passed(3, 0, after)
    logits(0, after)
    arrived(HD.at[VP : VP + 736], hs.at[0], hr.at[0])
    arrived(HD.at[VP + 736 : VP + 768], hs.at[1], hr.at[1])
    logits(1, q, True)
    logits(1, before)
    logits(1, after)
    turn(1, 0)
    passed(4, 0, across)
    passed(5, 1, across)
    in_slab = lax.broadcasted_iota(jnp.int32, (256, HALF), 0) < SLAB - 512

    def exponentials(slab, student_sum):
        for k in range(3):
            rr = slice(slab * VP + k * 256, slab * VP + (k + 1) * 256)
            capped = CAP * jnp.tanh(CP[rr] * (1.0 / CAP))
            exps = jnp.exp(capped)
            if k == 2:
                exps = jnp.where(in_slab, exps, 0.0)
            CP[rr] = capped
            ES[rr] = exps
            student_sum = student_sum + jnp.sum(exps, axis=0, keepdims=True)
        return student_sum

    logits(0, across)
    logits(1, across)
    student_sum = exponentials(0, jnp.zeros((1, HALF), F32))
    student_sum = exponentials(1, student_sum)
    my_rows = (mod4(a + 2 * c), mod4(a + 2 * c + 1))
    for i in range(2):
        TT[pl.ds(my_rows[i], 1)] = student_sum[:, i * 128 : (i + 1) * 128]

    def exchange_start(tile, slots, ssem, rsem, me, at):
        for k in FAR_FIRST:
            send(tile, slots.at[me], ssem.at[k - 1], rsem.at[k - 1], at(lax.rem(me + k, 16)))

    def exchange_end(tile, slots, ssem, rsem, me):
        slots[me] = tile[...]
        for k in range(1, 16):
            arrived(slots.at[lax.rem(me + 16 - k, 16)], ssem.at[k - 1], rsem.at[k - 1])
        total = slots[0]
        for k in range(1, 16):
            total = total + slots[k]
        return total

    gathered = list(pending), list(later)
    pending.clear()
    later.clear()
    exchange_start(TT, TG1, as1, ar1, me_xy, at_xy)

    def factors(slab, cross_sum):
        for k in range(6):
            rr = slice(slab * VP + k * 128, slab * VP + (k + 1) * 128)
            vv = slice(k * 128, (k + 1) * 128)
            if slab == 0:
                target = jnp.concatenate([TR[2 * c, vv], TR[2 * c + 1, vv]], axis=1).astype(F32)
            else:
                target = jnp.concatenate([TSIB[0, vv], TSIB[1, vv]], axis=1).astype(F32)
            expd = jnp.exp(target)
            capped = CP[rr]
            cross_sum = cross_sum + jnp.sum(expd * (target - capped), axis=0, keepdims=True)
            ratio = capped * (1.0 / CAP)
            slope = 1.0 - ratio * ratio
            ES[rr] = ES[rr] * slope
            CP[rr] = expd * slope
        return cross_sum

    turn(1, 1)

    def give(i):
        send(TR.at[2 * (1 - c) + i], TSIB.at[i], ts.at[4 + i], tr.at[4 + i], sib)

    arrived(TR.at[3], ts.at[0], tr.at[0])
    arrived(TR.at[1], ts.at[1], tr.at[1])
    give(1)
    TT2[...] = exchange_end(TT, TG1, as1, ar1, me_xy)
    exchange_start(TT2, TG2, as2, ar2, me_zc, at_zc)
    arrived(TR.at[2], ts.at[3], tr.at[3])
    give(0)
    cross_sum = factors(0, jnp.zeros((1, HALF), F32))
    for i in range(2):
        arrived(TSIB.at[i], ts.at[4 + i], tr.at[4 + i])
    cross_sum = factors(1, cross_sum)
    TOT[...] = exchange_end(TT2, TG2, as2, ar2, me_zc)

    valid = TOT[8:12] * (1.0 / 64.0)
    weight = valid * (512.0 / jnp.sum(valid))
    AL[0:4] = weight / TOT[0:4]
    BE[0:4] = weight / TOT[4:8]
    alpha = jnp.concatenate([AL[pl.ds(r, 1)] for r in my_rows], axis=1)
    beta = jnp.concatenate([BE[pl.ds(r, 1)] for r in my_rows], axis=1)
    for k in range(12):
        rr = slice(k * 128, (k + 1) * 128)
        grad = (ES[rr] * alpha - CP[rr] * beta).astype(BF16)
        GV[rr] = grad
        if k < 6:
            GTD[rr, my_half] = grad

    up, down, far = mod4(p + 1), mod4(p - 1), mod4(p + 2)

    def partial(n, p_):
        rows = []
        for i in range(4):
            rows.append(HDT[n, jnp.where(c == 0, i, p_), jnp.where(c == 0, p_, i)])
        return jnp.dot(jnp.concatenate(rows, axis=0), GV[...], preferred_element_type=F32)

    def put(ref, n, block):
        for i in range(4):
            ref[n, i] = block[i * CHIPCOL : (i + 1) * CHIPCOL].astype(ref.dtype)

    put(B1, 0, partial(0, far))
    send(B1.at[0], R1.at[0], q1s.at[0], q1r.at[0], at_p(up))
    put(B1, 1, partial(1, far))
    send(B1.at[1], R1.at[1], q1s.at[1], q1r.at[1], at_p(down))
    put(B1, 3, partial(0, down))
    send(B1.at[3], R1.at[3], q1s.at[3], q1r.at[3], at_p(down))
    put(B1, 2, partial(1, up))
    send(B1.at[2], R1.at[2], q1s.at[2], q1r.at[2], at_p(up))
    send(GV.at[VP : 2 * VP], GTD.at[:, my_half], gs.at[0], gr.at[0], sib)

    def share(g):
        return H.at[span(base(g), ROWS)]

    each_group(lambda g: send_group(g, lambda g: remote(share(g), share(g), cs.at[g], cr.at[g], sib)))


    def head_chunk(n):
        at = pl.ds(pl.multiple_of(n * 512, 512), 512)
        out = jnp.dot(GTD[...], H[:, at], preferred_element_type=F32)
        DH[:, at] = out[:SLAB].astype(BF16)

    def head_chunks(first, last):
        @pl.loop(first, last)
        def _(n):
            head_chunk(n)

    qup, qdown, qfar = mod4(q + 1), mod4(q - 1), mod4(q + 2)
    order = (qfar, qup, qdown, q)

    def relay(k):
        arrived(R1.at[k], q1s.at[k], q1r.at[k])
        near = up if k == 0 else down
        for n, i in enumerate(order):
            F1[k, i] = (NEXT[k, i] + R1[k, i].astype(F32)).astype(BF16)
            send(F1.at[k, i], R1.at[4 + k, i], f1s.at[k, n], f1r.at[k, n], at_p(near))

    def second(k, n):
        i = order[n]
        arrived(R1.at[4 + k, i], f1s.at[k, n], f1r.at[k, n])
        total = OWN[k, i] + R1[3 - k, i].astype(F32) + R1[4 + k, i].astype(F32)
        if n == 3:
            OWN[k, i] = total
        else:
            B2[k, i] = total.astype(BF16)
            send(B2.at[k, i], R2.at[k, n], q2s.at[k * 3 + n], q2r.at[k * 3 + n], at_q(i))

    put(NEXT, 0, partial(0, up))
    relay(0)
    put(NEXT, 1, partial(1, down))
    relay(1)

    CR[...] = jnp.zeros_like(CR)
    for i in range(2):
        CR[pl.ds(my_rows[i], 1)] = cross_sum[:, i * 128 : (i + 1) * 128]
    exchange_start(CR, CG1, bs1, br1, me_xy, at_xy)

    put(OWN, 0, partial(0, p))
    put(OWN, 1, partial(1, p))
    arrived(GTD.at[:, pl.ds(pl.multiple_of((1 - c) * HALF, HALF), HALF)], gs.at[0], gr.at[0])
    arrived(H.at[span(ROWS + (1 - c) * ROWS, ROWS)], cs.at[0], cr.at[0])

    @pl.when(c == 0)
    def _():
        arrived(H.at[3 * ROWS : 4 * ROWS], cs.at[1], cr.at[1])

    for copy in gathered[0]:
        copy.wait_send()

    @pl.when(c == 1)
    def _():
        for make in gathered[1]:
            make().wait_send()

    head_chunks(0, 2)
    arrived(R1.at[3], q1s.at[3], q1r.at[3])
    arrived(R1.at[2], q1s.at[2], q1r.at[2])
    for n in range(4):
        for k in range(2):
            second(k, n)
    CR2[...] = exchange_end(CR, CG1, bs1, br1, me_xy)
    exchange_start(CR2, CG2, bs2, br2, me_zc, at_zc)
    head_chunks(2, 4)

    at_home = (c == 0) & (zl == 0)
    at_home_hi = (c == 0) & (zl == 1)

    def to_owner(k, i, c_):
        n = k * 4 + i * 2 + c_
        return pltpu.make_async_remote_copy(
            src_ref=B3.at[k, i, c_], dst_ref=RZ.at[z], send_sem=rzs.at[n], recv_sem=rzr.at[z],
            device_id=dev(mod4(a + 2 * c + i), k, y, x, c_), device_id_type=MESH,
        )

    owners = [(k, i, c_) for k in range(2) for i in range(2) for c_ in range(2)]
    for k in range(2):
        total = OWN[k, q]
        for n in range(3):
            arrived(R2.at[k, n], q2s.at[k * 3 + n], q2r.at[k * 3 + n])
            total = total + R2[k, n].astype(F32)
        for i in range(2):
            for c_ in range(2):
                B3[k, i, c_] = total[48 * c_ : 48 * c_ + 64, i * 128 : (i + 1) * 128].astype(BF16)
                if i == 0 and c_ == 0:
                    home = at_home if k == 0 else at_home_hi

                    @pl.when(jnp.logical_not(home))
                    def _():
                        to_owner(k, i, c_).start()

                    @pl.when(home)
                    def _():
                        RZ[z] = B3[k, 0, 0]
                else:
                    to_owner(k, i, c_).start()

    head_chunks(4, 7)
    cross = exchange_end(CR2, CG2, bs2, br2, me_zc)
    KL[0:4] = cross[0:4] / TOT[4:8] - jnp.log(TOT[4:8]) + jnp.log(TOT[0:4])
    kl_out[...] = KL[pl.ds(a, 1)]

    flush()
    for k, i, c_ in owners:
        if i == 0 and c_ == 0:
            home = at_home if k == 0 else at_home_hi

            @pl.when(jnp.logical_not(home))
            def _():
                to_owner(k, i, c_).wait_send()
        else:
            to_owner(k, i, c_).wait_send()

    @pl.when(c == 1)
    def _():
        arrived(RZ.at[z], rzs.at[0], rzr.at[z])

    for k in range(1, 8):
        source = lax.rem(z + k, 8)
        arrived(RZ.at[source], rzs.at[0], rzr.at[source])
    total = RZ[0].astype(F32)
    for k in range(1, 8):
        total = total + RZ[k].astype(F32)
    dhid_out[...] = jnp.where(c == 0, total[0:56], total[8:64]).astype(BF16)


def results(kl, dhid, dhead, kl_out, dhid_out, dhead_out, sem):
    copies = [
        pltpu.make_async_copy(dhid, dhid_out, sem.at[7]),
        pltpu.make_async_copy(kl, kl_out, sem.at[8]),
    ]
    for n in range(7):
        at = pl.ds(n * 512, 512)
        copies.append(pltpu.make_async_copy(dhead.at[:, at], dhead_out.at[:, at], sem.at[n]))
    for copy in copies:
        copy.start()
    for copy in copies:
        copy.wait()


def on_device(hidden, valid_mask, student_head, teacher_logits):
    vm = pltpu.VMEM
    dma = pltpu.SemaphoreType.DMA
    any_spec = pl.BlockSpec(memory_space=pl.ANY)
    vmem_spec = pl.BlockSpec(memory_space=pltpu.VMEM)
    kl, dhid, dhead = pl.pallas_call(
        kernel,
        out_shape=(vm((1, ROWS), F32), vm((56, ROWS), BF16), vm((SLAB, D), BF16)),
        in_specs=[any_spec, vmem_spec, any_spec, any_spec],
        out_specs=(vmem_spec, vmem_spec, vmem_spec),
        scratch_shapes=[
            vm((512, D), BF16),
            vm((2 * VP, D), BF16),
            vm((2, 4, 4, CHIPCOL, 2 * VP), BF16),
            vm((256, 256), BF16),
            vm((3000, ROWS), BF16),
            vm((4, VP, ROWS), BF16),
            vm((4, VP, ROWS), BF16),
            vm((VP, ROWS), BF16),
            vm((2, VP, ROWS), BF16),
            vm((2 * VP, HALF), F32),
            vm((2 * VP, HALF), F32),
            vm((2 * VP, HALF), BF16),
            vm((VP, 512), BF16),
            vm((16, 128), F32),
            vm((16, 16, 128), F32),
            vm((16, 128), F32),
            vm((16, 16, 128), F32),
            vm((16, 128), F32),
            vm((8, 128), F32),
            vm((8, 128), F32),
            vm((8, 128), F32),
            vm((16, 8, 128), F32),
            vm((8, 128), F32),
            vm((16, 8, 128), F32),
            vm((8, 128), F32),
            vm((2, 4, CHIPCOL, HALF), F32),
            vm((2, 4, CHIPCOL, HALF), F32),
            vm((4, 4, CHIPCOL, HALF), BF16),
            vm((6, 4, CHIPCOL, HALF), BF16),
            vm((2, 4, CHIPCOL, HALF), BF16),
            vm((2, 4, CHIPCOL, HALF), BF16),
            vm((2, 3, CHIPCOL, HALF), BF16),
            vm((2, 2, 2, 64, 128), BF16),
            vm((8, 64, 128), BF16),
            dma((4,)),
            dma((2,)), dma((2,)),
            dma((2,)), dma((2,)),
            dma((2, 3)), dma((2, 3)), dma((2, 6)), dma((2, 6)),
            dma((2,)), dma((2,)),
            dma((6,)), dma((6,)),
            dma((1,)), dma((1,)),
            dma((15,)), dma((15,)), dma((15,)), dma((15,)),
            dma((15,)), dma((15,)), dma((15,)), dma((15,)),
            dma((4,)), dma((4,)), dma((2, 4)), dma((2, 4)), dma((6,)), dma((6,)),
            dma((8,)), dma((8,)),
        ],
        compiler_params=pltpu.CompilerParams(
            collective_id=0, has_side_effects=True, vmem_limit_bytes=50 * 1024 * 1024
        ),
        cost_estimate=pl.CostEstimate(flops=3 * 2 * 512 * 750 * 3584, bytes_accessed=13_000_000, transcendentals=0),
    )(hidden, valid_mask.reshape(1, ROWS), student_head, teacher_logits.T)
    kl, dhid, dhead = pl.pallas_call(
        results,
        out_shape=(
            jax.ShapeDtypeStruct((1, ROWS), F32),
            jax.ShapeDtypeStruct((56, ROWS), BF16),
            jax.ShapeDtypeStruct((SLAB, D), BF16),
        ),
        in_specs=[any_spec] * 3,
        out_specs=(any_spec,) * 3,
        scratch_shapes=[dma((9,))],
        compiler_params=pltpu.CompilerParams(vmem_limit_bytes=1024 * 1024),
    )(kl, dhid, dhead)
    return kl.reshape(ROWS), dhid.T, dhead


def solution(mesh):
    return jax.shard_map(
        on_device,
        mesh=mesh,
        in_specs=(P("tok", None), P("tok"), P(("voc", "tok"), None), P("tok", "voc")),
        out_specs=(P("tok"), P("tok", "voc"), P(("voc", "tok"), None)),
        check_vma=False,
    )
```

```python
import jax
import jax.numpy as jnp
from jax import lax
from jax.experimental import pallas as pl
from jax.experimental.pallas import tpu as pltpu
from jax.sharding import PartitionSpec as P

CAP = 30.0
D = 3584
ROWS = 128
HALF = 256
SLAB = 750
VP = 768
QCOL = D // 4
PIECE = ROWS // 4
CHIPCOL = 112
FAR_FIRST = (8, 10, 6, 9, 7, 11, 5, 12, 4, 2, 14, 13, 3, 15, 1)
MESH = pl.DeviceIdType.MESH
F32 = jnp.float32
BF16 = jnp.bfloat16


def kernel(
    hid, mask, head, teach, kl_out, dhid_out, DH,
    H, HD, HDT, EYE, tin, TS, TR, RLY, TSIB, CP, ES, GV, GTD,
    TT, TG1, TT2, TG2, TOT, AL, BE, CR, CG1, CR2, CG2, KL,
    OWN, NEXT, B1, R1, F1, B2, R2, B3, RZ,
    local, hs, hr, zs, zr, p1s, p1r, p2s, p2r, cs, cr, ts, tr, gs, gr,
    as1, ar1, as2, ar2, bs1, br1, bs2, br2, q1s, q1r, f1s, f1r, q2s, q2r, rzs, rzr,
):
    a = lax.axis_index("tok")
    v = lax.axis_index("voc")
    c = lax.rem(v, 2)
    x = lax.rem(v // 2, 4)
    y = lax.rem(v // 8, 4)
    zl = v // 32
    z = 2 * a + zl
    p = jnp.where(c == 0, x, y)
    q = jnp.where(c == 0, y, x)

    def dev(a_, zl_, y_, x_, c_):
        return (a_, zl_ * 32 + y_ * 8 + x_ * 2 + c_)

    def at_p(p_):
        return dev(a, zl, jnp.where(c == 0, y, p_), jnp.where(c == 0, p_, x), c)

    def at_q(q_):
        return dev(a, zl, jnp.where(c == 0, q_, y), jnp.where(c == 0, x, q_), c)

    sib = dev(a, zl, y, x, 1 - c)

    def at_a(a_):
        return dev(a_, zl, y, x, c)

    def at_xy(k):
        return dev(a, zl, k // 4, lax.rem(k, 4), c)

    def at_zc(k):
        return dev(k // 4, lax.rem(k // 2, 2), y, x, lax.rem(k, 2))

    def mod4(k):
        return lax.rem(k + 8, 4)

    me_xy = y * 4 + x
    me_zc = z * 2 + c

    pending = []

    def send(src, dst, ssem, rsem, to):
        copy = pltpu.make_async_remote_copy(
            src_ref=src, dst_ref=dst, send_sem=ssem, recv_sem=rsem, device_id=to, device_id_type=MESH
        )
        copy.start()
        pending.append(copy)

    def arrived(dst, ssem, rsem):
        pltpu.make_async_remote_copy(
            src_ref=dst, dst_ref=dst, send_sem=ssem, recv_sem=rsem, device_id=sib, device_id_type=MESH
        ).wait_recv()

    barrier = pltpu.get_barrier_semaphore()
    for k in FAR_FIRST:
        pl.semaphore_signal(barrier, inc=1, device_id=at_zc(lax.rem(me_zc + k, 16)), device_id_type=MESH)
    for k in range(1, 16):
        pl.semaphore_signal(barrier, inc=1, device_id=at_xy(lax.rem(me_xy + k, 16)), device_id_type=MESH)

    load_teach = pltpu.make_async_copy(teach, tin, local.at[0])
    load_teach.start()
    load_hid = pltpu.make_async_copy(hid, H.at[pl.ds(0, ROWS)], local.at[1])
    load_hid.start()

    pl.semaphore_wait(barrier, 30)

    def span(start, size):
        return pl.ds(pl.multiple_of(start, 16), size)

    def cols(q_):
        return pl.ds(pl.multiple_of(q_ * QCOL, 128), QCOL)

    def base(g):
        return ROWS + c * ROWS + g * ROWS

    later = []

    def flush():
        for copy in pending:
            copy.wait_send()
        pending.clear()

        @pl.when(c == 1)
        def _():
            for make in later:
                make().wait_send()

        later.clear()

    def each_group(step):
        step(0)

        @pl.when(c == 1)
        def _():
            step(1)

    def send_group(g, make):
        copy = make(g)
        copy.start()
        if g == 0:
            pending.append(copy)
        else:
            later.append(lambda: make(1))

    def remote(src, dst, ssem, rsem, to):
        return pltpu.make_async_remote_copy(
            src_ref=src, dst_ref=dst, send_sem=ssem, recv_sem=rsem, device_id=to, device_id_type=MESH
        )

    each_group(lambda g: send_group(g, lambda g: remote(
        hid.at[span(p * PIECE, PIECE), cols(q)], H.at[span(base(g) + p * PIECE, PIECE), cols(q)],
        zs.at[g], zr.at[g],
        dev(mod4(a - 1 - c - g), jnp.where((c == 1) & (g == 0), 1 - zl, zl), y, x, c),
    )))

    load_head = pltpu.make_async_copy(head.at[pl.ds(0, 736)], HD.at[0:736], local.at[2])
    load_head.start()
    send(head.at[pl.ds(0, 736)], HD.at[VP : VP + 736], hs.at[0], hr.at[0], sib)
    load_tail = pltpu.make_async_copy(head, DH, local.at[3])
    load_tail.start()

    load_teach.wait()
    place = lax.broadcasted_iota(jnp.int32, (VP, ROWS), 0)
    for t in range(4):
        start = t * SLAB // 16 * 16
        off = t * SLAB - start
        height = min(VP + 16, 3000 - start)
        tall = tin[start : start + height].astype(F32)
        if height < VP + 16:
            tall = jnp.concatenate([tall, jnp.zeros((VP + 16 - height, ROWS), F32)], axis=0)
        if off:
            tall = pltpu.roll(tall, VP + 16 - off, 0)
        part = jnp.where(place < SLAB, tall[:VP], -30000.0)
        TS[t] = part.astype(BF16)
    way = jnp.where(c == 0, 1, 3)
    send(TS.at[mod4(a + 2)], RLY, ts.at[2], tr.at[2], at_a(mod4(a + way)))
    TR[0] = TS[a]

    nt = (((1,), (1,)), ((), ()))
    EYE[...] = jnp.where(
        lax.broadcasted_iota(jnp.int32, (256, 256), 0) == lax.broadcasted_iota(jnp.int32, (256, 256), 1), 1.0, 0.0
    ).astype(BF16)

    def turn(slab, half):
        for n in range(7):
            at = pl.ds(half * 1792 + n * 256, 256)
            out = lax.dot_general(
                EYE[...], HD[slab * VP : (slab + 1) * VP, at], nt, preferred_element_type=F32
            ).astype(BF16)
            done = 0
            while done < 256:
                chip, row = divmod(n * 256 + done, CHIPCOL)
                size = min(CHIPCOL - row, 256 - done)
                p_, q_ = jnp.where(c == 0, chip % 4, chip // 4), jnp.where(c == 0, chip // 4, chip % 4)
                HDT[half, p_, q_, row : row + size, slab * VP : (slab + 1) * VP] = out[done : done + size]
                done += size

    def piece(g, p_):
        return H.at[span(base(g) + p_ * PIECE, PIECE), cols(q)]

    def first_step(g):
        arrived(piece(g, p), zs.at[g], zr.at[g])
        for d in (2, 1, 3):
            send_group(g, lambda g, d=d: remote(
                piece(g, p), piece(g, p), p1s.at[g, d - 1], p1r.at[g, d - 1], at_p(mod4(p + d)),
            ))

    each_group(first_step)

    TT[...] = jnp.zeros_like(TT)
    teacher_sum = jnp.zeros((1, ROWS), F32)
    for t in range(4):
        teacher_sum = teacher_sum + jnp.sum(jnp.exp(TS[t].astype(F32)), axis=0, keepdims=True)
    TT[pl.ds(4 + a, 1)] = teacher_sum
    TT[pl.ds(8 + a, 1)] = mask[...].astype(F32)

    load_tail.wait()
    HD[736:768] = jnp.concatenate([DH[736:750].astype(F32), jnp.zeros((18, D), F32)], axis=0).astype(BF16)
    send(HD.at[736:768], HD.at[VP + 736 : VP + 768], hs.at[1], hr.at[1], sib)
    load_head.wait()
    turn(0, 0)

    def first_end(g):
        for d in range(1, 4):
            arrived(piece(g, mod4(p - d)), p1s.at[g, d - 1], p1r.at[g, d - 1])

    right, left = at_q(mod4(q + 1)), at_q(mod4(q - 1))
    before, after, across = mod4(q - 1), mod4(q + 1), mod4(q + 2)

    def part_of(g, half, q_):
        return H.at[span(base(g) + half * 64, 64), cols(q_)]

    def pass_on(g, n, half, q_, to):
        send_group(g, lambda g: remote(part_of(g, half, q_), part_of(g, half, q_), p2s.at[g, n], p2r.at[g, n], to))

    def passed(n, half, q_):
        each_group(lambda g: arrived(part_of(g, half, q_), p2s.at[g, n], p2r.at[g, n]))

    def second_step(g):
        first_end(g)
        pass_on(g, 0, 0, q, right)
        pass_on(g, 1, 1, q, left)
        pass_on(g, 2, 1, q, right)
        pass_on(g, 3, 0, q, left)

    def relay_step(g):
        arrived(part_of(g, 0, before), p2s.at[g, 0], p2r.at[g, 0])
        pass_on(g, 4, 0, before, right)
        arrived(part_of(g, 1, after), p2s.at[g, 1], p2r.at[g, 1])
        pass_on(g, 5, 1, after, left)

    each_group(second_step)
    send(TS.at[mod4(a + 1)], TR.at[3], ts.at[0], tr.at[0], at_a(mod4(a + 1)))
    send(TS.at[mod4(a + 3)], TR.at[1], ts.at[1], tr.at[1], at_a(mod4(a + 3)))

    my_half = pl.ds(pl.multiple_of(c * HALF, HALF), HALF)

    def logits(slab, q_, first=False):
        rr = slice(slab * VP, (slab + 1) * VP)
        out = lax.dot_general(HD[rr, cols(q_)], H[my_half, cols(q_)], nt, preferred_element_type=F32)
        CP[rr] = out if first else CP[rr] + out

    load_hid.wait()
    logits(0, q, True)
    turn(0, 1)
    each_group(relay_step)

    arrived(RLY, ts.at[2], tr.at[2])
    send(RLY, TR.at[2], ts.at[3], tr.at[3], at_a(mod4(a + way)))
    passed(2, 1, before)
    logits(0, before)
    passed(3, 0, after)
    logits(0, after)
    arrived(HD.at[VP : VP + 736], hs.at[0], hr.at[0])
    arrived(HD.at[VP + 736 : VP + 768], hs.at[1], hr.at[1])
    logits(1, q, True)
    logits(1, before)
    logits(1, after)
    passed(4, 0, across)
    passed(5, 1, across)
    in_slab = lax.broadcasted_iota(jnp.int32, (256, HALF), 0) < SLAB - 512

    def exponentials(slab, student_sum):
        for k in range(3):
            rr = slice(slab * VP + k * 256, slab * VP + (k + 1) * 256)
            capped = CAP * jnp.tanh(CP[rr] * (1.0 / CAP))
            exps = jnp.exp(capped)
            if k == 2:
                exps = jnp.where(in_slab, exps, 0.0)
            CP[rr] = capped
            ES[rr] = exps
            student_sum = student_sum + jnp.sum(exps, axis=0, keepdims=True)
        return student_sum

    logits(0, across)
    logits(1, across)
    student_sum = exponentials(0, jnp.zeros((1, HALF), F32))
    student_sum = exponentials(1, student_sum)
    my_rows = (mod4(a + 2 * c), mod4(a + 2 * c + 1))
    for i in range(2):
        TT[pl.ds(my_rows[i], 1)] = student_sum[:, i * 128 : (i + 1) * 128]

    def exchange_start(tile, slots, ssem, rsem, me, at):
        for k in FAR_FIRST:
            send(tile, slots.at[me], ssem.at[k - 1], rsem.at[k - 1], at(lax.rem(me + k, 16)))

    def exchange_end(tile, slots, ssem, rsem, me):
        slots[me] = tile[...]
        for k in range(1, 16):
            arrived(slots.at[lax.rem(me + 16 - k, 16)], ssem.at[k - 1], rsem.at[k - 1])
        total = slots[0]
        for k in range(1, 16):
            total = total + slots[k]
        return total

    gathered = list(pending), list(later)
    pending.clear()
    later.clear()
    exchange_start(TT, TG1, as1, ar1, me_xy, at_xy)

    def factors(slab, cross_sum):
        for k in range(6):
            rr = slice(slab * VP + k * 128, slab * VP + (k + 1) * 128)
            vv = slice(k * 128, (k + 1) * 128)
            if slab == 0:
                target = jnp.concatenate([TR[2 * c, vv], TR[2 * c + 1, vv]], axis=1).astype(F32)
            else:
                target = jnp.concatenate([TSIB[0, vv], TSIB[1, vv]], axis=1).astype(F32)
            expd = jnp.exp(target)
            capped = CP[rr]
            cross_sum = cross_sum + jnp.sum(expd * (target - capped), axis=0, keepdims=True)
            ratio = capped * (1.0 / CAP)
            slope = 1.0 - ratio * ratio
            ES[rr] = ES[rr] * slope
            CP[rr] = expd * slope
        return cross_sum

    for copy in gathered[0]:
        copy.wait_send()

    @pl.when(c == 1)
    def _():
        for make in gathered[1]:
            make().wait_send()

    turn(1, 0)

    def give(i):
        send(TR.at[2 * (1 - c) + i], TSIB.at[i], ts.at[4 + i], tr.at[4 + i], sib)

    arrived(TR.at[3], ts.at[0], tr.at[0])
    arrived(TR.at[1], ts.at[1], tr.at[1])
    give(1)
    TT2[...] = exchange_end(TT, TG1, as1, ar1, me_xy)
    exchange_start(TT2, TG2, as2, ar2, me_zc, at_zc)
    arrived(TR.at[2], ts.at[3], tr.at[3])
    give(0)
    cross_sum = factors(0, jnp.zeros((1, HALF), F32))
    turn(1, 1)
    for i in range(2):
        arrived(TSIB.at[i], ts.at[4 + i], tr.at[4 + i])
    cross_sum = factors(1, cross_sum)
    TOT[...] = exchange_end(TT2, TG2, as2, ar2, me_zc)

    valid = TOT[8:12] * (1.0 / 64.0)
    weight = valid * (512.0 / jnp.sum(valid))
    AL[0:4] = weight / TOT[0:4]
    BE[0:4] = weight / TOT[4:8]
    alpha = jnp.concatenate([AL[pl.ds(r, 1)] for r in my_rows], axis=1)
    beta = jnp.concatenate([BE[pl.ds(r, 1)] for r in my_rows], axis=1)
    for k in range(12):
        rr = slice(k * 128, (k + 1) * 128)
        grad = (ES[rr] * alpha - CP[rr] * beta).astype(BF16)
        GV[rr] = grad
        if k < 6:
            GTD[rr, my_half] = grad

    up, down, far = mod4(p + 1), mod4(p - 1), mod4(p + 2)

    def partial(n, p_):
        rows = HDT[n, p_].reshape(4 * CHIPCOL, 2 * VP)
        return jnp.dot(rows, GV[...], preferred_element_type=F32)

    def put(ref, n, block):
        for i in range(4):
            ref[n, i] = block[i * CHIPCOL : (i + 1) * CHIPCOL].astype(ref.dtype)

    put(B1, 0, partial(0, far))
    send(B1.at[0], R1.at[0], q1s.at[0], q1r.at[0], at_p(up))
    put(B1, 1, partial(1, far))
    send(B1.at[1], R1.at[1], q1s.at[1], q1r.at[1], at_p(down))
    put(B1, 2, partial(1, up))
    send(B1.at[2], R1.at[2], q1s.at[2], q1r.at[2], at_p(up))
    put(B1, 3, partial(0, down))
    send(B1.at[3], R1.at[3], q1s.at[3], q1r.at[3], at_p(down))
    send(GV.at[VP : 2 * VP], GTD.at[:, my_half], gs.at[0], gr.at[0], sib)

    def share(g):
        return H.at[span(base(g), ROWS)]

    each_group(lambda g: send_group(g, lambda g: remote(share(g), share(g), cs.at[g], cr.at[g], sib)))


    def head_chunk(n):
        at = pl.ds(pl.multiple_of(n * 512, 512), 512)
        out = jnp.dot(GTD[...], H[:, at], preferred_element_type=F32)
        DH[:, at] = out[:SLAB].astype(BF16)

    def head_chunks(first, last):
        @pl.loop(first, last)
        def _(n):
            head_chunk(n)

    qup, qdown, qfar = mod4(q + 1), mod4(q - 1), mod4(q + 2)
    order = (qfar, qup, qdown, q)

    def relay(k):
        arrived(R1.at[k], q1s.at[k], q1r.at[k])
        near = up if k == 0 else down
        for n, i in enumerate(order):
            F1[k, i] = (NEXT[k, i] + R1[k, i].astype(F32)).astype(BF16)
            send(F1.at[k, i], R1.at[4 + k, i], f1s.at[k, n], f1r.at[k, n], at_p(near))

    def second(k, n):
        i = order[n]
        arrived(R1.at[4 + k, i], f1s.at[k, n], f1r.at[k, n])
        total = OWN[k, i] + R1[3 - k, i].astype(F32) + R1[4 + k, i].astype(F32)
        if n == 3:
            OWN[k, i] = total
        else:
            B2[k, i] = total.astype(BF16)
            send(B2.at[k, i], R2.at[k, n], q2s.at[k * 3 + n], q2r.at[k * 3 + n], at_q(i))

    put(NEXT, 0, partial(0, up))
    relay(0)
    put(NEXT, 1, partial(1, down))
    relay(1)

    CR[...] = jnp.zeros_like(CR)
    for i in range(2):
        CR[pl.ds(my_rows[i], 1)] = cross_sum[:, i * 128 : (i + 1) * 128]
    exchange_start(CR, CG1, bs1, br1, me_xy, at_xy)

    put(OWN, 0, partial(0, p))
    put(OWN, 1, partial(1, p))
    arrived(GTD.at[:, pl.ds(pl.multiple_of((1 - c) * HALF, HALF), HALF)], gs.at[0], gr.at[0])
    arrived(H.at[span(ROWS + (1 - c) * ROWS, ROWS)], cs.at[0], cr.at[0])

    @pl.when(c == 0)
    def _():
        arrived(H.at[3 * ROWS : 4 * ROWS], cs.at[1], cr.at[1])

    head_chunks(0, 2)
    arrived(R1.at[3], q1s.at[3], q1r.at[3])
    arrived(R1.at[2], q1s.at[2], q1r.at[2])
    for n in range(4):
        for k in range(2):
            second(k, n)
    CR2[...] = exchange_end(CR, CG1, bs1, br1, me_xy)
    exchange_start(CR2, CG2, bs2, br2, me_zc, at_zc)
    head_chunks(2, 4)

    at_home = (c == 0) & (zl == 0)
    at_home_hi = (c == 0) & (zl == 1)

    def to_owner(k, i, c_):
        n = k * 4 + i * 2 + c_
        return pltpu.make_async_remote_copy(
            src_ref=B3.at[k, i, c_], dst_ref=RZ.at[z], send_sem=rzs.at[n], recv_sem=rzr.at[z],
            device_id=dev(mod4(a + 2 * c + i), k, y, x, c_), device_id_type=MESH,
        )

    owners = [(k, i, c_) for k in range(2) for i in range(2) for c_ in range(2)]
    for k in range(2):
        total = OWN[k, q]
        for n in range(3):
            arrived(R2.at[k, n], q2s.at[k * 3 + n], q2r.at[k * 3 + n])
            total = total + R2[k, n].astype(F32)
        for i in range(2):
            for c_ in range(2):
                B3[k, i, c_] = total[48 * c_ : 48 * c_ + 64, i * 128 : (i + 1) * 128].astype(BF16)
                if i == 0 and c_ == 0:
                    home = at_home if k == 0 else at_home_hi

                    @pl.when(jnp.logical_not(home))
                    def _():
                        to_owner(k, i, c_).start()

                    @pl.when(home)
                    def _():
                        RZ[z] = B3[k, 0, 0]
                else:
                    to_owner(k, i, c_).start()

    head_chunks(4, 7)
    cross = exchange_end(CR2, CG2, bs2, br2, me_zc)
    KL[0:4] = cross[0:4] / TOT[4:8] - jnp.log(TOT[4:8]) + jnp.log(TOT[0:4])
    kl_out[...] = KL[pl.ds(a, 1)]

    flush()
    for k, i, c_ in owners:
        if i == 0 and c_ == 0:
            home = at_home if k == 0 else at_home_hi

            @pl.when(jnp.logical_not(home))
            def _():
                to_owner(k, i, c_).wait_send()
        else:
            to_owner(k, i, c_).wait_send()

    @pl.when(c == 1)
    def _():
        arrived(RZ.at[z], rzs.at[0], rzr.at[z])

    for k in range(1, 8):
        source = lax.rem(z + k, 8)
        arrived(RZ.at[source], rzs.at[0], rzr.at[source])
    total = RZ[0].astype(F32)
    for k in range(1, 8):
        total = total + RZ[k].astype(F32)
    dhid_out[...] = jnp.where(c == 0, total[0:56], total[8:64]).astype(BF16)


def results(kl, dhid, dhead, kl_out, dhid_out, dhead_out, sem):
    copies = [
        pltpu.make_async_copy(dhid, dhid_out, sem.at[7]),
        pltpu.make_async_copy(kl, kl_out, sem.at[8]),
    ]
    for n in range(7):
        at = pl.ds(n * 512, 512)
        copies.append(pltpu.make_async_copy(dhead.at[:, at], dhead_out.at[:, at], sem.at[n]))
    for copy in copies:
        copy.start()
    for copy in copies:
        copy.wait()


def on_device(hidden, valid_mask, student_head, teacher_logits):
    vm = pltpu.VMEM
    dma = pltpu.SemaphoreType.DMA
    any_spec = pl.BlockSpec(memory_space=pl.ANY)
    vmem_spec = pl.BlockSpec(memory_space=pltpu.VMEM)
    kl, dhid, dhead = pl.pallas_call(
        kernel,
        out_shape=(vm((1, ROWS), F32), vm((56, ROWS), BF16), vm((SLAB, D), BF16)),
        in_specs=[any_spec, vmem_spec, any_spec, any_spec],
        out_specs=(vmem_spec, vmem_spec, vmem_spec),
        scratch_shapes=[
            vm((512, D), BF16),
            vm((2 * VP, D), BF16),
            vm((2, 4, 4, CHIPCOL, 2 * VP), BF16),
            vm((256, 256), BF16),
            vm((3000, ROWS), BF16),
            vm((4, VP, ROWS), BF16),
            vm((4, VP, ROWS), BF16),
            vm((VP, ROWS), BF16),
            vm((2, VP, ROWS), BF16),
            vm((2 * VP, HALF), F32),
            vm((2 * VP, HALF), F32),
            vm((2 * VP, HALF), BF16),
            vm((VP, 512), BF16),
            vm((16, 128), F32),
            vm((16, 16, 128), F32),
            vm((16, 128), F32),
            vm((16, 16, 128), F32),
            vm((16, 128), F32),
            vm((8, 128), F32),
            vm((8, 128), F32),
            vm((8, 128), F32),
            vm((16, 8, 128), F32),
            vm((8, 128), F32),
            vm((16, 8, 128), F32),
            vm((8, 128), F32),
            vm((2, 4, CHIPCOL, HALF), F32),
            vm((2, 4, CHIPCOL, HALF), F32),
            vm((4, 4, CHIPCOL, HALF), BF16),
            vm((6, 4, CHIPCOL, HALF), BF16),
            vm((2, 4, CHIPCOL, HALF), BF16),
            vm((2, 4, CHIPCOL, HALF), BF16),
            vm((2, 3, CHIPCOL, HALF), BF16),
            vm((2, 2, 2, 64, 128), BF16),
            vm((8, 64, 128), BF16),
            dma((4,)),
            dma((2,)), dma((2,)),
            dma((2,)), dma((2,)),
            dma((2, 3)), dma((2, 3)), dma((2, 6)), dma((2, 6)),
            dma((2,)), dma((2,)),
            dma((6,)), dma((6,)),
            dma((1,)), dma((1,)),
            dma((15,)), dma((15,)), dma((15,)), dma((15,)),
            dma((15,)), dma((15,)), dma((15,)), dma((15,)),
            dma((4,)), dma((4,)), dma((2, 4)), dma((2, 4)), dma((6,)), dma((6,)),
            dma((8,)), dma((8,)),
        ],
        compiler_params=pltpu.CompilerParams(
            collective_id=0, has_side_effects=True, vmem_limit_bytes=50 * 1024 * 1024
        ),
        cost_estimate=pl.CostEstimate(flops=3 * 2 * 512 * 750 * 3584, bytes_accessed=13_000_000, transcendentals=0),
    )(hidden, valid_mask.reshape(1, ROWS), student_head, teacher_logits.T)
    kl, dhid, dhead = pl.pallas_call(
        results,
        out_shape=(
            jax.ShapeDtypeStruct((1, ROWS), F32),
            jax.ShapeDtypeStruct((56, ROWS), BF16),
            jax.ShapeDtypeStruct((SLAB, D), BF16),
        ),
        in_specs=[any_spec] * 3,
        out_specs=(any_spec,) * 3,
        scratch_shapes=[dma((9,))],
        compiler_params=pltpu.CompilerParams(vmem_limit_bytes=1024 * 1024),
    )(kl, dhid, dhead)
    return kl.reshape(ROWS), dhid.T, dhead


def solution(mesh):
    return jax.shard_map(
        on_device,
        mesh=mesh,
        in_specs=(P("tok", None), P("tok"), P(("voc", "tok"), None), P("tok", "voc")),
        out_specs=(P("tok"), P("tok", "voc"), P(("voc", "tok"), None)),
        check_vma=False,
    )
```

```python
import jax
import jax.numpy as jnp
from jax import lax
from jax.experimental import pallas as pl
from jax.experimental.pallas import tpu as pltpu
from jax.sharding import PartitionSpec as P

CAP = 30.0
D = 3584
ROWS = 128
HALF = 256
SLAB = 750
VP = 768
QCOL = D // 4
PIECE = ROWS // 4
CHIPCOL = 112
FAR_FIRST = (8, 10, 6, 9, 7, 11, 5, 12, 4, 2, 14, 13, 3, 15, 1)
MESH = pl.DeviceIdType.MESH
F32 = jnp.float32
BF16 = jnp.bfloat16


def kernel(
    hid, mask, head, teach, kl_out, dhid_out, DH,
    H, HD, HDT, EYE, tin, TS, TR, RLY, TSIB, CP, ES, GV, GTD,
    TT, TG1, TT2, TG2, TOT, AL, BE, CR, CG1, CR2, CG2, KL,
    OWN, NEXT, B1, R1, F1, B2, R2, B3, RZ,
    local, hs, hr, zs, zr, p1s, p1r, p2s, p2r, cs, cr, ts, tr, gs, gr,
    as1, ar1, as2, ar2, bs1, br1, bs2, br2, q1s, q1r, f1s, f1r, q2s, q2r, rzs, rzr,
):
    a = lax.axis_index("tok")
    v = lax.axis_index("voc")
    c = lax.rem(v, 2)
    x = lax.rem(v // 2, 4)
    y = lax.rem(v // 8, 4)
    zl = v // 32
    z = 2 * a + zl
    p = jnp.where(c == 0, x, y)
    q = jnp.where(c == 0, y, x)

    def dev(a_, zl_, y_, x_, c_):
        return (a_, zl_ * 32 + y_ * 8 + x_ * 2 + c_)

    def at_p(p_):
        return dev(a, zl, jnp.where(c == 0, y, p_), jnp.where(c == 0, p_, x), c)

    def at_q(q_):
        return dev(a, zl, jnp.where(c == 0, q_, y), jnp.where(c == 0, x, q_), c)

    sib = dev(a, zl, y, x, 1 - c)

    def at_a(a_):
        return dev(a_, zl, y, x, c)

    def at_xy(k):
        return dev(a, zl, k // 4, lax.rem(k, 4), c)

    def at_zc(k):
        return dev(k // 4, lax.rem(k // 2, 2), y, x, lax.rem(k, 2))

    def mod4(k):
        return lax.rem(k + 8, 4)

    me_xy = y * 4 + x
    me_zc = z * 2 + c

    pending = []

    def send(src, dst, ssem, rsem, to):
        copy = pltpu.make_async_remote_copy(
            src_ref=src, dst_ref=dst, send_sem=ssem, recv_sem=rsem, device_id=to, device_id_type=MESH
        )
        copy.start()
        pending.append(copy)

    def arrived(dst, ssem, rsem):
        pltpu.make_async_remote_copy(
            src_ref=dst, dst_ref=dst, send_sem=ssem, recv_sem=rsem, device_id=sib, device_id_type=MESH
        ).wait_recv()

    barrier = pltpu.get_barrier_semaphore()
    for k in FAR_FIRST:
        pl.semaphore_signal(barrier, inc=1, device_id=at_zc(lax.rem(me_zc + k, 16)), device_id_type=MESH)
    for k in range(1, 16):
        pl.semaphore_signal(barrier, inc=1, device_id=at_xy(lax.rem(me_xy + k, 16)), device_id_type=MESH)

    load_teach = pltpu.make_async_copy(teach, tin, local.at[0])
    load_teach.start()
    load_hid = pltpu.make_async_copy(hid, H.at[pl.ds(0, ROWS)], local.at[1])
    load_hid.start()

    pl.semaphore_wait(barrier, 30)

    def span(start, size):
        return pl.ds(pl.multiple_of(start, 16), size)

    def cols(q_):
        return pl.ds(pl.multiple_of(q_ * QCOL, 128), QCOL)

    def base(g):
        return ROWS + c * ROWS + g * ROWS

    later = []

    def flush():
        for copy in pending:
            copy.wait_send()
        pending.clear()

        @pl.when(c == 1)
        def _():
            for make in later:
                make().wait_send()

        later.clear()

    def each_group(step):
        step(0)

        @pl.when(c == 1)
        def _():
            step(1)

    def send_group(g, make):
        copy = make(g)
        copy.start()
        if g == 0:
            pending.append(copy)
        else:
            later.append(lambda: make(1))

    def remote(src, dst, ssem, rsem, to):
        return pltpu.make_async_remote_copy(
            src_ref=src, dst_ref=dst, send_sem=ssem, recv_sem=rsem, device_id=to, device_id_type=MESH
        )

    each_group(lambda g: send_group(g, lambda g: remote(
        hid.at[span(p * PIECE, PIECE), cols(q)], H.at[span(base(g) + p * PIECE, PIECE), cols(q)],
        zs.at[g], zr.at[g],
        dev(mod4(a - 1 - c - g), jnp.where((c == 1) & (g == 0), 1 - zl, zl), y, x, c),
    )))

    load_head = pltpu.make_async_copy(head.at[pl.ds(0, 736)], HD.at[0:736], local.at[2])
    load_head.start()
    send(head.at[pl.ds(0, 736)], HD.at[VP : VP + 736], hs.at[0], hr.at[0], sib)
    load_tail = pltpu.make_async_copy(head, DH, local.at[3])
    load_tail.start()

    load_teach.wait()
    place = lax.broadcasted_iota(jnp.int32, (VP, ROWS), 0)
    for t in range(4):
        start = t * SLAB // 16 * 16
        off = t * SLAB - start
        height = min(VP + 16, 3000 - start)
        tall = tin[start : start + height].astype(F32)
        if height < VP + 16:
            tall = jnp.concatenate([tall, jnp.zeros((VP + 16 - height, ROWS), F32)], axis=0)
        if off:
            tall = pltpu.roll(tall, VP + 16 - off, 0)
        part = jnp.where(place < SLAB, tall[:VP], -30000.0)
        TS[t] = part.astype(BF16)
    way = jnp.where(c == 0, 1, 3)
    send(TS.at[mod4(a + 2)], RLY, ts.at[2], tr.at[2], at_a(mod4(a + way)))
    TR[0] = TS[a]

    nt = (((1,), (1,)), ((), ()))
    EYE[...] = jnp.where(
        lax.broadcasted_iota(jnp.int32, (256, 256), 0) == lax.broadcasted_iota(jnp.int32, (256, 256), 1), 1.0, 0.0
    ).astype(BF16)

    def turn(slab, half):
        for n in range(7):
            at = pl.ds(half * 1792 + n * 256, 256)
            out = lax.dot_general(
                EYE[...], HD[slab * VP : (slab + 1) * VP, at], nt, preferred_element_type=F32
            ).astype(BF16)
            done = 0
            while done < 256:
                chip, row = divmod(n * 256 + done, CHIPCOL)
                size = min(CHIPCOL - row, 256 - done)
                p_, q_ = jnp.where(c == 0, chip % 4, chip // 4), jnp.where(c == 0, chip // 4, chip % 4)
                HDT[half, p_, q_, row : row + size, slab * VP : (slab + 1) * VP] = out[done : done + size]
                done += size

    def piece(g, p_):
        return H.at[span(base(g) + p_ * PIECE, PIECE), cols(q)]

    def first_step(g):
        arrived(piece(g, p), zs.at[g], zr.at[g])
        for d in (2, 1, 3):
            send_group(g, lambda g, d=d: remote(
                piece(g, p), piece(g, p), p1s.at[g, d - 1], p1r.at[g, d - 1], at_p(mod4(p + d)),
            ))

    each_group(first_step)

    TT[...] = jnp.zeros_like(TT)
    teacher_sum = jnp.zeros((1, ROWS), F32)
    for t in range(4):
        teacher_sum = teacher_sum + jnp.sum(jnp.exp(TS[t].astype(F32)), axis=0, keepdims=True)
    TT[pl.ds(4 + a, 1)] = teacher_sum
    TT[pl.ds(8 + a, 1)] = mask[...].astype(F32)

    load_tail.wait()
    HD[736:768] = jnp.concatenate([DH[736:750].astype(F32), jnp.zeros((18, D), F32)], axis=0).astype(BF16)
    send(HD.at[736:768], HD.at[VP + 736 : VP + 768], hs.at[1], hr.at[1], sib)
    load_head.wait()
    turn(0, 0)

    def first_end(g):
        for d in range(1, 4):
            arrived(piece(g, mod4(p - d)), p1s.at[g, d - 1], p1r.at[g, d - 1])

    right, left = at_q(mod4(q + 1)), at_q(mod4(q - 1))
    before, after, across = mod4(q - 1), mod4(q + 1), mod4(q + 2)

    def part_of(g, half, q_):
        return H.at[span(base(g) + half * 64, 64), cols(q_)]

    def pass_on(g, n, half, q_, to):
        send_group(g, lambda g: remote(part_of(g, half, q_), part_of(g, half, q_), p2s.at[g, n], p2r.at[g, n], to))

    def passed(n, half, q_):
        each_group(lambda g: arrived(part_of(g, half, q_), p2s.at[g, n], p2r.at[g, n]))

    def second_step(g):
        first_end(g)
        pass_on(g, 0, 0, q, right)
        pass_on(g, 1, 1, q, left)
        pass_on(g, 2, 1, q, right)
        pass_on(g, 3, 0, q, left)

    def relay_step(g):
        arrived(part_of(g, 0, before), p2s.at[g, 0], p2r.at[g, 0])
        pass_on(g, 4, 0, before, right)
        arrived(part_of(g, 1, after), p2s.at[g, 1], p2r.at[g, 1])
        pass_on(g, 5, 1, after, left)

    each_group(second_step)
    send(TS.at[mod4(a + 1)], TR.at[3], ts.at[0], tr.at[0], at_a(mod4(a + 1)))
    send(TS.at[mod4(a + 3)], TR.at[1], ts.at[1], tr.at[1], at_a(mod4(a + 3)))

    my_half = pl.ds(pl.multiple_of(c * HALF, HALF), HALF)

    def logits(slab, q_, first=False):
        rr = slice(slab * VP, (slab + 1) * VP)
        out = lax.dot_general(HD[rr, cols(q_)], H[my_half, cols(q_)], nt, preferred_element_type=F32)
        CP[rr] = out if first else CP[rr] + out

    load_hid.wait()
    logits(0, q, True)
    turn(0, 1)
    each_group(relay_step)

    arrived(RLY, ts.at[2], tr.at[2])
    send(RLY, TR.at[2], ts.at[3], tr.at[3], at_a(mod4(a + way)))
    passed(2, 1, before)
    logits(0, before)
    passed(3, 0, after)
    logits(0, after)
    arrived(HD.at[VP : VP + 736], hs.at[0], hr.at[0])
    arrived(HD.at[VP + 736 : VP + 768], hs.at[1], hr.at[1])
    logits(1, q, True)
    logits(1, before)
    logits(1, after)
    passed(4, 0, across)
    passed(5, 1, across)
    in_slab = lax.broadcasted_iota(jnp.int32, (256, HALF), 0) < SLAB - 512

    def exponentials(slab, student_sum):
        for k in range(3):
            rr = slice(slab * VP + k * 256, slab * VP + (k + 1) * 256)
            capped = CAP * jnp.tanh(CP[rr] * (1.0 / CAP))
            exps = jnp.exp(capped)
            if k == 2:
                exps = jnp.where(in_slab, exps, 0.0)
            CP[rr] = capped
            ES[rr] = exps
            student_sum = student_sum + jnp.sum(exps, axis=0, keepdims=True)
        return student_sum

    logits(0, across)
    logits(1, across)
    student_sum = exponentials(0, jnp.zeros((1, HALF), F32))
    student_sum = exponentials(1, student_sum)
    my_rows = (mod4(a + 2 * c), mod4(a + 2 * c + 1))
    for i in range(2):
        TT[pl.ds(my_rows[i], 1)] = student_sum[:, i * 128 : (i + 1) * 128]

    def exchange_start(tile, slots, ssem, rsem, me, at):
        for k in FAR_FIRST:
            send(tile, slots.at[me], ssem.at[k - 1], rsem.at[k - 1], at(lax.rem(me + k, 16)))

    def exchange_end(tile, slots, ssem, rsem, me):
        slots[me] = tile[...]
        for k in range(1, 16):
            arrived(slots.at[lax.rem(me + 16 - k, 16)], ssem.at[k - 1], rsem.at[k - 1])
        total = slots[0]
        for k in range(1, 16):
            total = total + slots[k]
        return total

    gathered = list(pending), list(later)
    pending.clear()
    later.clear()
    exchange_start(TT, TG1, as1, ar1, me_xy, at_xy)

    def factors(slab, cross_sum):
        for k in range(6):
            rr = slice(slab * VP + k * 128, slab * VP + (k + 1) * 128)
            vv = slice(k * 128, (k + 1) * 128)
            if slab == 0:
                target = jnp.concatenate([TR[2 * c, vv], TR[2 * c + 1, vv]], axis=1).astype(F32)
            else:
                target = jnp.concatenate([TSIB[0, vv], TSIB[1, vv]], axis=1).astype(F32)
            expd = jnp.exp(target)
            capped = CP[rr]
            cross_sum = cross_sum + jnp.sum(expd * (target - capped), axis=0, keepdims=True)
            ratio = capped * (1.0 / CAP)
            slope = 1.0 - ratio * ratio
            ES[rr] = ES[rr] * slope
            CP[rr] = expd * slope
        return cross_sum

    for copy in gathered[0]:
        copy.wait_send()

    @pl.when(c == 1)
    def _():
        for make in gathered[1]:
            make().wait_send()

    turn(1, 0)

    def give(i):
        send(TR.at[2 * (1 - c) + i], TSIB.at[i], ts.at[4 + i], tr.at[4 + i], sib)

    arrived(TR.at[3], ts.at[0], tr.at[0])
    arrived(TR.at[1], ts.at[1], tr.at[1])
    give(1)
    TT2[...] = exchange_end(TT, TG1, as1, ar1, me_xy)
    exchange_start(TT2, TG2, as2, ar2, me_zc, at_zc)
    arrived(TR.at[2], ts.at[3], tr.at[3])
    give(0)
    cross_sum = factors(0, jnp.zeros((1, HALF), F32))
    turn(1, 1)
    for i in range(2):
        arrived(TSIB.at[i], ts.at[4 + i], tr.at[4 + i])
    cross_sum = factors(1, cross_sum)
    TOT[...] = exchange_end(TT2, TG2, as2, ar2, me_zc)

    valid = TOT[8:12] * (1.0 / 64.0)
    weight = valid * (512.0 / jnp.sum(valid))
    AL[0:4] = weight / TOT[0:4]
    BE[0:4] = weight / TOT[4:8]
    alpha = jnp.concatenate([AL[pl.ds(r, 1)] for r in my_rows], axis=1)
    beta = jnp.concatenate([BE[pl.ds(r, 1)] for r in my_rows], axis=1)
    for k in range(12):
        rr = slice(k * 128, (k + 1) * 128)
        grad = (ES[rr] * alpha - CP[rr] * beta).astype(BF16)
        GV[rr] = grad
        if k < 6:
            GTD[rr, my_half] = grad

    up, down, far = mod4(p + 1), mod4(p - 1), mod4(p + 2)

    def partial(n, p_):
        rows = HDT[n, p_].reshape(4 * CHIPCOL, 2 * VP)
        return jnp.dot(rows, GV[...], preferred_element_type=F32)

    def put(ref, n, block):
        for i in range(4):
            ref[n, i] = block[i * CHIPCOL : (i + 1) * CHIPCOL].astype(ref.dtype)

    put(B1, 0, partial(0, far))
    send(B1.at[0], R1.at[0], q1s.at[0], q1r.at[0], at_p(up))
    put(B1, 1, partial(1, far))
    send(B1.at[1], R1.at[1], q1s.at[1], q1r.at[1], at_p(down))
    put(B1, 2, partial(1, up))
    send(B1.at[2], R1.at[2], q1s.at[2], q1r.at[2], at_p(up))
    put(B1, 3, partial(0, down))
    send(B1.at[3], R1.at[3], q1s.at[3], q1r.at[3], at_p(down))
    send(GV.at[VP : 2 * VP], GTD.at[:, my_half], gs.at[0], gr.at[0], sib)

    def share(g):
        return H.at[span(base(g), ROWS)]

    each_group(lambda g: send_group(g, lambda g: remote(share(g), share(g), cs.at[g], cr.at[g], sib)))


    def head_chunk(n):
        at = pl.ds(pl.multiple_of(n * 512, 512), 512)
        out = jnp.dot(GTD[...], H[:, at], preferred_element_type=F32)
        DH[:, at] = out[:SLAB].astype(BF16)

    def head_chunks(first, last):
        @pl.loop(first, last)
        def _(n):
            head_chunk(n)

    qup, qdown, qfar = mod4(q + 1), mod4(q - 1), mod4(q + 2)
    order = (qfar, qup, qdown, q)

    def relay(k):
        arrived(R1.at[k], q1s.at[k], q1r.at[k])
        near = up if k == 0 else down
        for n, i in enumerate(order):
            F1[k, i] = (NEXT[k, i] + R1[k, i].astype(F32)).astype(BF16)
            send(F1.at[k, i], R1.at[4 + k, i], f1s.at[k, n], f1r.at[k, n], at_p(near))

    def second(k, n):
        i = order[n]
        arrived(R1.at[4 + k, i], f1s.at[k, n], f1r.at[k, n])
        total = OWN[k, i] + R1[3 - k, i].astype(F32) + R1[4 + k, i].astype(F32)
        if n == 3:
            OWN[k, i] = total
        else:
            B2[k, i] = total.astype(BF16)
            send(B2.at[k, i], R2.at[k, n], q2s.at[k * 3 + n], q2r.at[k * 3 + n], at_q(i))

    put(NEXT, 0, partial(0, up))
    relay(0)
    put(NEXT, 1, partial(1, down))
    relay(1)

    CR[...] = jnp.zeros_like(CR)
    for i in range(2):
        CR[pl.ds(my_rows[i], 1)] = cross_sum[:, i * 128 : (i + 1) * 128]
    exchange_start(CR, CG1, bs1, br1, me_xy, at_xy)

    put(OWN, 0, partial(0, p))
    put(OWN, 1, partial(1, p))
    arrived(GTD.at[:, pl.ds(pl.multiple_of((1 - c) * HALF, HALF), HALF)], gs.at[0], gr.at[0])
    arrived(H.at[span(ROWS + (1 - c) * ROWS, ROWS)], cs.at[0], cr.at[0])

    @pl.when(c == 0)
    def _():
        arrived(H.at[3 * ROWS : 4 * ROWS], cs.at[1], cr.at[1])

    head_chunks(0, 2)
    arrived(R1.at[3], q1s.at[3], q1r.at[3])
    arrived(R1.at[2], q1s.at[2], q1r.at[2])
    for n in range(4):
        for k in range(2):
            second(k, n)
    CR2[...] = exchange_end(CR, CG1, bs1, br1, me_xy)
    exchange_start(CR2, CG2, bs2, br2, me_zc, at_zc)
    head_chunks(2, 5)

    at_home = (c == 0) & (zl == 0)
    at_home_hi = (c == 0) & (zl == 1)

    def to_owner(k, i, c_):
        n = k * 4 + i * 2 + c_
        return pltpu.make_async_remote_copy(
            src_ref=B3.at[k, i, c_], dst_ref=RZ.at[z], send_sem=rzs.at[n], recv_sem=rzr.at[z],
            device_id=dev(mod4(a + 2 * c + i), k, y, x, c_), device_id_type=MESH,
        )

    owners = [(k, i, c_) for k in range(2) for i in range(2) for c_ in range(2)]
    for k in range(2):
        total = OWN[k, q]
        for n in range(3):
            arrived(R2.at[k, n], q2s.at[k * 3 + n], q2r.at[k * 3 + n])
            total = total + R2[k, n].astype(F32)
        for i in range(2):
            for c_ in range(2):
                B3[k, i, c_] = total[48 * c_ : 48 * c_ + 64, i * 128 : (i + 1) * 128].astype(BF16)
                if i == 0 and c_ == 0:
                    home = at_home if k == 0 else at_home_hi

                    @pl.when(jnp.logical_not(home))
                    def _():
                        to_owner(k, i, c_).start()

                    @pl.when(home)
                    def _():
                        RZ[z] = B3[k, 0, 0]
                else:
                    to_owner(k, i, c_).start()

    head_chunks(5, 7)
    cross = exchange_end(CR2, CG2, bs2, br2, me_zc)
    KL[0:4] = cross[0:4] / TOT[4:8] - jnp.log(TOT[4:8]) + jnp.log(TOT[0:4])
    kl_out[...] = KL[pl.ds(a, 1)]

    flush()
    for k, i, c_ in owners:
        if i == 0 and c_ == 0:
            home = at_home if k == 0 else at_home_hi

            @pl.when(jnp.logical_not(home))
            def _():
                to_owner(k, i, c_).wait_send()
        else:
            to_owner(k, i, c_).wait_send()

    @pl.when(c == 1)
    def _():
        arrived(RZ.at[z], rzs.at[0], rzr.at[z])

    for k in range(1, 8):
        source = lax.rem(z + k, 8)
        arrived(RZ.at[source], rzs.at[0], rzr.at[source])
    total = RZ[0].astype(F32)
    for k in range(1, 8):
        total = total + RZ[k].astype(F32)
    dhid_out[...] = jnp.where(c == 0, total[0:56], total[8:64]).astype(BF16)


def results(kl, dhid, dhead, kl_out, dhid_out, dhead_out, sem):
    copies = [
        pltpu.make_async_copy(dhid, dhid_out, sem.at[7]),
        pltpu.make_async_copy(kl, kl_out, sem.at[8]),
    ]
    for n in range(7):
        at = pl.ds(n * 512, 512)
        copies.append(pltpu.make_async_copy(dhead.at[:, at], dhead_out.at[:, at], sem.at[n]))
    for copy in copies:
        copy.start()
    for copy in copies:
        copy.wait()


def on_device(hidden, valid_mask, student_head, teacher_logits):
    vm = pltpu.VMEM
    dma = pltpu.SemaphoreType.DMA
    any_spec = pl.BlockSpec(memory_space=pl.ANY)
    vmem_spec = pl.BlockSpec(memory_space=pltpu.VMEM)
    kl, dhid, dhead = pl.pallas_call(
        kernel,
        out_shape=(vm((1, ROWS), F32), vm((56, ROWS), BF16), vm((SLAB, D), BF16)),
        in_specs=[any_spec, vmem_spec, any_spec, any_spec],
        out_specs=(vmem_spec, vmem_spec, vmem_spec),
        scratch_shapes=[
            vm((512, D), BF16),
            vm((2 * VP, D), BF16),
            vm((2, 4, 4, CHIPCOL, 2 * VP), BF16),
            vm((256, 256), BF16),
            vm((3000, ROWS), BF16),
            vm((4, VP, ROWS), BF16),
            vm((4, VP, ROWS), BF16),
            vm((VP, ROWS), BF16),
            vm((2, VP, ROWS), BF16),
            vm((2 * VP, HALF), F32),
            vm((2 * VP, HALF), F32),
            vm((2 * VP, HALF), BF16),
            vm((VP, 512), BF16),
            vm((16, 128), F32),
            vm((16, 16, 128), F32),
            vm((16, 128), F32),
            vm((16, 16, 128), F32),
            vm((16, 128), F32),
            vm((8, 128), F32),
            vm((8, 128), F32),
            vm((8, 128), F32),
            vm((16, 8, 128), F32),
            vm((8, 128), F32),
            vm((16, 8, 128), F32),
            vm((8, 128), F32),
            vm((2, 4, CHIPCOL, HALF), F32),
            vm((2, 4, CHIPCOL, HALF), F32),
            vm((4, 4, CHIPCOL, HALF), BF16),
            vm((6, 4, CHIPCOL, HALF), BF16),
            vm((2, 4, CHIPCOL, HALF), BF16),
            vm((2, 4, CHIPCOL, HALF), BF16),
            vm((2, 3, CHIPCOL, HALF), BF16),
            vm((2, 2, 2, 64, 128), BF16),
            vm((8, 64, 128), BF16),
            dma((4,)),
            dma((2,)), dma((2,)),
            dma((2,)), dma((2,)),
            dma((2, 3)), dma((2, 3)), dma((2, 6)), dma((2, 6)),
            dma((2,)), dma((2,)),
            dma((6,)), dma((6,)),
            dma((1,)), dma((1,)),
            dma((15,)), dma((15,)), dma((15,)), dma((15,)),
            dma((15,)), dma((15,)), dma((15,)), dma((15,)),
            dma((4,)), dma((4,)), dma((2, 4)), dma((2, 4)), dma((6,)), dma((6,)),
            dma((8,)), dma((8,)),
        ],
        compiler_params=pltpu.CompilerParams(
            collective_id=0, has_side_effects=True, vmem_limit_bytes=50 * 1024 * 1024
        ),
        cost_estimate=pl.CostEstimate(flops=3 * 2 * 512 * 750 * 3584, bytes_accessed=13_000_000, transcendentals=0),
    )(hidden, valid_mask.reshape(1, ROWS), student_head, teacher_logits.T)
    kl, dhid, dhead = pl.pallas_call(
        results,
        out_shape=(
            jax.ShapeDtypeStruct((1, ROWS), F32),
            jax.ShapeDtypeStruct((56, ROWS), BF16),
            jax.ShapeDtypeStruct((SLAB, D), BF16),
        ),
        in_specs=[any_spec] * 3,
        out_specs=(any_spec,) * 3,
        scratch_shapes=[dma((9,))],
        compiler_params=pltpu.CompilerParams(vmem_limit_bytes=1024 * 1024),
    )(kl, dhid, dhead)
    return kl.reshape(ROWS), dhid.T, dhead


def solution(mesh):
    return jax.shard_map(
        on_device,
        mesh=mesh,
        in_specs=(P("tok", None), P("tok"), P(("voc", "tok"), None), P("tok", "voc")),
        out_specs=(P("tok"), P("tok", "voc"), P(("voc", "tok"), None)),
        check_vma=False,
    )
```

```python
import jax
import jax.numpy as jnp
from jax import lax
from jax.experimental import pallas as pl
from jax.experimental.pallas import tpu as pltpu
from jax.sharding import PartitionSpec as P

CAP = 30.0
D = 3584
ROWS = 128
HALF = 256
SLAB = 750
VP = 768
QCOL = D // 4
PIECE = ROWS // 4
CHIPCOL = 112
FAR_FIRST = (8, 10, 6, 9, 7, 11, 5, 12, 4, 2, 14, 13, 3, 15, 1)
MESH = pl.DeviceIdType.MESH
F32 = jnp.float32
BF16 = jnp.bfloat16


def kernel(
    hid, mask, head, teach, kl_out, dhid_out, DH,
    H, HD, HDT, EYE, tin, TS, TR, RLY, TSIB, CP, ES, GV, GTD,
    TT, TG1, TT2, TG2, TOT, AL, BE, CR, CG1, CR2, CG2, KL,
    OWN, NEXT, B1, R1, F1, B2, R2, B3, RZ,
    local, hs, hr, zs, zr, p1s, p1r, p2s, p2r, cs, cr, ts, tr, gs, gr,
    as1, ar1, as2, ar2, bs1, br1, bs2, br2, q1s, q1r, f1s, f1r, q2s, q2r, rzs, rzr,
):
    a = lax.axis_index("tok")
    v = lax.axis_index("voc")
    c = lax.rem(v, 2)
    x = lax.rem(v // 2, 4)
    y = lax.rem(v // 8, 4)
    zl = v // 32
    z = 2 * a + zl
    p = jnp.where(c == 0, x, y)
    q = jnp.where(c == 0, y, x)

    def dev(a_, zl_, y_, x_, c_):
        return (a_, zl_ * 32 + y_ * 8 + x_ * 2 + c_)

    def at_p(p_):
        return dev(a, zl, jnp.where(c == 0, y, p_), jnp.where(c == 0, p_, x), c)

    def at_q(q_):
        return dev(a, zl, jnp.where(c == 0, q_, y), jnp.where(c == 0, x, q_), c)

    sib = dev(a, zl, y, x, 1 - c)

    def at_a(a_):
        return dev(a_, zl, y, x, c)

    def at_xy(k):
        return dev(a, zl, k // 4, lax.rem(k, 4), c)

    def at_zc(k):
        return dev(k // 4, lax.rem(k // 2, 2), y, x, lax.rem(k, 2))

    def mod4(k):
        return lax.rem(k + 8, 4)

    me_xy = y * 4 + x
    me_zc = z * 2 + c

    pending = []

    def send(src, dst, ssem, rsem, to):
        copy = pltpu.make_async_remote_copy(
            src_ref=src, dst_ref=dst, send_sem=ssem, recv_sem=rsem, device_id=to, device_id_type=MESH
        )
        copy.start()
        pending.append(copy)

    def arrived(dst, ssem, rsem):
        pltpu.make_async_remote_copy(
            src_ref=dst, dst_ref=dst, send_sem=ssem, recv_sem=rsem, device_id=sib, device_id_type=MESH
        ).wait_recv()

    barrier = pltpu.get_barrier_semaphore()
    for k in FAR_FIRST:
        pl.semaphore_signal(barrier, inc=1, device_id=at_zc(lax.rem(me_zc + k, 16)), device_id_type=MESH)
    for k in range(1, 16):
        pl.semaphore_signal(barrier, inc=1, device_id=at_xy(lax.rem(me_xy + k, 16)), device_id_type=MESH)

    load_teach = pltpu.make_async_copy(teach, tin, local.at[0])
    load_teach.start()
    load_hid = pltpu.make_async_copy(hid, H.at[pl.ds(0, ROWS)], local.at[1])
    load_hid.start()

    pl.semaphore_wait(barrier, 30)

    def span(start, size):
        return pl.ds(pl.multiple_of(start, 16), size)

    def cols(q_):
        return pl.ds(pl.multiple_of(q_ * QCOL, 128), QCOL)

    def base(g):
        return ROWS + c * ROWS + g * ROWS

    later = []

    def flush():
        for copy in pending:
            copy.wait_send()
        pending.clear()

        @pl.when(c == 1)
        def _():
            for make in later:
                make().wait_send()

        later.clear()

    def each_group(step):
        step(0)

        @pl.when(c == 1)
        def _():
            step(1)

    def send_group(g, make):
        copy = make(g)
        copy.start()
        if g == 0:
            pending.append(copy)
        else:
            later.append(lambda: make(1))

    def remote(src, dst, ssem, rsem, to):
        return pltpu.make_async_remote_copy(
            src_ref=src, dst_ref=dst, send_sem=ssem, recv_sem=rsem, device_id=to, device_id_type=MESH
        )

    each_group(lambda g: send_group(g, lambda g: remote(
        hid.at[span(p * PIECE, PIECE), cols(q)], H.at[span(base(g) + p * PIECE, PIECE), cols(q)],
        zs.at[g], zr.at[g],
        dev(mod4(a - 1 - c - g), jnp.where((c == 1) & (g == 0), 1 - zl, zl), y, x, c),
    )))

    load_head = pltpu.make_async_copy(head.at[pl.ds(0, 736)], HD.at[0:736], local.at[2])
    load_head.start()
    send(head.at[pl.ds(0, 736)], HD.at[VP : VP + 736], hs.at[0], hr.at[0], sib)
    load_tail = pltpu.make_async_copy(head, DH, local.at[3])
    load_tail.start()

    load_teach.wait()
    place = lax.broadcasted_iota(jnp.int32, (VP, ROWS), 0)
    for t in range(4):
        start = t * SLAB // 16 * 16
        off = t * SLAB - start
        height = min(VP + 16, 3000 - start)
        tall = tin[start : start + height].astype(F32)
        if height < VP + 16:
            tall = jnp.concatenate([tall, jnp.zeros((VP + 16 - height, ROWS), F32)], axis=0)
        if off:
            tall = pltpu.roll(tall, VP + 16 - off, 0)
        part = jnp.where(place < SLAB, tall[:VP], -30000.0)
        TS[t] = part.astype(BF16)
    way = jnp.where(c == 0, 1, 3)
    send(TS.at[mod4(a + 2)], RLY, ts.at[2], tr.at[2], at_a(mod4(a + way)))
    TR[0] = TS[a]

    nt = (((1,), (1,)), ((), ()))
    EYE[...] = jnp.where(
        lax.broadcasted_iota(jnp.int32, (256, 256), 0) == lax.broadcasted_iota(jnp.int32, (256, 256), 1), 1.0, 0.0
    ).astype(BF16)

    def turn(slab, half):
        for n in range(7):
            at = pl.ds(half * 1792 + n * 256, 256)
            out = lax.dot_general(
                EYE[...], HD[slab * VP : (slab + 1) * VP, at], nt, preferred_element_type=F32
            ).astype(BF16)
            done = 0
            while done < 256:
                chip, row = divmod(n * 256 + done, CHIPCOL)
                size = min(CHIPCOL - row, 256 - done)
                p_, q_ = jnp.where(c == 0, chip % 4, chip // 4), jnp.where(c == 0, chip // 4, chip % 4)
                HDT[half, p_, q_, row : row + size, slab * VP : (slab + 1) * VP] = out[done : done + size]
                done += size

    def piece(g, p_):
        return H.at[span(base(g) + p_ * PIECE, PIECE), cols(q)]

    def first_step(g):
        arrived(piece(g, p), zs.at[g], zr.at[g])
        for d in (2, 1, 3):
            send_group(g, lambda g, d=d: remote(
                piece(g, p), piece(g, p), p1s.at[g, d - 1], p1r.at[g, d - 1], at_p(mod4(p + d)),
            ))

    each_group(first_step)

    TT[...] = jnp.zeros_like(TT)
    teacher_sum = jnp.zeros((1, ROWS), F32)
    for t in range(4):
        teacher_sum = teacher_sum + jnp.sum(jnp.exp(TS[t].astype(F32)), axis=0, keepdims=True)
    TT[pl.ds(4 + a, 1)] = teacher_sum
    TT[pl.ds(8 + a, 1)] = mask[...].astype(F32)

    load_tail.wait()
    HD[736:768] = jnp.concatenate([DH[736:750].astype(F32), jnp.zeros((18, D), F32)], axis=0).astype(BF16)
    send(HD.at[736:768], HD.at[VP + 736 : VP + 768], hs.at[1], hr.at[1], sib)
    load_head.wait()
    turn(0, 0)

    def first_end(g):
        for d in range(1, 4):
            arrived(piece(g, mod4(p - d)), p1s.at[g, d - 1], p1r.at[g, d - 1])

    right, left = at_q(mod4(q + 1)), at_q(mod4(q - 1))
    before, after, across = mod4(q - 1), mod4(q + 1), mod4(q + 2)

    def part_of(g, half, q_):
        return H.at[span(base(g) + half * 64, 64), cols(q_)]

    def pass_on(g, n, half, q_, to):
        send_group(g, lambda g: remote(part_of(g, half, q_), part_of(g, half, q_), p2s.at[g, n], p2r.at[g, n], to))

    def passed(n, half, q_):
        each_group(lambda g: arrived(part_of(g, half, q_), p2s.at[g, n], p2r.at[g, n]))

    def second_step(g):
        first_end(g)
        pass_on(g, 0, 0, q, right)
        pass_on(g, 1, 1, q, left)
        pass_on(g, 2, 1, q, right)
        pass_on(g, 3, 0, q, left)

    def relay_step(g):
        arrived(part_of(g, 0, before), p2s.at[g, 0], p2r.at[g, 0])
        pass_on(g, 4, 0, before, right)
        arrived(part_of(g, 1, after), p2s.at[g, 1], p2r.at[g, 1])
        pass_on(g, 5, 1, after, left)

    each_group(second_step)
    send(TS.at[mod4(a + 1)], TR.at[3], ts.at[0], tr.at[0], at_a(mod4(a + 1)))
    send(TS.at[mod4(a + 3)], TR.at[1], ts.at[1], tr.at[1], at_a(mod4(a + 3)))

    my_half = pl.ds(pl.multiple_of(c * HALF, HALF), HALF)

    def logits(slab, q_, first=False):
        rr = slice(slab * VP, (slab + 1) * VP)
        out = lax.dot_general(HD[rr, cols(q_)], H[my_half, cols(q_)], nt, preferred_element_type=F32)
        CP[rr] = out if first else CP[rr] + out

    load_hid.wait()
    logits(0, q, True)
    turn(0, 1)
    each_group(relay_step)

    arrived(RLY, ts.at[2], tr.at[2])
    send(RLY, TR.at[2], ts.at[3], tr.at[3], at_a(mod4(a + way)))
    passed(2, 1, before)
    logits(0, before)
    passed(3, 0, after)
    logits(0, after)
    arrived(HD.at[VP : VP + 736], hs.at[0], hr.at[0])
    arrived(HD.at[VP + 736 : VP + 768], hs.at[1], hr.at[1])
    logits(1, q, True)
    logits(1, before)
    logits(1, after)
    passed(4, 0, across)
    passed(5, 1, across)
    in_slab = lax.broadcasted_iota(jnp.int32, (256, HALF), 0) < SLAB - 512

    def exponentials(slab, student_sum):
        for k in range(3):
            rr = slice(slab * VP + k * 256, slab * VP + (k + 1) * 256)
            capped = CAP * jnp.tanh(CP[rr] * (1.0 / CAP))
            exps = jnp.exp(capped)
            if k == 2:
                exps = jnp.where(in_slab, exps, 0.0)
            CP[rr] = capped
            ES[rr] = exps
            student_sum = student_sum + jnp.sum(exps, axis=0, keepdims=True)
        return student_sum

    logits(0, across)
    logits(1, across)
    student_sum = exponentials(0, jnp.zeros((1, HALF), F32))
    student_sum = exponentials(1, student_sum)
    my_rows = (mod4(a + 2 * c), mod4(a + 2 * c + 1))
    for i in range(2):
        TT[pl.ds(my_rows[i], 1)] = student_sum[:, i * 128 : (i + 1) * 128]

    def exchange_start(tile, slots, ssem, rsem, me, at):
        for k in FAR_FIRST:
            send(tile, slots.at[me], ssem.at[k - 1], rsem.at[k - 1], at(lax.rem(me + k, 16)))

    def exchange_end(tile, slots, ssem, rsem, me):
        slots[me] = tile[...]
        for k in range(1, 16):
            arrived(slots.at[lax.rem(me + 16 - k, 16)], ssem.at[k - 1], rsem.at[k - 1])
        total = slots[0]
        for k in range(1, 16):
            total = total + slots[k]
        return total

    gathered = list(pending), list(later)
    pending.clear()
    later.clear()
    exchange_start(TT, TG1, as1, ar1, me_xy, at_xy)

    def factors(slab, cross_sum):
        for k in range(6):
            rr = slice(slab * VP + k * 128, slab * VP + (k + 1) * 128)
            vv = slice(k * 128, (k + 1) * 128)
            if slab == 0:
                target = jnp.concatenate([TR[2 * c, vv], TR[2 * c + 1, vv]], axis=1).astype(F32)
            else:
                target = jnp.concatenate([TSIB[0, vv], TSIB[1, vv]], axis=1).astype(F32)
            expd = jnp.exp(target)
            capped = CP[rr]
            cross_sum = cross_sum + jnp.sum(expd * (target - capped), axis=0, keepdims=True)
            ratio = capped * (1.0 / CAP)
            slope = 1.0 - ratio * ratio
            ES[rr] = ES[rr] * slope
            CP[rr] = expd * slope
        return cross_sum

    turn(1, 0)

    def give(i):
        send(TR.at[2 * (1 - c) + i], TSIB.at[i], ts.at[4 + i], tr.at[4 + i], sib)

    arrived(TR.at[3], ts.at[0], tr.at[0])
    arrived(TR.at[1], ts.at[1], tr.at[1])
    give(1)
    TT2[...] = exchange_end(TT, TG1, as1, ar1, me_xy)
    exchange_start(TT2, TG2, as2, ar2, me_zc, at_zc)
    arrived(TR.at[2], ts.at[3], tr.at[3])
    give(0)
    cross_sum = factors(0, jnp.zeros((1, HALF), F32))
    turn(1, 1)
    for i in range(2):
        arrived(TSIB.at[i], ts.at[4 + i], tr.at[4 + i])
    cross_sum = factors(1, cross_sum)
    TOT[...] = exchange_end(TT2, TG2, as2, ar2, me_zc)

    valid = TOT[8:12] * (1.0 / 64.0)
    weight = valid * (512.0 / jnp.sum(valid))
    AL[0:4] = weight / TOT[0:4]
    BE[0:4] = weight / TOT[4:8]
    alpha = jnp.concatenate([AL[pl.ds(r, 1)] for r in my_rows], axis=1)
    beta = jnp.concatenate([BE[pl.ds(r, 1)] for r in my_rows], axis=1)
    for k in range(12):
        rr = slice(k * 128, (k + 1) * 128)
        grad = (ES[rr] * alpha - CP[rr] * beta).astype(BF16)
        GV[rr] = grad
        if k < 6:
            GTD[rr, my_half] = grad

    up, down, far = mod4(p + 1), mod4(p - 1), mod4(p + 2)

    def partial(n, p_):
        rows = HDT[n, p_].reshape(4 * CHIPCOL, 2 * VP)
        return jnp.dot(rows, GV[...], preferred_element_type=F32)

    def put(ref, n, block):
        for i in range(4):
            ref[n, i] = block[i * CHIPCOL : (i + 1) * CHIPCOL].astype(ref.dtype)

    put(B1, 0, partial(0, far))
    send(B1.at[0], R1.at[0], q1s.at[0], q1r.at[0], at_p(up))
    put(B1, 1, partial(1, far))
    send(B1.at[1], R1.at[1], q1s.at[1], q1r.at[1], at_p(down))
    put(B1, 2, partial(1, up))
    send(B1.at[2], R1.at[2], q1s.at[2], q1r.at[2], at_p(up))
    put(B1, 3, partial(0, down))
    send(B1.at[3], R1.at[3], q1s.at[3], q1r.at[3], at_p(down))
    send(GV.at[VP : 2 * VP], GTD.at[:, my_half], gs.at[0], gr.at[0], sib)

    def share(g):
        return H.at[span(base(g), ROWS)]

    each_group(lambda g: send_group(g, lambda g: remote(share(g), share(g), cs.at[g], cr.at[g], sib)))


    def head_chunk(n):
        at = pl.ds(pl.multiple_of(n * 512, 512), 512)
        out = jnp.dot(GTD[...], H[:, at], preferred_element_type=F32)
        DH[:, at] = out[:SLAB].astype(BF16)

    def head_chunks(first, last):
        @pl.loop(first, last)
        def _(n):
            head_chunk(n)

    qup, qdown, qfar = mod4(q + 1), mod4(q - 1), mod4(q + 2)
    order = (qfar, qup, qdown, q)

    def relay(k):
        arrived(R1.at[k], q1s.at[k], q1r.at[k])
        near = up if k == 0 else down
        for n, i in enumerate(order):
            F1[k, i] = (NEXT[k, i] + R1[k, i].astype(F32)).astype(BF16)
            send(F1.at[k, i], R1.at[4 + k, i], f1s.at[k, n], f1r.at[k, n], at_p(near))

    def second(k, n):
        i = order[n]
        arrived(R1.at[4 + k, i], f1s.at[k, n], f1r.at[k, n])
        total = OWN[k, i] + R1[3 - k, i].astype(F32) + R1[4 + k, i].astype(F32)
        if n == 3:
            OWN[k, i] = total
        else:
            B2[k, i] = total.astype(BF16)
            send(B2.at[k, i], R2.at[k, n], q2s.at[k * 3 + n], q2r.at[k * 3 + n], at_q(i))

    put(NEXT, 0, partial(0, up))
    relay(0)
    put(NEXT, 1, partial(1, down))
    relay(1)

    CR[...] = jnp.zeros_like(CR)
    for i in range(2):
        CR[pl.ds(my_rows[i], 1)] = cross_sum[:, i * 128 : (i + 1) * 128]
    exchange_start(CR, CG1, bs1, br1, me_xy, at_xy)

    put(OWN, 0, partial(0, p))
    put(OWN, 1, partial(1, p))
    arrived(GTD.at[:, pl.ds(pl.multiple_of((1 - c) * HALF, HALF), HALF)], gs.at[0], gr.at[0])
    arrived(H.at[span(ROWS + (1 - c) * ROWS, ROWS)], cs.at[0], cr.at[0])

    @pl.when(c == 0)
    def _():
        arrived(H.at[3 * ROWS : 4 * ROWS], cs.at[1], cr.at[1])

    head_chunks(0, 2)
    arrived(R1.at[3], q1s.at[3], q1r.at[3])
    arrived(R1.at[2], q1s.at[2], q1r.at[2])
    for n in range(4):
        for k in range(2):
            second(k, n)
    CR2[...] = exchange_end(CR, CG1, bs1, br1, me_xy)
    exchange_start(CR2, CG2, bs2, br2, me_zc, at_zc)
    head_chunks(2, 4)

    at_home = (c == 0) & (zl == 0)
    at_home_hi = (c == 0) & (zl == 1)

    def to_owner(k, i, c_):
        n = k * 4 + i * 2 + c_
        return pltpu.make_async_remote_copy(
            src_ref=B3.at[k, i, c_], dst_ref=RZ.at[z], send_sem=rzs.at[n], recv_sem=rzr.at[z],
            device_id=dev(mod4(a + 2 * c + i), k, y, x, c_), device_id_type=MESH,
        )

    owners = [(k, i, c_) for k in range(2) for i in range(2) for c_ in range(2)]
    for k in range(2):
        total = OWN[k, q]
        for n in range(3):
            arrived(R2.at[k, n], q2s.at[k * 3 + n], q2r.at[k * 3 + n])
            total = total + R2[k, n].astype(F32)
        for i in range(2):
            for c_ in range(2):
                B3[k, i, c_] = total[48 * c_ : 48 * c_ + 64, i * 128 : (i + 1) * 128].astype(BF16)
                if i == 0 and c_ == 0:
                    home = at_home if k == 0 else at_home_hi

                    @pl.when(jnp.logical_not(home))
                    def _():
                        to_owner(k, i, c_).start()

                    @pl.when(home)
                    def _():
                        RZ[z] = B3[k, 0, 0]
                else:
                    to_owner(k, i, c_).start()

    for copy in gathered[0]:
        copy.wait_send()

    @pl.when(c == 1)
    def _():
        for make in gathered[1]:
            make().wait_send()

    head_chunks(4, 7)
    cross = exchange_end(CR2, CG2, bs2, br2, me_zc)
    KL[0:4] = cross[0:4] / TOT[4:8] - jnp.log(TOT[4:8]) + jnp.log(TOT[0:4])
    kl_out[...] = KL[pl.ds(a, 1)]

    flush()
    for k, i, c_ in owners:
        if i == 0 and c_ == 0:
            home = at_home if k == 0 else at_home_hi

            @pl.when(jnp.logical_not(home))
            def _():
                to_owner(k, i, c_).wait_send()
        else:
            to_owner(k, i, c_).wait_send()

    @pl.when(c == 1)
    def _():
        arrived(RZ.at[z], rzs.at[0], rzr.at[z])

    for k in range(1, 8):
        source = lax.rem(z + k, 8)
        arrived(RZ.at[source], rzs.at[0], rzr.at[source])
    total = RZ[0].astype(F32)
    for k in range(1, 8):
        total = total + RZ[k].astype(F32)
    dhid_out[...] = jnp.where(c == 0, total[0:56], total[8:64]).astype(BF16)


def results(kl, dhid, dhead, kl_out, dhid_out, dhead_out, sem):
    copies = [
        pltpu.make_async_copy(dhid, dhid_out, sem.at[7]),
        pltpu.make_async_copy(kl, kl_out, sem.at[8]),
    ]
    for n in range(7):
        at = pl.ds(n * 512, 512)
        copies.append(pltpu.make_async_copy(dhead.at[:, at], dhead_out.at[:, at], sem.at[n]))
    for copy in copies:
        copy.start()
    for copy in copies:
        copy.wait()


def on_device(hidden, valid_mask, student_head, teacher_logits):
    vm = pltpu.VMEM
    dma = pltpu.SemaphoreType.DMA
    any_spec = pl.BlockSpec(memory_space=pl.ANY)
    vmem_spec = pl.BlockSpec(memory_space=pltpu.VMEM)
    kl, dhid, dhead = pl.pallas_call(
        kernel,
        out_shape=(vm((1, ROWS), F32), vm((56, ROWS), BF16), vm((SLAB, D), BF16)),
        in_specs=[any_spec, vmem_spec, any_spec, any_spec],
        out_specs=(vmem_spec, vmem_spec, vmem_spec),
        scratch_shapes=[
            vm((512, D), BF16),
            vm((2 * VP, D), BF16),
            vm((2, 4, 4, CHIPCOL, 2 * VP), BF16),
            vm((256, 256), BF16),
            vm((3000, ROWS), BF16),
            vm((4, VP, ROWS), BF16),
            vm((4, VP, ROWS), BF16),
            vm((VP, ROWS), BF16),
            vm((2, VP, ROWS), BF16),
            vm((2 * VP, HALF), F32),
            vm((2 * VP, HALF), F32),
            vm((2 * VP, HALF), BF16),
            vm((VP, 512), BF16),
            vm((16, 128), F32),
            vm((16, 16, 128), F32),
            vm((16, 128), F32),
            vm((16, 16, 128), F32),
            vm((16, 128), F32),
            vm((8, 128), F32),
            vm((8, 128), F32),
            vm((8, 128), F32),
            vm((16, 8, 128), F32),
            vm((8, 128), F32),
            vm((16, 8, 128), F32),
            vm((8, 128), F32),
            vm((2, 4, CHIPCOL, HALF), F32),
            vm((2, 4, CHIPCOL, HALF), F32),
            vm((4, 4, CHIPCOL, HALF), BF16),
            vm((6, 4, CHIPCOL, HALF), BF16),
            vm((2, 4, CHIPCOL, HALF), BF16),
            vm((2, 4, CHIPCOL, HALF), BF16),
            vm((2, 3, CHIPCOL, HALF), BF16),
            vm((2, 2, 2, 64, 128), BF16),
            vm((8, 64, 128), BF16),
            dma((4,)),
            dma((2,)), dma((2,)),
            dma((2,)), dma((2,)),
            dma((2, 3)), dma((2, 3)), dma((2, 6)), dma((2, 6)),
            dma((2,)), dma((2,)),
            dma((6,)), dma((6,)),
            dma((1,)), dma((1,)),
            dma((15,)), dma((15,)), dma((15,)), dma((15,)),
            dma((15,)), dma((15,)), dma((15,)), dma((15,)),
            dma((4,)), dma((4,)), dma((2, 4)), dma((2, 4)), dma((6,)), dma((6,)),
            dma((8,)), dma((8,)),
        ],
        compiler_params=pltpu.CompilerParams(
            collective_id=0, has_side_effects=True, vmem_limit_bytes=50 * 1024 * 1024
        ),
        cost_estimate=pl.CostEstimate(flops=3 * 2 * 512 * 750 * 3584, bytes_accessed=13_000_000, transcendentals=0),
    )(hidden, valid_mask.reshape(1, ROWS), student_head, teacher_logits.T)
    kl, dhid, dhead = pl.pallas_call(
        results,
        out_shape=(
            jax.ShapeDtypeStruct((1, ROWS), F32),
            jax.ShapeDtypeStruct((56, ROWS), BF16),
            jax.ShapeDtypeStruct((SLAB, D), BF16),
        ),
        in_specs=[any_spec] * 3,
        out_specs=(any_spec,) * 3,
        scratch_shapes=[dma((9,))],
        compiler_params=pltpu.CompilerParams(vmem_limit_bytes=1024 * 1024),
    )(kl, dhid, dhead)
    return kl.reshape(ROWS), dhid.T, dhead


def solution(mesh):
    return jax.shard_map(
        on_device,
        mesh=mesh,
        in_specs=(P("tok", None), P("tok"), P(("voc", "tok"), None), P("tok", "voc")),
        out_specs=(P("tok"), P("tok", "voc"), P(("voc", "tok"), None)),
        check_vma=False,
    )
```
